32 devices in a mesh: row: 4 (over z), col: 8 (over y, x, core).
Axes of the slice: x: 2, y: 2, z: 4, core: 2. Of those that a mesh axis runs over, the one named last changes fastest.
Arguments:
- tokens: bfloat16 [512, 8192], P('col', 'row'), may hold values from -6 to 6
- gate_weight: bfloat16 [8192, 16384], P('row', 'col'), may hold values from -0.0625 to 0.0625
- up_weight: bfloat16 [8192, 16384], P('row', 'col'), may hold values from -0.0625 to 0.0625
- block_mask: int32 [64, 128], P('row', 'col'), may hold values 0 or 1
- hidden_grad: bfloat16 [512, 16384], P('row', 'col'), may hold values from -0.26367188 to 0.26367188
Outputs:
- hidden: bfloat16 [512, 16384], P('row', 'col')
- gate_weight_grad: float32 [8192, 16384], P('row', 'col')
- up_weight_grad: float32 [8192, 16384], P('row', 'col')
The draws below stay inside these ranges and needn't reach their ends.
All inputs are finite; a program needn't handle non-finite values. No bound on the sum of `block_mask` on one device may be relied on, other than what follows from the above.
Results may differ from the reference program's by a relative error of at most 0.003.
Values may be sent and summed in bfloat16 or wider, within the bound.
No kernel may reach another device: no remote copies, remote signals or barrier semaphores. Data moves between devices by JAX's collectives and lax.ppermute only.
A program may use at most 192 MiB of HBM per device.

```python
import jax
import jax.numpy as jnp

D = 8192
FF = 16384
BLOCK = 128
TOKENS = 512


def with_ends(result, stream_key, low, top_value):
    longest = result.shape.index(max(result.shape))
    spots = []
    for shift in (0, 1):
        where = [jax.random.randint(jax.random.fold_in(stream_key, axis), (), 0, length) for axis, length in enumerate(result.shape)]
        where[longest] = (where[longest] + shift) % result.shape[longest]
        spots.append(tuple(where))
    return result.at[spots[0]].set(low).at[spots[1]].set(top_value)


def block_scale(key, extent, split, low, high):
    factor_of = 1.0
    for position, blocks in split:
        draws = jax.random.uniform(jax.random.fold_in(jax.random.fold_in(key, 6), position), (blocks,), jnp.float32, low / len(split), high / len(split))
        factor_of = factor_of * jnp.repeat(jnp.exp(draws), extent[position] // blocks).reshape((-1,) + (1,) * (len(extent) - 1 - position))
    return factor_of


def normal_values(own_key, extent, scale, limit, cuts=(), dtype=jnp.bfloat16):
    loudness = block_scale(own_key, extent, cuts, -0.22, 0.18) if cuts else 1.0
    values = jax.random.normal(own_key, extent, jnp.float32) * scale * loudness
    return jnp.minimum(jnp.maximum(values, -limit), limit).astype(dtype)


def setup_inputs(seed: int = 0) -> dict:
    key_of = jax.random.split(jax.random.key(seed), 6)
    tokens = normal_values(key_of[0], (TOKENS, D), 1.0, 6.0, ((0, 8), (1, 4)))
    gate_weight = normal_values(key_of[1], (D, FF), D ** -0.5, 0.0625, ((0, 4), (1, 8)))
    up_weight = normal_values(key_of[2], (D, FF), D ** -0.5, 0.0625, ((0, 4), (1, 8)))
    block_mask = with_ends((jax.random.randint(key_of[3], (D // BLOCK, FF // BLOCK), 0, 2) < 1).astype(jnp.int32), jax.random.fold_in(key_of[3], 1), 0, 1)
    hidden_grad = normal_values(key_of[4], (TOKENS, FF), (TOKENS ** -0.5), 0.26367188, ((0, 4), (1, 8)))
    return dict(tokens=tokens, gate_weight=gate_weight, up_weight=up_weight, block_mask=block_mask, hidden_grad=hidden_grad)


def spread(block_mask):
    rows, cols = block_mask.shape
    ones = block_mask.astype(jnp.bfloat16)
    wide = jnp.broadcast_to(ones[:, None, :, None], (rows, BLOCK, cols, BLOCK))
    return wide.reshape(rows * BLOCK, cols * BLOCK)


def local_grads(gate, up, cotangent):
    sig = jax.nn.sigmoid(gate)
    silu = gate * sig
    hidden = (silu * up).astype(jnp.bfloat16)
    back = cotangent.astype(jnp.float32)
    gate_delta = (back * up * sig * (1.0 + gate * (1.0 - sig))).astype(jnp.bfloat16)
    up_delta = (back * silu).astype(jnp.bfloat16)
    return hidden, gate_delta, up_delta


def reference(tokens, gate_weight, up_weight, block_mask, hidden_grad):
    keep = spread(block_mask)
    stacked = jnp.concatenate([gate_weight * keep, up_weight * keep], axis=1)
    both = jnp.dot(tokens, stacked, preferred_element_type=jnp.float32)
    hidden, gate_delta, up_delta = local_grads(both[:, :FF], both[:, FF:], hidden_grad)
    deltas = jnp.concatenate([gate_delta, up_delta], axis=1)
    grads = jnp.dot(tokens.T, deltas, preferred_element_type=jnp.float32)
    keep_wide = keep.astype(jnp.float32)
    return hidden, grads[:, :FF] * keep_wide, grads[:, FF:] * keep_wide
```

```python
import functools

import jax
import jax.numpy as jnp
from jax import lax
from jax.experimental import pallas as pl
from jax.experimental.pallas import tpu as pltpu
from jax.sharding import PartitionSpec as P

BLOCK = 128
GROUPS = 16
CHUNKS = 4
VMEM_LIMIT = 48 * 1024 * 1024


def params():
    return pltpu.CompilerParams(vmem_limit_bytes=VMEM_LIMIT)


def encode(value):
    rows, cols = value.shape
    grouped = value.reshape(GROUPS, rows // GROUPS, cols)
    top = jnp.max(jnp.abs(grouped), axis=1)
    power = jnp.floor(jnp.log2(jnp.maximum(top, 1e-30))) + 1.0
    codes = jnp.round(grouped * jnp.exp2(15.0 - power)[:, None, :])
    codes = jnp.clip(codes, -32767.0, 32767.0).reshape(rows, cols)
    return codes.astype(jnp.int32).astype(jnp.int16), power.astype(jnp.int32).astype(jnp.int16)


def put(ref, value):
    rows = value.shape[0]
    codes, power = encode(value)
    ref[0:rows, :] = codes
    ref[rows : rows + GROUPS, :] = power


def get(ref):
    rows = ref.shape[0] - GROUPS
    cols = ref.shape[1]
    codes = ref[0:rows, :].astype(jnp.int32).astype(jnp.float32)
    power = ref[rows : rows + GROUPS, :].astype(jnp.int32).astype(jnp.float32)
    grouped = codes.reshape(GROUPS, rows // GROUPS, cols) * jnp.exp2(power - 15.0)[:, None, :]
    return grouped.reshape(rows, cols)


def forward_kernel(side_ref, mask_ref, far_ref, near_ref, gate_ref, up_ref, far_out, near_out, held, *, first):
    depth, width = gate_ref.shape
    base = (first + pl.program_id(0)) * (width // BLOCK)
    for r in range(depth // BLOCK):
        rows = slice(r * BLOCK, (r + 1) * BLOCK)
        for q in range(width // BLOCK):
            cols = slice(q * BLOCK, (q + 1) * BLOCK)
            keep = mask_ref[r, base + q] != 0
            gate = gate_ref[rows, cols]
            up = up_ref[rows, cols]
            held[rows, cols] = jnp.where(keep, gate, jnp.zeros_like(gate))
            held[rows, width + q * BLOCK : width + (q + 1) * BLOCK] = jnp.where(keep, up, jnp.zeros_like(up))
    put(far_out, jnp.dot(far_ref[...], held[...], preferred_element_type=jnp.float32))
    put(near_out, jnp.dot(near_ref[...], held[...], preferred_element_type=jnp.float32))


def forward(side, mask, tokens, gate_weight, up_weight, first, steps, width):
    count, depth = tokens.shape
    half = count // 2
    message = jax.ShapeDtypeStruct((half + GROUPS, 2 * width * steps), jnp.int16)
    weight = pl.BlockSpec((depth, width), lambda j, side, mask: (0, first + j))
    out = pl.BlockSpec((half + GROUPS, 2 * width), lambda j, side, mask: (0, j))
    return pl.pallas_call(
        functools.partial(forward_kernel, first=first),
        grid_spec=pltpu.PrefetchScalarGridSpec(
            num_scalar_prefetch=2,
            grid=(steps,),
            in_specs=[
                pl.BlockSpec((half, depth), lambda j, side, mask: (1 - side[0], 0)),
                pl.BlockSpec((half, depth), lambda j, side, mask: (side[0], 0)),
                weight,
                weight,
            ],
            out_specs=[out, out],
            scratch_shapes=[pltpu.VMEM((depth, 2 * width), jnp.bfloat16)],
        ),
        out_shape=[message, message],
        compiler_params=params(),
        cost_estimate=pl.CostEstimate(
            flops=4 * count * depth * width * steps,
            bytes_accessed=4 * depth * width * steps + 2 * count * depth + 4 * count * width * steps,
            transcendentals=0,
        ),
        name="forward",
    )(side, mask, tokens, tokens, gate_weight, up_weight)


def add_kernel(a_ref, b_ref, out_ref):
    put(out_ref, get(a_ref) + get(b_ref))


def add(a, b, width):
    rows, cols = a.shape
    spec = pl.BlockSpec((rows, 2 * width), lambda j: (0, j))
    return pl.pallas_call(
        add_kernel,
        grid=(cols // (2 * width),),
        in_specs=[spec, spec],
        out_specs=spec,
        out_shape=jax.ShapeDtypeStruct(a.shape, a.dtype),
        compiler_params=params(),
        cost_estimate=pl.CostEstimate(flops=16 * rows * cols, bytes_accessed=6 * rows * cols, transcendentals=0),
        name="add",
    )(a, b)


def grads_kernel(a_ref, b_ref, c_ref, back_ref, deltas_ref, hidden_ref):
    width = back_ref.shape[1]
    both = get(a_ref) + get(b_ref) + get(c_ref)
    gate, up = both[:, :width], both[:, width:]
    sig = jax.nn.sigmoid(gate)
    silu = gate * sig
    back = back_ref[...].astype(jnp.float32)
    hidden_ref[...] = (silu * up).astype(jnp.bfloat16)
    deltas_ref[:, :width] = (back * up * sig * (1.0 + gate * (1.0 - sig))).astype(jnp.bfloat16)
    deltas_ref[:, width:] = (back * silu).astype(jnp.bfloat16)


def grads(a, b, c, back, first, width):
    rows, cols = a.shape
    half = rows - GROUPS
    spec = pl.BlockSpec((rows, 2 * width), lambda j: (0, j))
    return pl.pallas_call(
        grads_kernel,
        grid=(cols // (2 * width),),
        in_specs=[spec, spec, spec, pl.BlockSpec((half, width), lambda j: (0, first + j))],
        out_specs=[
            pl.BlockSpec((half, 2 * width), lambda j: (0, j)),
            pl.BlockSpec((half, width), lambda j: (0, j)),
        ],
        out_shape=[
            jax.ShapeDtypeStruct((half, cols), jnp.bfloat16),
            jax.ShapeDtypeStruct((half, cols // 2), jnp.bfloat16),
        ],
        compiler_params=params(),
        cost_estimate=pl.CostEstimate(flops=20 * rows * cols, bytes_accessed=10 * rows * cols, transcendentals=rows * cols),
        name="grads",
    )(a, b, c, back)


def weights_kernel(side_ref, mask_ref, near_ref, far_ref, first_ref, second_ref, *rest, first):
    gate_ref, up_ref = rest[-2:]
    depth, width = gate_ref.shape
    base = (first + pl.program_id(0)) * (width // BLOCK)
    total = jnp.dot(near_ref[...], first_ref[...], preferred_element_type=jnp.float32)
    total += jnp.dot(far_ref[...], second_ref[...], preferred_element_type=jnp.float32)
    for r in range(depth // BLOCK):
        rows = slice(r * BLOCK, (r + 1) * BLOCK)
        for q in range(width // BLOCK):
            cols = slice(q * BLOCK, (q + 1) * BLOCK)
            keep = mask_ref[r, base + q].astype(jnp.float32)
            gate_ref[rows, cols] = total[rows, cols] * keep
            up_ref[rows, cols] = total[rows, width + q * BLOCK : width + (q + 1) * BLOCK] * keep


def weight_grads(side, mask, turned, first_half, second_half, previous, shape, first, width):
    depth, count = turned.shape
    half = count // 2
    steps = first_half.shape[1] // (2 * width)
    deltas = pl.BlockSpec((half, 2 * width), lambda j, side, mask: (0, j))
    out = pl.BlockSpec((depth, width), lambda j, side, mask: (0, first + j))
    whole = jax.ShapeDtypeStruct(shape, jnp.float32)
    return pl.pallas_call(
        functools.partial(weights_kernel, first=first),
        grid_spec=pltpu.PrefetchScalarGridSpec(
            num_scalar_prefetch=2,
            grid=(steps,),
            in_specs=[
                pl.BlockSpec((depth, half), lambda j, side, mask: (0, side[0])),
                pl.BlockSpec((depth, half), lambda j, side, mask: (0, 1 - side[0])),
                deltas,
                deltas,
            ]
            + [pl.BlockSpec(memory_space=pl.ANY)] * len(previous),
            out_specs=[out, out],
        ),
        out_shape=[whole, whole],
        input_output_aliases={6 + i: i for i in range(len(previous))},
        compiler_params=params(),
        cost_estimate=pl.CostEstimate(
            flops=4 * count * depth * width * steps,
            bytes_accessed=8 * depth * width * steps + 2 * count * depth + 4 * count * width * steps,
            transcendentals=0,
        ),
        name="weight_grads",
    )(side, mask, turned, turned, first_half, second_half, *previous)


def on_device(tokens, gate_weight, up_weight, block_mask, hidden_grad, *, ring):
    me = lax.axis_index("row")
    depth, local = gate_weight.shape
    left, right = ring // 2 - 1, ring // 2
    reach = ring // 2 - 1
    on_right = me >= right
    distance = jnp.where(on_right, me - right, left - me)
    side = on_right.astype(jnp.int32).reshape(1)
    chunks = min(CHUNKS, local // BLOCK)
    span = local // chunks
    width = min(2 * BLOCK, span)
    steps = span // width

    def outward(value, hop):
        return lax.ppermute(value, "row", [(left - hop, left - hop - 1), (right + hop, right + hop + 1)])

    def inward(value, hop):
        return lax.ppermute(value, "row", [(left - hop - 1, left - hop), (right + hop + 1, right + hop)])

    def swap(value):
        return lax.ppermute(value, "row", [(left, right), (right, left)])

    def pick(condition, a, b):
        return lax.select(jnp.broadcast_to(condition, a.shape), a, b)

    gathered = lax.all_gather(tokens, "col", axis=0, tiled=True)
    turned = gathered.T

    pieces = [hidden_grad]
    for hop in range(1, reach + 1):
        pieces.append(lax.ppermute(hidden_grad, "row", [(left - hop, left), (right + hop, right)]))
    back = pick(on_right, jnp.concatenate(pieces, axis=0), jnp.concatenate(pieces[::-1], axis=0))

    outs = ()
    hiddens = []
    for chunk in range(chunks):
        first = chunk * steps
        far, near = forward(side, block_mask, gathered, gate_weight, up_weight, first, steps, width)
        far_sum, near_sum = far, near
        for hop in reversed(range(reach)):
            far_in, near_in = inward(far_sum, hop), inward(near_sum, hop)
            far_sum = add(far, far_in, width)
            if hop:
                near_sum = add(near, near_in, width)
        across = swap(far_sum)
        if not reach:
            near_in = jnp.zeros_like(near)
        deltas, hidden = grads(near, near_in, across, back, first, width)
        hiddens.append(hidden)
        other = swap(deltas)
        for hop in range(reach):
            moved, moved_other = outward(deltas, hop), outward(other, hop)
            deltas = pick(distance == hop + 1, moved, deltas)
            other = pick(distance == hop + 1, moved_other, other)
        outs = weight_grads(side, block_mask, turned, deltas, other, outs, (depth, local), first, width)

    hidden = jnp.concatenate(hiddens, axis=1)
    share = hidden.shape[0] // (reach + 1)

    def piece(hop):
        start = jnp.where(on_right, hop, reach - hop) * share
        return lax.dynamic_slice_in_dim(hidden, start, share, axis=0)

    result = piece(0)
    for hop in range(1, reach + 1):
        moved = lax.ppermute(piece(hop), "row", [(left, left - hop), (right, right + hop)])
        result = pick(distance == hop, moved, result)
    return (result, *outs)


def solution(mesh):
    placed = (P("col", "row"), P("row", "col"), P("row", "col"), P("row", "col"), P("row", "col"))
    return jax.shard_map(
        functools.partial(on_device, ring=mesh.shape["row"]),
        mesh=mesh,
        in_specs=placed,
        out_specs=(P("row", "col"), P("row", "col"), P("row", "col")),
        check_vma=False,
    )
```

```python
import functools

import jax
import jax.numpy as jnp
from jax import lax
from jax.experimental import pallas as pl
from jax.experimental.pallas import tpu as pltpu
from jax.sharding import PartitionSpec as P

BLOCK = 128
GROUPS = 16
AHEAD = 6
VMEM_LIMIT = 48 * 1024 * 1024


def params():
    return pltpu.CompilerParams(vmem_limit_bytes=VMEM_LIMIT)


def cost():
    return pl.CostEstimate(flops=1000, bytes_accessed=1000, transcendentals=0)


def chunk_widths(local):
    units = local // BLOCK
    if units < 4 or units % 2:
        return [BLOCK] * units
    return [2 * BLOCK] * (units // 2 - 1) + [BLOCK] * 2


def put(ref, value):
    rows, cols = value.shape
    grouped = value.reshape(GROUPS, rows // GROUPS, cols)
    top = jnp.max(jnp.abs(grouped), axis=1)
    power = jnp.floor(jnp.log2(jnp.maximum(top, 1e-30))) + 1.0
    codes = jnp.round(grouped * jnp.exp2(15.0 - power)[:, None, :])
    codes = jnp.clip(codes, -32767.0, 32767.0).reshape(rows, cols)
    ref[0:rows, :] = codes.astype(jnp.int32).astype(jnp.int16)
    ref[rows : rows + GROUPS, :] = power.astype(jnp.int32).astype(jnp.int16)


def scales(ref):
    rows = ref.shape[0] - GROUPS
    return jnp.exp2(ref[rows : rows + GROUPS, :].astype(jnp.int32).astype(jnp.float32) - 15.0)


def get(ref):
    rows = ref.shape[0] - GROUPS
    cols = ref.shape[1]
    codes = ref[0:rows, :].astype(jnp.int32).astype(jnp.float32)
    grouped = codes.reshape(GROUPS, rows // GROUPS, cols) * scales(ref)[:, None, :]
    return grouped.reshape(rows, cols)


def forward_kernel(place_ref, mask_ref, tokens_ref, gate_ref, up_ref, out_ref, total, held, *, first):
    step = pl.program_id(0)
    depth, width = gate_ref.shape
    for r in range(depth // BLOCK):
        rows = slice(r * BLOCK, (r + 1) * BLOCK)
        for q in range(width // BLOCK):
            cols = slice(q * BLOCK, (q + 1) * BLOCK)
            keep = mask_ref[step * (depth // BLOCK) + r, first + q] != 0
            gate = gate_ref[rows, cols]
            up = up_ref[rows, cols]
            held[rows, cols] = jnp.where(keep, gate, jnp.zeros_like(gate))
            held[rows, width + q * BLOCK : width + (q + 1) * BLOCK] = jnp.where(keep, up, jnp.zeros_like(up))
    part = jnp.dot(tokens_ref[...], held[...], preferred_element_type=jnp.float32)

    @pl.when(step == 0)
    def _():
        total[...] = part

    @pl.when(step > 0)
    def _():
        total[...] += part

    @pl.when(step == pl.num_programs(0) - 1)
    def _():
        put(out_ref, total[...])


def forward(place, mask, tokens, gate_weight, up_weight, start, width):
    count, depth = tokens.shape
    steps = max(1, depth // 512)
    deep = depth // steps
    weight = pl.BlockSpec((deep, width), lambda k, place, mask: (k, start // width))
    return pl.pallas_call(
        functools.partial(forward_kernel, first=start // BLOCK),
        grid_spec=pltpu.PrefetchScalarGridSpec(
            num_scalar_prefetch=2,
            grid=(steps,),
            in_specs=[pl.BlockSpec((count, deep), lambda k, place, mask: (0, k)), weight, weight],
            out_specs=pl.BlockSpec((count + GROUPS, 2 * width), lambda k, place, mask: (0, 0)),
            scratch_shapes=[
                pltpu.VMEM((count, 2 * width), jnp.float32),
                pltpu.VMEM((deep, 2 * width), jnp.bfloat16),
            ],
        ),
        out_shape=jax.ShapeDtypeStruct((count + GROUPS, 2 * width), jnp.int16),
        compiler_params=params(),
        cost_estimate=cost(),
        name="forward",
    )(place, mask, tokens, gate_weight, up_weight)


def add_kernel(place_ref, a_ref, b_ref, out_ref):
    put(out_ref, get(a_ref) + get(b_ref))


def add(place, a, b):
    spec = pl.BlockSpec(a.shape, lambda i, place: (0, 0))
    return pl.pallas_call(
        add_kernel,
        grid_spec=pltpu.PrefetchScalarGridSpec(
            num_scalar_prefetch=1, grid=(1,), in_specs=[spec, spec], out_specs=spec
        ),
        out_shape=jax.ShapeDtypeStruct(a.shape, a.dtype),
        compiler_params=params(),
        cost_estimate=cost(),
        name="add",
    )(place, a, b)


def turn_kernel(place_ref, value_ref, out_ref):
    out_ref[...] = value_ref[...].T


def turn(place, value):
    rows, cols = value.shape
    deep = min(512, cols)
    return pl.pallas_call(
        turn_kernel,
        grid_spec=pltpu.PrefetchScalarGridSpec(
            num_scalar_prefetch=1,
            grid=(cols // deep,),
            in_specs=[pl.BlockSpec((rows, deep), lambda i, place: (0, i))],
            out_specs=pl.BlockSpec((deep, rows), lambda i, place: (i, 0)),
        ),
        out_shape=jax.ShapeDtypeStruct((cols, rows), value.dtype),
        compiler_params=params(),
        cost_estimate=cost(),
        name="turn",
    )(place, value)


def weights_kernel(place_ref, mask_ref, turned_ref, back_ref, *rest, first, terms, devices):
    coded = rest[:terms]
    hidden_ref, gate_ref, up_ref, deltas, hidden = rest[-5:]
    step = pl.program_id(0)
    depth, width = gate_ref.shape
    count = deltas.shape[0]
    share = count // devices
    col, row = place_ref[0], place_ref[1]

    @pl.when(step == 0)
    def _():
        scale = [scales(ref) for ref in coded]
        size = min(share, count // GROUPS)
        for at in range(0, count, size):
            rows = slice(at, at + size)
            group = at // (count // GROUPS)
            both = sum(
                ref[rows, :].astype(jnp.int32).astype(jnp.float32) * s[group : group + 1, :]
                for ref, s in zip(coded, scale)
            )
            gate, up = both[:, :width], both[:, width:]
            slot = at // share
            other = (slot % (devices // 2)) * 2 + slot // (devices // 2)
            start = pl.multiple_of(jnp.bitwise_xor(col, other) * share + at % share, size)
            back = back_ref[pl.ds(start, size), :].astype(jnp.float32)
            sig = jax.nn.sigmoid(gate)
            silu = gate * sig
            hidden[rows, :] = (silu * up).astype(jnp.bfloat16)
            deltas[rows, :width] = (back * up * sig * (1.0 + gate * (1.0 - sig))).astype(jnp.bfloat16)
            deltas[rows, width:] = (back * silu).astype(jnp.bfloat16)
        owned = hidden_ref.shape[0]
        for at in range(0, owned, share):
            other = jnp.bitwise_xor(col, row * (owned // share) + at // share)
            slot = (other % 2) * (devices // 2) + other // 2
            hidden_ref[at : at + share, :] = hidden[pl.ds(pl.multiple_of(slot * share, share), share), :]

    total = jnp.dot(turned_ref[...], deltas[...], preferred_element_type=jnp.float32)
    for r in range(depth // BLOCK):
        rows = slice(r * BLOCK, (r + 1) * BLOCK)
        for q in range(width // BLOCK):
            cols = slice(q * BLOCK, (q + 1) * BLOCK)
            keep = mask_ref[step * (depth // BLOCK) + r, first + q].astype(jnp.float32)
            gate_ref[rows, cols] = total[rows, cols] * keep
            up_ref[rows, cols] = total[rows, width + q * BLOCK : width + (q + 1) * BLOCK] * keep


def weight_grads(place, mask, turned, back, coded, previous, shapes, start, width, devices):
    depth, count = turned.shape
    owned = shapes[0].shape[0]
    steps = max(1, depth // 512)
    deep = depth // steps
    message = pl.BlockSpec((count + GROUPS, 2 * width), lambda m, place, mask: (0, 0))
    out = pl.BlockSpec((deep, width), lambda m, place, mask: (m, start // width))
    return pl.pallas_call(
        functools.partial(weights_kernel, first=start // BLOCK, terms=len(coded), devices=devices),
        grid_spec=pltpu.PrefetchScalarGridSpec(
            num_scalar_prefetch=2,
            grid=(steps,),
            in_specs=[
                pl.BlockSpec((deep, count), lambda m, place, mask: (m, 0)),
                pl.BlockSpec((count, width), lambda m, place, mask: (0, start // width)),
            ]
            + [message] * len(coded)
            + [pl.BlockSpec(memory_space=pl.ANY)] * len(previous),
            out_specs=[pl.BlockSpec((owned, width), lambda m, place, mask: (0, start // width)), out, out],
            scratch_shapes=[
                pltpu.VMEM((count, 2 * width), jnp.bfloat16),
                pltpu.VMEM((count, width), jnp.bfloat16),
            ],
        ),
        out_shape=shapes,
        input_output_aliases={4 + len(coded) + i: i for i in range(len(previous))},
        compiler_params=params(),
        cost_estimate=cost(),
        name="weight_grads",
    )(place, mask, turned, back, *coded, *previous)


def tie(value, *others):
    return lax.optimization_barrier((value, *others))[0]


def pick(condition, a, b):
    return lax.select(jnp.broadcast_to(condition, a.shape), a, b)


def gather_tokens(tokens, devices):
    pieces = [tokens]
    for other in range(2, devices, 2):
        pieces.append(lax.ppermute(tokens, "col", [(i, i ^ other) for i in range(devices)]))
    mine = jnp.concatenate(pieces, axis=0)
    return jnp.concatenate([mine, lax.ppermute(mine, "col", [(i, i ^ 1) for i in range(devices)])], axis=0)


def on_device(tokens, gate_weight, up_weight, block_mask, hidden_grad, *, ring, devices):
    me = lax.axis_index("row")
    place = jnp.stack([lax.axis_index("col"), me]).astype(jnp.int32)
    depth, local = gate_weight.shape
    left, right = ring // 2 - 1, ring // 2
    reach = ring // 2 - 1
    distance = jnp.where(me >= right, me - right, left - me)
    shapes = [
        jax.ShapeDtypeStruct(hidden_grad.shape, jnp.bfloat16),
        jax.ShapeDtypeStruct((depth, local), jnp.float32),
        jax.ShapeDtypeStruct((depth, local), jnp.float32),
    ]

    def outward(value, hop):
        return lax.ppermute(value, "row", [(left - hop, left - hop - 1), (right + hop, right + hop + 1)])

    def inward(value, hop):
        return lax.ppermute(value, "row", [(left - hop - 1, left - hop), (right + hop + 1, right + hop)])

    def swap(value):
        return lax.ppermute(value, "row", [(left, right), (right, left)])

    back = lax.all_gather(hidden_grad, "row", axis=0, tiled=True)
    gathered = gather_tokens(tokens, devices)

    widths = chunk_widths(local)
    starts = [sum(widths[:c]) for c in range(len(widths))]
    chunks = len(widths)
    own, came, sums, across, terms = [], [], [], [], []
    outs = ()
    turned = None

    def ordered(kernel, *args):
        nonlocal place
        out = kernel(place, *args)
        place = tie(place, out[0] if isinstance(out, (list, tuple)) else out)
        return out

    def send_in(c):
        value = own[c]
        if reach:
            came.append(inward(value if c < 2 else tie(value, came[c - 2]), reach - 1))

    def run_forward(c):
        own.append(ordered(forward, block_mask, gathered, gate_weight, up_weight, starts[c], widths[c]))
        if c < 2:
            send_in(c)

    def run_in(c):
        total = own[c]
        for hop in reversed(range(reach)):
            arrived = came[c] if hop == reach - 1 else inward(total, hop)
            if hop == reach - 1 and c + 2 < chunks:
                send_in(c + 2)
            new = ordered(add, own[c], arrived)
            total = new if reach == 1 else pick(distance == hop, new, total)
        sums.append(total)
        across.append(swap(total))

    def run_out(c):
        coming = across[c]
        parts = [sums[c], coming]
        for hop in range(reach):
            arrived = outward(ordered(add, own[c], coming), hop)
            if reach == 1:
                parts.append(arrived)
            else:
                coming = pick(distance == hop + 1, arrived, coming)
                parts[1] = coming
        terms.append(parts)

    ahead = min(AHEAD, chunks)
    for c in range(min(ahead, chunks)):
        run_forward(c)
    turned = ordered(turn, gathered)
    for c in range(chunks + 2):
        if c < chunks:
            run_in(c)
        if 0 <= c - 1 < chunks:
            run_out(c - 1)
        if c + ahead < chunks:
            run_forward(c + ahead)
        if c >= 2:
            d = c - 2
            outs = ordered(
                weight_grads, block_mask, turned, back, terms[d], outs, shapes, starts[d], widths[d], devices
            )
    return tuple(outs)


def solution(mesh):
    placed = (P("col", "row"), P("row", "col"), P("row", "col"), P("row", "col"), P("row", "col"))
    return jax.shard_map(
        functools.partial(on_device, ring=mesh.shape["row"], devices=mesh.shape["col"]),
        mesh=mesh,
        in_specs=placed,
        out_specs=(P("row", "col"), P("row", "col"), P("row", "col")),
        check_vma=False,
    )
```

```python
import functools

import jax
import jax.numpy as jnp
from jax import lax
from jax.experimental import pallas as pl
from jax.experimental.pallas import tpu as pltpu
from jax.sharding import PartitionSpec as P

BLOCK = 128
GROUPS = 16
AHEAD = 4
ROWS = 1024
VMEM_LIMIT = 48 * 1024 * 1024


def params():
    return pltpu.CompilerParams(vmem_limit_bytes=VMEM_LIMIT)


def cost():
    return pl.CostEstimate(flops=4 * 10**9, bytes_accessed=10**7, transcendentals=0)


def chunk_widths(local):
    part = part_width(local)
    parts = local // part
    inner = [2 * part] * ((parts - 2) // 2)
    return [part] + inner + [part] * (parts - 1 - 2 * len(inner))


def part_width(local):
    return 2 * BLOCK if local % (2 * BLOCK) == 0 and local >= 8 * BLOCK else BLOCK


def put(ref, value):
    rows, cols = value.shape
    grouped = value.reshape(GROUPS, rows // GROUPS, cols)
    top = jnp.max(jnp.abs(grouped), axis=1)
    power = jnp.floor(jnp.log2(jnp.maximum(top, 1e-30))) + 1.0
    codes = jnp.round(grouped * jnp.exp2(15.0 - power)[:, None, :])
    codes = jnp.clip(codes, -32767.0, 32767.0).reshape(rows, cols)
    ref[0:rows, :] = codes.astype(jnp.int32).astype(jnp.int16)
    ref[rows : rows + GROUPS, :] = power.astype(jnp.int32).astype(jnp.int16)


def scales(ref):
    rows = ref.shape[0] - GROUPS
    return jnp.exp2(ref[rows : rows + GROUPS, :].astype(jnp.int32).astype(jnp.float32) - 15.0)


def get(ref):
    rows = ref.shape[0] - GROUPS
    cols = ref.shape[1]
    codes = ref[0:rows, :].astype(jnp.int32).astype(jnp.float32)
    grouped = codes.reshape(GROUPS, rows // GROUPS, cols) * scales(ref)[:, None, :]
    return grouped.reshape(rows, cols)


def forward_kernel(place_ref, mask_ref, tokens_ref, gate_ref, up_ref, out_ref, held, *, first):
    depth, width = gate_ref.shape
    base = first + pl.program_id(0) * (width // BLOCK)
    for r in range(depth // BLOCK):
        rows = slice(r * BLOCK, (r + 1) * BLOCK)
        for q in range(width // BLOCK):
            cols = slice(q * BLOCK, (q + 1) * BLOCK)
            keep = jnp.full((BLOCK, BLOCK), mask_ref[r, base + q].astype(jnp.float32)).astype(jnp.bfloat16)
            held[rows, cols] = gate_ref[rows, cols] * keep
            held[rows, width + q * BLOCK : width + (q + 1) * BLOCK] = up_ref[rows, cols] * keep
    put(out_ref, jnp.dot(tokens_ref[...], held[...], preferred_element_type=jnp.float32))


def forward(place, mask, tokens, gate_weight, up_weight, start, width):
    count, depth = tokens.shape
    part = part_width(gate_weight.shape[1])
    weight = pl.BlockSpec((depth, part), lambda j, place, mask: (0, start // part + j))
    return pl.pallas_call(
        functools.partial(forward_kernel, first=start // BLOCK),
        grid_spec=pltpu.PrefetchScalarGridSpec(
            num_scalar_prefetch=2,
            grid=(width // part,),
            in_specs=[pl.BlockSpec((count, depth), lambda j, place, mask: (0, 0)), weight, weight],
            out_specs=pl.BlockSpec((count + GROUPS, 2 * part), lambda j, place, mask: (0, j)),
            scratch_shapes=[pltpu.VMEM((depth, 2 * part), jnp.bfloat16)],
        ),
        out_shape=jax.ShapeDtypeStruct((count + GROUPS, 2 * width), jnp.int16),
        compiler_params=params(),
        cost_estimate=cost(),
        name="forward",
    )(place, mask, tokens, gate_weight, up_weight)


def add_kernel(place_ref, a_ref, b_ref, out_ref):
    put(out_ref, get(a_ref) + get(b_ref))


def add(place, a, b, part):
    rows, cols = a.shape
    spec = pl.BlockSpec((rows, 2 * part), lambda j, place: (0, j))
    return pl.pallas_call(
        add_kernel,
        grid_spec=pltpu.PrefetchScalarGridSpec(
            num_scalar_prefetch=1, grid=(cols // (2 * part),), in_specs=[spec, spec], out_specs=spec
        ),
        out_shape=jax.ShapeDtypeStruct(a.shape, a.dtype),
        compiler_params=params(),
        cost_estimate=cost(),
        name="add",
    )(place, a, b)


def turn_kernel(place_ref, value_ref, out_ref):
    out_ref[...] = value_ref[...].T


def turn(place, value):
    rows, cols = value.shape
    deep = min(512, cols)
    return pl.pallas_call(
        turn_kernel,
        grid_spec=pltpu.PrefetchScalarGridSpec(
            num_scalar_prefetch=1,
            grid=(cols // deep,),
            in_specs=[pl.BlockSpec((rows, deep), lambda i, place: (0, i))],
            out_specs=pl.BlockSpec((deep, rows), lambda i, place: (i, 0)),
        ),
        out_shape=jax.ShapeDtypeStruct((cols, rows), value.dtype),
        compiler_params=params(),
        cost_estimate=cost(),
        name="turn",
    )(place, value)


def weights_kernel(place_ref, mask_ref, turned_ref, back_ref, *rest, first, terms, devices):
    coded = rest[:terms]
    hidden_ref, gate_ref, up_ref, deltas, hidden = rest[-5:]
    step = pl.program_id(1)
    depth, width = gate_ref.shape
    base = first + pl.program_id(0) * (width // BLOCK)
    count = deltas.shape[0]
    share = count // devices
    col, row = place_ref[0], place_ref[1]

    @pl.when(step == 0)
    def _():
        scale = [scales(ref) for ref in coded]
        size = min(share, count // GROUPS)
        for at in range(0, count, size):
            rows = slice(at, at + size)
            group = at // (count // GROUPS)
            both = sum(
                ref[rows, :].astype(jnp.int32).astype(jnp.float32) * s[group : group + 1, :]
                for ref, s in zip(coded, scale)
            )
            gate, up = both[:, :width], both[:, width:]
            slot = at // share
            other = (slot % (devices // 2)) * 2 + slot // (devices // 2)
            start = pl.multiple_of(jnp.bitwise_xor(col, other) * share + at % share, size)
            back = back_ref[pl.ds(start, size), :].astype(jnp.float32)
            sig = jax.nn.sigmoid(gate)
            silu = gate * sig
            hidden[rows, :] = (silu * up).astype(jnp.bfloat16)
            deltas[rows, :width] = (back * up * sig * (1.0 + gate * (1.0 - sig))).astype(jnp.bfloat16)
            deltas[rows, width:] = (back * silu).astype(jnp.bfloat16)
        owned = hidden_ref.shape[0]
        for at in range(0, owned, share):
            other = jnp.bitwise_xor(col, row * (owned // share) + at // share)
            slot = (other % 2) * (devices // 2) + other // 2
            hidden_ref[at : at + share, :] = hidden[pl.ds(pl.multiple_of(slot * share, share), share), :]

    total = jnp.dot(turned_ref[...], deltas[...], preferred_element_type=jnp.float32)
    for r in range(depth // BLOCK):
        rows = slice(r * BLOCK, (r + 1) * BLOCK)
        for q in range(width // BLOCK):
            cols = slice(q * BLOCK, (q + 1) * BLOCK)
            keep = mask_ref[step * (depth // BLOCK) + r, base + q].astype(jnp.float32)
            gate_ref[rows, cols] = total[rows, cols] * keep
            up_ref[rows, cols] = total[rows, width + q * BLOCK : width + (q + 1) * BLOCK] * keep


def weight_grads(place, mask, turned, back, coded, previous, shapes, start, width, devices):
    depth, count = turned.shape
    owned = shapes[0].shape[0]
    part = part_width(shapes[1].shape[1])
    deep = min(ROWS, depth)
    message = pl.BlockSpec((count + GROUPS, 2 * part), lambda j, m, place, mask: (0, j))
    out = pl.BlockSpec((deep, part), lambda j, m, place, mask: (m, start // part + j))
    return pl.pallas_call(
        functools.partial(weights_kernel, first=start // BLOCK, terms=len(coded), devices=devices),
        grid_spec=pltpu.PrefetchScalarGridSpec(
            num_scalar_prefetch=2,
            grid=(width // part, depth // deep),
            in_specs=[
                pl.BlockSpec((deep, count), lambda j, m, place, mask: (m, 0)),
                pl.BlockSpec((count, part), lambda j, m, place, mask: (0, start // part + j)),
            ]
            + [message] * len(coded)
            + [pl.BlockSpec(memory_space=pl.ANY)] * len(previous),
            out_specs=[pl.BlockSpec((owned, part), lambda j, m, place, mask: (0, start // part + j)), out, out],
            scratch_shapes=[
                pltpu.VMEM((count, 2 * part), jnp.bfloat16),
                pltpu.VMEM((count, part), jnp.bfloat16),
            ],
        ),
        out_shape=shapes,
        input_output_aliases={4 + len(coded) + i: i for i in range(len(previous))},
        compiler_params=params(),
        cost_estimate=cost(),
        name="weight_grads",
    )(place, mask, turned, back, *coded, *previous)


def tie(value, *others):
    return lax.optimization_barrier((value, *others))[0]


def pick(condition, a, b):
    return lax.select(jnp.broadcast_to(condition, a.shape), a, b)


def gather_tokens(tokens, devices):
    pieces = [tokens]
    for other in range(2, devices, 2):
        pieces.append(lax.ppermute(tokens, "col", [(i, i ^ other) for i in range(devices)]))
    mine = jnp.concatenate(pieces, axis=0)
    return jnp.concatenate([mine, lax.ppermute(mine, "col", [(i, i ^ 1) for i in range(devices)])], axis=0)


def on_device(tokens, gate_weight, up_weight, block_mask, hidden_grad, *, ring, devices):
    me = lax.axis_index("row")
    place = jnp.stack([lax.axis_index("col"), me]).astype(jnp.int32)
    depth, local = gate_weight.shape
    left, right = ring // 2 - 1, ring // 2
    reach = ring // 2 - 1
    distance = jnp.where(me >= right, me - right, left - me)
    shapes = [
        jax.ShapeDtypeStruct(hidden_grad.shape, jnp.bfloat16),
        jax.ShapeDtypeStruct((depth, local), jnp.float32),
        jax.ShapeDtypeStruct((depth, local), jnp.float32),
    ]

    def outward(value, hop):
        return lax.ppermute(value, "row", [(left - hop, left - hop - 1), (right + hop, right + hop + 1)])

    def inward(value, hop):
        return lax.ppermute(value, "row", [(left - hop - 1, left - hop), (right + hop + 1, right + hop)])

    def swap(value):
        return lax.ppermute(value, "row", [(left, right), (right, left)])

    back = lax.all_gather(hidden_grad, "row", axis=0, tiled=True)
    gathered = gather_tokens(tokens, devices)

    part = part_width(local)
    widths = chunk_widths(local)
    starts = [sum(widths[:c]) for c in range(len(widths))]
    chunks = len(widths)
    own, came, sums, across, terms = [], [], [], [], []
    outs = ()
    turned = None

    def ordered(kernel, *args):
        nonlocal place
        out = kernel(place, *args)
        place = tie(place, out[0] if isinstance(out, (list, tuple)) else out)
        return out

    def send_in(c):
        value = own[c]
        if reach:
            came.append(inward(value if c < 2 else tie(value, came[c - 2]), reach - 1))

    def run_forward(c):
        own.append(ordered(forward, block_mask, gathered, gate_weight, up_weight, starts[c], widths[c]))
        if c < 2:
            send_in(c)

    def run_in(c):
        total = own[c]
        for hop in reversed(range(reach)):
            arrived = came[c] if hop == reach - 1 else inward(total, hop)
            if hop == reach - 1 and c + 2 < chunks:
                send_in(c + 2)
            new = ordered(add, own[c], arrived, part)
            total = new if reach == 1 else pick(distance == hop, new, total)
        sums.append(total)
        across.append(swap(total))

    def run_out(c):
        coming = across[c]
        parts = [sums[c], coming]
        for hop in range(reach):
            arrived = outward(ordered(add, own[c], coming, part), hop)
            if reach == 1:
                parts.append(arrived)
            else:
                coming = pick(distance == hop + 1, arrived, coming)
                parts[1] = coming
        terms.append(parts)

    ahead = min(AHEAD, chunks)
    for c in range(min(ahead, chunks)):
        run_forward(c)
    turned = ordered(turn, gathered)
    for c in range(chunks + 2):
        if c < chunks:
            run_in(c)
        if 0 <= c - 1 < chunks:
            run_out(c - 1)
        if c + ahead < chunks:
            run_forward(c + ahead)
        if c >= 2:
            d = c - 2
            outs = ordered(
                weight_grads, block_mask, turned, back, terms[d], outs, shapes, starts[d], widths[d], devices
            )
    return tuple(outs)


def solution(mesh):
    placed = (P("col", "row"), P("row", "col"), P("row", "col"), P("row", "col"), P("row", "col"))
    return jax.shard_map(
        functools.partial(on_device, ring=mesh.shape["row"], devices=mesh.shape["col"]),
        mesh=mesh,
        in_specs=placed,
        out_specs=(P("row", "col"), P("row", "col"), P("row", "col")),
        check_vma=False,
    )
```

```python
import functools

import jax
import jax.numpy as jnp
from jax import lax
from jax.experimental import pallas as pl
from jax.experimental.pallas import tpu as pltpu
from jax.sharding import PartitionSpec as P

BLOCK = 128
GROUPS = 16
AHEAD = 4
ROWS = 1024
VMEM_LIMIT = 48 * 1024 * 1024


def params():
    return pltpu.CompilerParams(vmem_limit_bytes=VMEM_LIMIT)


def cost():
    return pl.CostEstimate(flops=4 * 10**9, bytes_accessed=10**7, transcendentals=0)


def chunk_widths(local):
    part = part_width(local)
    parts = local // part
    inner = [2 * part] * ((parts - 2) // 2)
    return [part] + inner + [part] * (parts - 1 - 2 * len(inner))


def part_width(local):
    return 2 * BLOCK if local % (2 * BLOCK) == 0 and local >= 8 * BLOCK else BLOCK


def put(ref, value):
    rows, cols = value.shape
    grouped = value.reshape(GROUPS, rows // GROUPS, cols)
    top = jnp.max(jnp.abs(grouped), axis=1)
    power = jnp.floor(jnp.log2(jnp.maximum(top, 1e-30))) + 1.0
    codes = jnp.round(grouped * jnp.exp2(15.0 - power)[:, None, :])
    codes = jnp.clip(codes, -32767.0, 32767.0).reshape(rows, cols)
    ref[0:rows, :] = codes.astype(jnp.int32).astype(jnp.int16)
    ref[rows : rows + GROUPS, :] = power.astype(jnp.int32).astype(jnp.int16)


def scales(ref):
    rows = ref.shape[0] - GROUPS
    return jnp.exp2(ref[rows : rows + GROUPS, :].astype(jnp.int32).astype(jnp.float32) - 15.0)


def get(ref):
    rows = ref.shape[0] - GROUPS
    cols = ref.shape[1]
    codes = ref[0:rows, :].astype(jnp.int32).astype(jnp.float32)
    grouped = codes.reshape(GROUPS, rows // GROUPS, cols) * scales(ref)[:, None, :]
    return grouped.reshape(rows, cols)


def forward_kernel(place_ref, mask_ref, tokens_ref, gate_ref, up_ref, out_ref, held, *, first):
    depth, width = gate_ref.shape
    base = first + pl.program_id(0) * (width // BLOCK)
    for r in range(depth // BLOCK):
        rows = slice(r * BLOCK, (r + 1) * BLOCK)
        for q in range(width // BLOCK):
            cols = slice(q * BLOCK, (q + 1) * BLOCK)
            keep = jnp.full((BLOCK, BLOCK), mask_ref[r, base + q].astype(jnp.float32)).astype(jnp.bfloat16)
            held[rows, cols] = gate_ref[rows, cols] * keep
            held[rows, width + q * BLOCK : width + (q + 1) * BLOCK] = up_ref[rows, cols] * keep
    put(out_ref, jnp.dot(tokens_ref[...], held[...], preferred_element_type=jnp.float32))


def forward(place, mask, tokens, gate_weight, up_weight, start, width):
    count, depth = tokens.shape
    part = part_width(gate_weight.shape[1])
    weight = pl.BlockSpec((depth, part), lambda j, place, mask: (0, start // part + j))
    return pl.pallas_call(
        functools.partial(forward_kernel, first=start // BLOCK),
        grid_spec=pltpu.PrefetchScalarGridSpec(
            num_scalar_prefetch=2,
            grid=(width // part,),
            in_specs=[pl.BlockSpec((count, depth), lambda j, place, mask: (0, 0)), weight, weight],
            out_specs=pl.BlockSpec((count + GROUPS, 2 * part), lambda j, place, mask: (0, j)),
            scratch_shapes=[pltpu.VMEM((depth, 2 * part), jnp.bfloat16)],
        ),
        out_shape=jax.ShapeDtypeStruct((count + GROUPS, 2 * width), jnp.int16),
        compiler_params=params(),
        cost_estimate=cost(),
        name="forward",
    )(place, mask, tokens, gate_weight, up_weight)


def add_kernel(place_ref, a_ref, b_ref, out_ref):
    put(out_ref, get(a_ref) + get(b_ref))


def add(place, a, b, part):
    rows, cols = a.shape
    spec = pl.BlockSpec((rows, 2 * part), lambda j, place: (0, j))
    return pl.pallas_call(
        add_kernel,
        grid_spec=pltpu.PrefetchScalarGridSpec(
            num_scalar_prefetch=1, grid=(cols // (2 * part),), in_specs=[spec, spec], out_specs=spec
        ),
        out_shape=jax.ShapeDtypeStruct(a.shape, a.dtype),
        compiler_params=params(),
        cost_estimate=cost(),
        name="add",
    )(place, a, b)


def turn_kernel(place_ref, value_ref, out_ref):
    out_ref[...] = value_ref[...].T


def turn(place, value):
    rows, cols = value.shape
    deep = min(512, cols)
    return pl.pallas_call(
        turn_kernel,
        grid_spec=pltpu.PrefetchScalarGridSpec(
            num_scalar_prefetch=1,
            grid=(cols // deep,),
            in_specs=[pl.BlockSpec((rows, deep), lambda i, place: (0, i))],
            out_specs=pl.BlockSpec((deep, rows), lambda i, place: (i, 0)),
        ),
        out_shape=jax.ShapeDtypeStruct((cols, rows), value.dtype),
        compiler_params=params(),
        cost_estimate=cost(),
        name="turn",
    )(place, value)


def weights_kernel(place_ref, mask_ref, turned_ref, back_ref, *rest, first, terms, devices):
    coded = rest[:terms]
    hidden_ref, gate_ref, up_ref, deltas, hidden = rest[-5:]
    step = pl.program_id(1)
    depth, width = gate_ref.shape
    base = first + pl.program_id(0) * (width // BLOCK)
    count = deltas.shape[0]
    share = count // devices
    col, row = place_ref[0], place_ref[1]
    owned = hidden_ref.shape[0]
    ahead = (count // owned - 1 - row) * owned

    @pl.when(step == 0)
    def _():
        scale = [scales(ref) for ref in coded]
        size = min(share, count // GROUPS)
        for at in range(0, count, size):
            rows = slice(at, at + size)
            group = at // (count // GROUPS)
            both = sum(
                ref[rows, :].astype(jnp.int32).astype(jnp.float32) * s[group : group + 1, :]
                for ref, s in zip(coded, scale)
            )
            gate, up = both[:, :width], both[:, width:]
            slot = at // share
            other = (slot % (devices // 2)) * 2 + slot // (devices // 2)
            start = pl.multiple_of(ahead + jnp.bitwise_xor(col, other) * share + at % share, size)
            back = back_ref[pl.ds(start, size), :].astype(jnp.float32)
            sig = jax.nn.sigmoid(gate)
            silu = gate * sig
            hidden[rows, :] = (silu * up).astype(jnp.bfloat16)
            deltas[rows, :width] = (back * up * sig * (1.0 + gate * (1.0 - sig))).astype(jnp.bfloat16)
            deltas[rows, width:] = (back * silu).astype(jnp.bfloat16)
        for at in range(0, owned, share):
            other = jnp.bitwise_xor(col, row * (owned // share) + at // share)
            slot = (other % 2) * (devices // 2) + other // 2
            hidden_ref[at : at + share, :] = hidden[pl.ds(pl.multiple_of(slot * share, share), share), :]

    total = jnp.dot(turned_ref[...], deltas[...], preferred_element_type=jnp.float32)
    for r in range(depth // BLOCK):
        rows = slice(r * BLOCK, (r + 1) * BLOCK)
        for q in range(width // BLOCK):
            cols = slice(q * BLOCK, (q + 1) * BLOCK)
            keep = mask_ref[step * (depth // BLOCK) + r, base + q].astype(jnp.float32)
            gate_ref[rows, cols] = total[rows, cols] * keep
            up_ref[rows, cols] = total[rows, width + q * BLOCK : width + (q + 1) * BLOCK] * keep


def weight_grads(place, mask, turned, back, coded, previous, shapes, start, width, devices):
    depth, count = turned.shape
    owned = shapes[0].shape[0]
    part = part_width(shapes[1].shape[1])
    deep = min(ROWS, depth)
    message = pl.BlockSpec((count + GROUPS, 2 * part), lambda j, m, place, mask: (0, j))
    out = pl.BlockSpec((deep, part), lambda j, m, place, mask: (m, start // part + j))
    return pl.pallas_call(
        functools.partial(weights_kernel, first=start // BLOCK, terms=len(coded), devices=devices),
        grid_spec=pltpu.PrefetchScalarGridSpec(
            num_scalar_prefetch=2,
            grid=(width // part, depth // deep),
            in_specs=[
                pl.BlockSpec((deep, count), lambda j, m, place, mask: (m, 0)),
                pl.BlockSpec((back.shape[0], part), lambda j, m, place, mask: (0, start // part + j)),
            ]
            + [message] * len(coded)
            + [pl.BlockSpec(memory_space=pl.ANY)] * len(previous),
            out_specs=[pl.BlockSpec((owned, part), lambda j, m, place, mask: (0, start // part + j)), out, out],
            scratch_shapes=[
                pltpu.VMEM((count, 2 * part), jnp.bfloat16),
                pltpu.VMEM((count, part), jnp.bfloat16),
            ],
        ),
        out_shape=shapes,
        input_output_aliases={4 + len(coded) + i: i for i in range(len(previous))},
        compiler_params=params(),
        cost_estimate=cost(),
        name="weight_grads",
    )(place, mask, turned, back, *coded, *previous)


def tie(value, *others):
    return lax.optimization_barrier((value, *others))[0]


def pick(condition, a, b):
    return lax.select(jnp.broadcast_to(condition, a.shape), a, b)


def gather_tokens(tokens, devices, others):
    pieces = [tokens]
    for other in range(2, devices, 2):
        pieces.append(lax.ppermute(tokens, "col", [(i, i ^ other) for i in range(devices)]))
    mine = tie(jnp.concatenate(pieces, axis=0), *others)
    return jnp.concatenate([mine, lax.ppermute(mine, "col", [(i, i ^ 1) for i in range(devices)])], axis=0)


def on_device(tokens, gate_weight, up_weight, block_mask, hidden_grad, *, ring, devices):
    me = lax.axis_index("row")
    place = jnp.stack([lax.axis_index("col"), me]).astype(jnp.int32)
    depth, local = gate_weight.shape
    left, right = ring // 2 - 1, ring // 2
    reach = ring // 2 - 1
    distance = jnp.where(me >= right, me - right, left - me)
    shapes = [
        jax.ShapeDtypeStruct(hidden_grad.shape, jnp.bfloat16),
        jax.ShapeDtypeStruct((depth, local), jnp.float32),
        jax.ShapeDtypeStruct((depth, local), jnp.float32),
    ]

    def outward(value, hop):
        return lax.ppermute(value, "row", [(left - hop, left - hop - 1), (right + hop, right + hop + 1)])

    def inward(value, hop):
        return lax.ppermute(value, "row", [(left - hop - 1, left - hop), (right + hop + 1, right + hop)])

    def swap(value):
        return lax.ppermute(value, "row", [(left, right), (right, left)])


    part = part_width(local)
    widths = chunk_widths(local)
    starts = [sum(widths[:c]) for c in range(len(widths))]
    chunks = len(widths)
    before, after = [hidden_grad], [hidden_grad]

    def pass_on(sources):
        before.append(lax.ppermute(sources[0], "row", [(i, i + 1) for i in range(ring - 1)]))
        after.append(lax.ppermute(sources[1], "row", [(i + 1, i) for i in range(ring - 1)]))

    pass_on((hidden_grad, hidden_grad))
    gathered = gather_tokens(tokens, devices, (before[-1], after[-1]))
    own, came, sums, across, terms = [], [], [], [], []
    outs = ()
    turned = None

    def ordered(kernel, *args):
        nonlocal place
        out = kernel(place, *args)
        place = tie(place, out[0] if isinstance(out, (list, tuple)) else out)
        return out

    def send_in(c):
        value = own[c]
        if reach:
            came.append(inward(value if c < 2 else tie(value, came[c - 2]), reach - 1))

    def run_forward(c):
        own.append(ordered(forward, block_mask, gathered, gate_weight, up_weight, starts[c], widths[c]))
        if c < 2:
            send_in(c)

    def run_in(c):
        total = own[c]
        for hop in reversed(range(reach)):
            arrived = came[c] if hop == reach - 1 else inward(total, hop)
            if hop == reach - 1 and c + 2 < chunks:
                send_in(c + 2)
            new = ordered(add, own[c], arrived, part)
            total = new if reach == 1 else pick(distance == hop, new, total)
        sums.append(total)
        across.append(swap(total))

    def run_out(c):
        coming = across[c]
        parts = [sums[c], coming]
        for hop in range(reach):
            arrived = outward(ordered(add, own[c], coming, part), hop)
            if reach == 1:
                parts.append(arrived)
            else:
                coming = pick(distance == hop + 1, arrived, coming)
                parts[1] = coming
        terms.append(parts)

    ahead = min(AHEAD, chunks)
    for hop in range(2, ring):
        if hop == 2:
            pass_on((before[-1], after[-1]))
            run_forward(0)
        else:
            pass_on(lax.optimization_barrier((before[-1], after[-1], place))[:2])
    for c in range(len(own), ahead):
        run_forward(c)
    turned = ordered(turn, gathered)
    back = jnp.concatenate(lax.optimization_barrier((*before[:0:-1], *after, place))[:-1], axis=0)
    for c in range(chunks + 2):
        if c < chunks:
            run_in(c)
        if 0 <= c - 1 < chunks:
            run_out(c - 1)
        if c + ahead < chunks:
            run_forward(c + ahead)
        if c >= 2:
            d = c - 2
            outs = ordered(
                weight_grads, block_mask, turned, back, terms[d], outs, shapes, starts[d], widths[d], devices
            )
    return tuple(outs)


def solution(mesh):
    placed = (P("col", "row"), P("row", "col"), P("row", "col"), P("row", "col"), P("row", "col"))
    return jax.shard_map(
        functools.partial(on_device, ring=mesh.shape["row"], devices=mesh.shape["col"]),
        mesh=mesh,
        in_specs=placed,
        out_specs=(P("row", "col"), P("row", "col"), P("row", "col")),
        check_vma=False,
    )
```

```python
import functools

import jax
import jax.numpy as jnp
from jax import lax
from jax.experimental import pallas as pl
from jax.experimental.pallas import tpu as pltpu
from jax.sharding import PartitionSpec as P

BLOCK = 128
GROUPS = 16
CHUNK = 3
AHEAD = 3
LAG = 3
ROWS = 512
VMEM_LIMIT = 48 * 1024 * 1024


def params():
    return pltpu.CompilerParams(vmem_limit_bytes=VMEM_LIMIT)


def cost(megaflops=1):
    return pl.CostEstimate(flops=megaflops * 10**6, bytes_accessed=megaflops * 2500, transcendentals=0)


def chunk_widths(local):
    units = local // BLOCK
    rest = [CHUNK] * ((units - 1) // CHUNK)
    return [BLOCK * u for u in [units - sum(rest), *rest]]


def put(ref, value):
    rows, cols = value.shape
    grouped = value.reshape(GROUPS, rows // GROUPS, cols)
    top = jnp.max(jnp.abs(grouped), axis=1)
    power = jnp.floor(jnp.log2(jnp.maximum(top, 1e-30))) + 1.0
    codes = jnp.round(grouped * jnp.exp2(15.0 - power)[:, None, :])
    codes = jnp.clip(codes, -32767.0, 32767.0).reshape(rows, cols)
    ref[0:rows, :] = codes.astype(jnp.int32).astype(jnp.int16)
    ref[rows : rows + GROUPS, :] = power.astype(jnp.int32).astype(jnp.int16)


def scales(ref):
    rows = ref.shape[0] - GROUPS
    return jnp.exp2(ref[rows : rows + GROUPS, :].astype(jnp.int32).astype(jnp.float32) - 15.0)


def get(ref):
    rows = ref.shape[0] - GROUPS
    cols = ref.shape[1]
    codes = ref[0:rows, :].astype(jnp.int32).astype(jnp.float32)
    grouped = codes.reshape(GROUPS, rows // GROUPS, cols) * scales(ref)[:, None, :]
    return grouped.reshape(rows, cols)


def forward_kernel(place_ref, mask_ref, tokens_ref, gate_ref, up_ref, out_ref, held, *, first):
    depth = gate_ref.shape[0]
    for r in range(depth // BLOCK):
        rows = slice(r * BLOCK, (r + 1) * BLOCK)
        keep = mask_ref[r, first + pl.program_id(0)].astype(jnp.float32)
        keep = jnp.full((BLOCK, BLOCK), keep).astype(jnp.bfloat16)
        held[rows, :BLOCK] = gate_ref[rows, :] * keep
        held[rows, BLOCK:] = up_ref[rows, :] * keep
    put(out_ref, jnp.dot(tokens_ref[...], held[...], preferred_element_type=jnp.float32))


def forward(place, mask, tokens, gate_weight, up_weight, start, width):
    count, depth = tokens.shape
    weight = pl.BlockSpec((depth, BLOCK), lambda j, place, mask: (0, start // BLOCK + j))
    return pl.pallas_call(
        functools.partial(forward_kernel, first=start // BLOCK),
        grid_spec=pltpu.PrefetchScalarGridSpec(
            num_scalar_prefetch=2,
            grid=(width // BLOCK,),
            in_specs=[pl.BlockSpec((count, depth), lambda j, place, mask: (0, 0)), weight, weight],
            out_specs=pl.BlockSpec((count + GROUPS, 2 * BLOCK), lambda j, place, mask: (0, j)),
            scratch_shapes=[pltpu.VMEM((depth, 2 * BLOCK), jnp.bfloat16)],
        ),
        out_shape=jax.ShapeDtypeStruct((count + GROUPS, 2 * width), jnp.int16),
        compiler_params=params(),
        cost_estimate=cost(8000),
        name="forward",
    )(place, mask, tokens, gate_weight, up_weight)


def add_kernel(place_ref, a_ref, b_ref, out_ref):
    inner = place_ref[2] != 0

    @pl.when(inner)
    def _():
        put(out_ref, get(a_ref) + get(b_ref))

    @pl.when(jnp.logical_not(inner))
    def _():
        out_ref[...] = a_ref[...]


def add(place, a, b):
    return pl.pallas_call(
        add_kernel,
        grid_spec=pltpu.PrefetchScalarGridSpec(
            num_scalar_prefetch=1,
            grid=(1,),
            in_specs=[pl.BlockSpec(x.shape, lambda j, place: (0, 0)) for x in (a, b)],
            out_specs=pl.BlockSpec(a.shape, lambda j, place: (0, 0)),
        ),
        out_shape=jax.ShapeDtypeStruct(a.shape, a.dtype),
        compiler_params=params(),
        cost_estimate=cost(),
        name="add",
    )(place, a, b)


def reply_kernel(place_ref, a_ref, b_ref, next_ref, out_ref):
    inner = place_ref[2] != 0

    @pl.when(inner)
    def _():
        put(out_ref.at[:, 0 : a_ref.shape[1]], get(a_ref) + get(b_ref))

    @pl.when(jnp.logical_not(inner))
    def _():
        out_ref[...] = next_ref[...]


def reply(place, a, b, following):
    return pl.pallas_call(
        reply_kernel,
        grid_spec=pltpu.PrefetchScalarGridSpec(
            num_scalar_prefetch=1,
            grid=(1,),
            in_specs=[pl.BlockSpec(x.shape, lambda j, place: (0, 0)) for x in (a, b, following)],
            out_specs=pl.BlockSpec(following.shape, lambda j, place: (0, 0)),
        ),
        out_shape=jax.ShapeDtypeStruct(following.shape, a.dtype),
        compiler_params=params(),
        cost_estimate=cost(),
        name="reply",
    )(place, a, b, following)


def turn_kernel(place_ref, value_ref, out_ref):
    out_ref[...] = value_ref[...].T


def turn(place, value):
    rows, cols = value.shape
    deep = min(512, cols)
    return pl.pallas_call(
        turn_kernel,
        grid_spec=pltpu.PrefetchScalarGridSpec(
            num_scalar_prefetch=1,
            grid=(cols // deep,),
            in_specs=[pl.BlockSpec((rows, deep), lambda i, place: (0, i))],
            out_specs=pl.BlockSpec((deep, rows), lambda i, place: (i, 0)),
        ),
        out_shape=jax.ShapeDtypeStruct((cols, rows), value.dtype),
        compiler_params=params(),
        cost_estimate=cost(8000),
        name="turn",
    )(place, value)


def weights_kernel(place_ref, mask_ref, turned_ref, back_ref, own_ref, across_ref, out_ref, *rest, first, devices):
    hidden_ref, gate_ref, up_ref, deltas, hidden = rest[-5:]
    step = pl.program_id(0)
    depth, width = gate_ref.shape
    count = deltas.shape[0]
    share = count // devices
    col, row, inner = place_ref[0], place_ref[1], place_ref[2] != 0
    owned = hidden_ref.shape[0]

    @pl.when(step == 0)
    def _():
        span = 2 * width
        power = jnp.where(inner, across_ref[count : count + GROUPS, :span], out_ref[count : count + GROUPS, :span])
        scale = jnp.exp2(power.astype(jnp.int32).astype(jnp.float32) - 15.0)
        own_scale = scales(own_ref)
        size = min(share, count // GROUPS)
        for at in range(0, count, size):
            rows = slice(at, at + size)
            group = at // (count // GROUPS)
            slot = at // share
            other = (slot % (devices // 2)) * 2 + slot // (devices // 2)
            token = jnp.bitwise_xor(col, other) * share + at % share
            source = place_ref[3 + token // owned]
            start = pl.multiple_of(source * owned + token % owned, size)
            codes = jnp.where(inner, across_ref[rows, :span], out_ref[rows, :span])
            both = (
                own_ref[rows, :].astype(jnp.int32).astype(jnp.float32) * own_scale[group : group + 1, :]
                + codes.astype(jnp.int32).astype(jnp.float32) * scale[group : group + 1, :]
            )
            for q in range(width // BLOCK):
                cols = slice(q * BLOCK, (q + 1) * BLOCK)
                gate = both[:, 2 * q * BLOCK : (2 * q + 1) * BLOCK]
                up = both[:, (2 * q + 1) * BLOCK : (2 * q + 2) * BLOCK]
                back = back_ref[pl.ds(start, size), cols].astype(jnp.float32)
                sig = jax.nn.sigmoid(gate)
                silu = gate * sig
                hidden[rows, cols] = (silu * up).astype(jnp.bfloat16)
                delta = back * up * sig * (1.0 + gate * (1.0 - sig))
                deltas[rows, 2 * q * BLOCK : (2 * q + 1) * BLOCK] = delta.astype(jnp.bfloat16)
                deltas[rows, (2 * q + 1) * BLOCK : (2 * q + 2) * BLOCK] = (back * silu).astype(jnp.bfloat16)
        for at in range(0, owned, share):
            other = jnp.bitwise_xor(col, row * (owned // share) + at // share)
            slot = (other % 2) * (devices // 2) + other // 2
            hidden_ref[at : at + share, :] = hidden[pl.ds(pl.multiple_of(slot * share, share), share), :]

    total = jnp.dot(turned_ref[...], deltas[...], preferred_element_type=jnp.float32)
    for r in range(depth // BLOCK):
        rows = slice(r * BLOCK, (r + 1) * BLOCK)
        for q in range(width // BLOCK):
            cols = slice(q * BLOCK, (q + 1) * BLOCK)
            keep = mask_ref[step * (depth // BLOCK) + r, first + q].astype(jnp.float32)
            gate_ref[rows, cols] = total[rows, 2 * q * BLOCK : (2 * q + 1) * BLOCK] * keep
            up_ref[rows, cols] = total[rows, (2 * q + 1) * BLOCK : (2 * q + 2) * BLOCK] * keep


def weight_grads(place, mask, turned, back, coded, previous, shapes, start, width, devices):
    depth, count = turned.shape
    owned = shapes[0].shape[0]
    deep = min(ROWS, depth)
    place_of = lambda m, place, mask: (0, 0)
    first = start // BLOCK
    column = pl.Element(width)
    out = pl.BlockSpec((pl.Element(deep), column), lambda m, place, mask: (m * deep, start))
    return pl.pallas_call(
        functools.partial(weights_kernel, first=first, devices=devices),
        grid_spec=pltpu.PrefetchScalarGridSpec(
            num_scalar_prefetch=2,
            grid=(depth // deep,),
            in_specs=[
                pl.BlockSpec((deep, count), lambda m, place, mask: (m, 0)),
                pl.BlockSpec((pl.Element(back.shape[0]), column), lambda m, place, mask: (0, start)),
            ]
            + [pl.BlockSpec(x.shape, place_of) for x in coded]
            + [pl.BlockSpec(memory_space=pl.ANY)] * len(previous),
            out_specs=[pl.BlockSpec((pl.Element(owned), column), lambda m, place, mask: (0, start)), out, out],
            scratch_shapes=[
                pltpu.VMEM((count, 2 * width), jnp.bfloat16),
                pltpu.VMEM((count, width), jnp.bfloat16),
            ],
        ),
        out_shape=shapes,
        input_output_aliases={4 + len(coded) + i: i for i in range(len(previous))},
        compiler_params=params(),
        cost_estimate=cost(),
        name="weight_grads",
    )(place, mask, turned, back, *coded, *previous)


def tie(value, *others):
    return lax.optimization_barrier((value, *others))[0]


def pick(condition, a, b):
    return lax.select(jnp.broadcast_to(condition, a.shape), a, b)


def gather_tokens(tokens, devices, others):
    pieces = [tokens]
    for other in range(2, devices, 2):
        pieces.append(lax.ppermute(tokens, "col", [(i, i ^ other) for i in range(devices)]))
    mine = tie(jnp.concatenate(pieces, axis=0), *others)
    return jnp.concatenate([mine, lax.ppermute(mine, "col", [(i, i ^ 1) for i in range(devices)])], axis=0)


def on_device(tokens, gate_weight, up_weight, block_mask, hidden_grad, *, ring, devices):
    me = lax.axis_index("row")
    depth, local = gate_weight.shape
    left, right = ring // 2 - 1, ring // 2
    reach = ring // 2 - 1
    short = reach == 1
    distance = jnp.where(me >= right, me - right, left - me)
    shapes = [
        jax.ShapeDtypeStruct(hidden_grad.shape, jnp.bfloat16),
        jax.ShapeDtypeStruct((depth, local), jnp.float32),
        jax.ShapeDtypeStruct((depth, local), jnp.float32),
    ]
    widths = chunk_widths(local)
    starts = [sum(widths[:c]) for c in range(len(widths))]
    chunks = len(widths)

    def outward(value, hop):
        return lax.ppermute(value, "row", [(left - hop, left - hop - 1), (right + hop, right + hop + 1)])

    def inward(value, hop):
        return lax.ppermute(value, "row", [(left - hop - 1, left - hop), (right + hop + 1, right + hop)])

    def swap(value):
        return lax.ppermute(value, "row", [(left, right), (right, left)])

    def exchange(value):
        return lax.ppermute(value, "row", [(i, i ^ 1) for i in range(ring)])

    pair = [exchange(hidden_grad)] if short else []
    gathered = gather_tokens(tokens, devices, pair)
    on_left = me < right
    if short:
        sources = [jnp.where(on_left, i != me, 3 - i) for i in range(2)]
        sources += [jnp.where(on_left, i, i != me) for i in range(2, 4)]
    else:
        sources = list(range(ring))
    inner = (distance == 0) if short else 1
    place = jnp.stack([lax.axis_index("col"), me, inner, *sources]).astype(jnp.int32)
    own, sums, across, arrived, terms = [], [], [], [], []
    outs = ()

    def ordered(kernel, *args):
        nonlocal place
        out = kernel(place, *args)
        place = tie(place, out[0] if isinstance(out, (list, tuple)) else out)
        return out

    def run_forward(c):
        own.append(ordered(forward, block_mask, gathered, gate_weight, up_weight, starts[c], widths[c]))

    def run_weights(c, coded, back):
        nonlocal outs
        outs = ordered(
            weight_grads, block_mask, turned, back, coded, outs, shapes, starts[c], widths[c], devices
        )

    if not short:
        back = lax.all_gather(hidden_grad, "row", axis=0, tiled=True)
        turned = ordered(turn, gathered)
        for c in range(chunks):
            run_forward(c)
            total = own[c]
            for hop in reversed(range(reach)):
                new = ordered(add, own[c], inward(total, hop))
                total = pick(distance == hop, new, total)
            coming = swap(total)
            for hop in range(reach):
                came = outward(ordered(add, own[c], coming), hop)
                coming = pick(distance == hop + 1, came, coming)
            run_weights(c, (total, coming, coming), back)
        return tuple(outs)

    ahead = min(AHEAD, chunks)
    run_forward(0)
    arrived.append(inward(own[0], 0))
    half = jnp.concatenate([hidden_grad, *pair], axis=0)
    other_half = swap(tie(half, place))
    for c in range(1, ahead):
        run_forward(c)
        if c == 1:
            arrived.append(inward(own[1], 0))
    turned = ordered(turn, gathered)
    for s in range(chunks + LAG):
        if s < chunks:
            if s + 2 < min(chunks, LAG):
                arrived.append(inward(tie(own[s + 2], arrived[s]), 0))
            sums.append(ordered(add, own[s], arrived[s]))
            across.append(swap(sums[s]))
        if s == 0:
            moved = outward(tie(other_half, place), 0)
        if s + ahead < chunks:
            run_forward(s + ahead)
        if s == LAG:
            there, moved = lax.optimization_barrier((other_half, moved, place))[:2]
            back = jnp.concatenate([half, pick(distance == 0, there, moved)], axis=0)
        if s >= LAG:
            c = s - LAG
            run_weights(c, (sums[c], across[c], arrived[s]), back)
        c = s - 1
        if 0 <= c < chunks:
            both_ways = c + LAG < chunks
            message = ordered(reply, own[c], across[c], own[c + LAG] if both_ways else own[c])
            arrived.append(exchange(message) if both_ways else outward(message, 0))
    return tuple(outs)


def solution(mesh):
    placed = (P("col", "row"), P("row", "col"), P("row", "col"), P("row", "col"), P("row", "col"))
    return jax.shard_map(
        functools.partial(on_device, ring=mesh.shape["row"], devices=mesh.shape["col"]),
        mesh=mesh,
        in_specs=placed,
        out_specs=(P("row", "col"), P("row", "col"), P("row", "col")),
        check_vma=False,
    )
```

```python
import functools

import jax
import jax.numpy as jnp
from jax import lax
from jax.experimental import pallas as pl
from jax.experimental.pallas import tpu as pltpu
from jax.sharding import PartitionSpec as P

BLOCK = 128
GROUPS = 16
CHUNK = 3
AHEAD = 3
LAG = 3
EARLY, LATE, TURN = 8000, 1, 8000
ROWS = 512
VMEM_LIMIT = 48 * 1024 * 1024


def params():
    return pltpu.CompilerParams(vmem_limit_bytes=VMEM_LIMIT)


def cost(megaflops=1):
    return pl.CostEstimate(flops=megaflops * 10**6, bytes_accessed=megaflops * 2500, transcendentals=0)


def chunk_widths(local):
    units = local // BLOCK
    rest = [CHUNK] * ((units - 1) // CHUNK)
    return [BLOCK * u for u in [units - sum(rest), *rest]]


def put(ref, value):
    rows, cols = value.shape
    grouped = value.reshape(GROUPS, rows // GROUPS, cols)
    top = jnp.max(jnp.abs(grouped), axis=1)
    power = jnp.floor(jnp.log2(jnp.maximum(top, 1e-30))) + 1.0
    codes = jnp.round(grouped * jnp.exp2(15.0 - power)[:, None, :])
    codes = jnp.clip(codes, -32767.0, 32767.0).reshape(rows, cols)
    ref[0:rows, :] = codes.astype(jnp.int32).astype(jnp.int16)
    ref[rows : rows + GROUPS, :] = power.astype(jnp.int32).astype(jnp.int16)


def scales(ref):
    rows = ref.shape[0] - GROUPS
    return jnp.exp2(ref[rows : rows + GROUPS, :].astype(jnp.int32).astype(jnp.float32) - 15.0)


def get(ref):
    rows = ref.shape[0] - GROUPS
    cols = ref.shape[1]
    codes = ref[0:rows, :].astype(jnp.int32).astype(jnp.float32)
    grouped = codes.reshape(GROUPS, rows // GROUPS, cols) * scales(ref)[:, None, :]
    return grouped.reshape(rows, cols)


def forward_kernel(place_ref, mask_ref, low_ref, high_ref, gate_ref, up_ref, out_ref, joined, held, *, first):
    depth = gate_ref.shape[0]
    half = low_ref.shape[0]

    @pl.when(pl.program_id(0) == 0)
    def _():
        joined[0:half, :] = low_ref[...]
        joined[half : 2 * half, :] = high_ref[...]

    for r in range(depth // BLOCK):
        rows = slice(r * BLOCK, (r + 1) * BLOCK)
        keep = mask_ref[r, first + pl.program_id(0)].astype(jnp.float32)
        keep = jnp.full((BLOCK, BLOCK), keep).astype(jnp.bfloat16)
        held[rows, :BLOCK] = gate_ref[rows, :] * keep
        held[rows, BLOCK:] = up_ref[rows, :] * keep
    put(out_ref, jnp.dot(joined[...], held[...], preferred_element_type=jnp.float32))


def forward(place, mask, tokens, gate_weight, up_weight, start, width):
    half, depth = tokens[0].shape
    count = 2 * half
    weight = pl.BlockSpec((depth, BLOCK), lambda j, place, mask: (0, start // BLOCK + j))
    return pl.pallas_call(
        functools.partial(forward_kernel, first=start // BLOCK),
        grid_spec=pltpu.PrefetchScalarGridSpec(
            num_scalar_prefetch=2,
            grid=(width // BLOCK,),
            in_specs=[pl.BlockSpec((half, depth), lambda j, place, mask: (0, 0))] * 2 + [weight] * 2,
            out_specs=pl.BlockSpec((count + GROUPS, 2 * BLOCK), lambda j, place, mask: (0, j)),
            scratch_shapes=[
                pltpu.VMEM((count, depth), jnp.bfloat16),
                pltpu.VMEM((depth, 2 * BLOCK), jnp.bfloat16),
            ],
        ),
        out_shape=jax.ShapeDtypeStruct((count + GROUPS, 2 * width), jnp.int16),
        compiler_params=params(),
        cost_estimate=cost(EARLY if start < 2 * width else LATE),
        name="forward",
    )(place, mask, *tokens, gate_weight, up_weight)


def add_kernel(place_ref, a_ref, b_ref, out_ref):
    inner = place_ref[2] != 0

    @pl.when(inner)
    def _():
        put(out_ref, get(a_ref) + get(b_ref))

    @pl.when(jnp.logical_not(inner))
    def _():
        out_ref[...] = a_ref[...]


def add(place, a, b):
    return pl.pallas_call(
        add_kernel,
        grid_spec=pltpu.PrefetchScalarGridSpec(
            num_scalar_prefetch=1,
            grid=(1,),
            in_specs=[pl.BlockSpec(x.shape, lambda j, place: (0, 0)) for x in (a, b)],
            out_specs=pl.BlockSpec(a.shape, lambda j, place: (0, 0)),
        ),
        out_shape=jax.ShapeDtypeStruct(a.shape, a.dtype),
        compiler_params=params(),
        cost_estimate=cost(),
        name="add",
    )(place, a, b)


def reply_kernel(place_ref, a_ref, b_ref, next_ref, out_ref):
    inner = place_ref[2] != 0

    @pl.when(inner)
    def _():
        put(out_ref.at[:, 0 : a_ref.shape[1]], get(a_ref) + get(b_ref))

    @pl.when(jnp.logical_not(inner))
    def _():
        out_ref[...] = next_ref[...]


def reply(place, a, b, following):
    return pl.pallas_call(
        reply_kernel,
        grid_spec=pltpu.PrefetchScalarGridSpec(
            num_scalar_prefetch=1,
            grid=(1,),
            in_specs=[pl.BlockSpec(x.shape, lambda j, place: (0, 0)) for x in (a, b, following)],
            out_specs=pl.BlockSpec(following.shape, lambda j, place: (0, 0)),
        ),
        out_shape=jax.ShapeDtypeStruct(following.shape, a.dtype),
        compiler_params=params(),
        cost_estimate=cost(),
        name="reply",
    )(place, a, b, following)


def turn_kernel(place_ref, low_ref, high_ref, out_ref):
    half = low_ref.shape[0]
    out_ref[:, 0:half] = low_ref[...].T
    out_ref[:, half : 2 * half] = high_ref[...].T


def turn(place, low, high):
    half, cols = low.shape
    deep = min(512, cols)
    return pl.pallas_call(
        turn_kernel,
        grid_spec=pltpu.PrefetchScalarGridSpec(
            num_scalar_prefetch=1,
            grid=(cols // deep,),
            in_specs=[pl.BlockSpec((half, deep), lambda i, place: (0, i))] * 2,
            out_specs=pl.BlockSpec((deep, 2 * half), lambda i, place: (i, 0)),
        ),
        out_shape=jax.ShapeDtypeStruct((cols, 2 * half), low.dtype),
        compiler_params=params(),
        cost_estimate=cost(TURN),
        name="turn",
    )(place, low, high)


def weights_kernel(place_ref, mask_ref, turned_ref, back_ref, own_ref, across_ref, out_ref, *rest, first, devices):
    hidden_ref, gate_ref, up_ref, deltas, hidden = rest[-5:]
    step = pl.program_id(0)
    depth, width = gate_ref.shape
    count = deltas.shape[0]
    share = count // devices
    col, row, inner = place_ref[0], place_ref[1], place_ref[2] != 0
    owned = hidden_ref.shape[0]

    @pl.when(step == 0)
    def _():
        span = 2 * width
        power = jnp.where(inner, across_ref[count : count + GROUPS, :span], out_ref[count : count + GROUPS, :span])
        scale = jnp.exp2(power.astype(jnp.int32).astype(jnp.float32) - 15.0)
        own_scale = scales(own_ref)
        size = min(share, count // GROUPS)
        for at in range(0, count, size):
            rows = slice(at, at + size)
            group = at // (count // GROUPS)
            slot = at // share
            other = (slot % (devices // 2)) * 2 + slot // (devices // 2)
            token = jnp.bitwise_xor(col, other) * share + at % share
            source = place_ref[3 + token // owned]
            start = pl.multiple_of(source * owned + token % owned, size)
            codes = jnp.where(inner, across_ref[rows, :span], out_ref[rows, :span])
            both = (
                own_ref[rows, :].astype(jnp.int32).astype(jnp.float32) * own_scale[group : group + 1, :]
                + codes.astype(jnp.int32).astype(jnp.float32) * scale[group : group + 1, :]
            )
            for q in range(width // BLOCK):
                cols = slice(q * BLOCK, (q + 1) * BLOCK)
                gate = both[:, 2 * q * BLOCK : (2 * q + 1) * BLOCK]
                up = both[:, (2 * q + 1) * BLOCK : (2 * q + 2) * BLOCK]
                back = back_ref[pl.ds(start, size), cols].astype(jnp.float32)
                sig = jax.nn.sigmoid(gate)
                silu = gate * sig
                hidden[rows, cols] = (silu * up).astype(jnp.bfloat16)
                delta = back * up * sig * (1.0 + gate * (1.0 - sig))
                deltas[rows, 2 * q * BLOCK : (2 * q + 1) * BLOCK] = delta.astype(jnp.bfloat16)
                deltas[rows, (2 * q + 1) * BLOCK : (2 * q + 2) * BLOCK] = (back * silu).astype(jnp.bfloat16)
        for at in range(0, owned, share):
            other = jnp.bitwise_xor(col, row * (owned // share) + at // share)
            slot = (other % 2) * (devices // 2) + other // 2
            hidden_ref[at : at + share, :] = hidden[pl.ds(pl.multiple_of(slot * share, share), share), :]

    total = jnp.dot(turned_ref[...], deltas[...], preferred_element_type=jnp.float32)
    for r in range(depth // BLOCK):
        rows = slice(r * BLOCK, (r + 1) * BLOCK)
        for q in range(width // BLOCK):
            cols = slice(q * BLOCK, (q + 1) * BLOCK)
            keep = mask_ref[step * (depth // BLOCK) + r, first + q].astype(jnp.float32)
            gate_ref[rows, cols] = total[rows, 2 * q * BLOCK : (2 * q + 1) * BLOCK] * keep
            up_ref[rows, cols] = total[rows, (2 * q + 1) * BLOCK : (2 * q + 2) * BLOCK] * keep


def weight_grads(place, mask, turned, back, coded, previous, shapes, start, width, devices):
    depth, count = turned.shape
    owned = shapes[0].shape[0]
    deep = min(ROWS, depth)
    place_of = lambda m, place, mask: (0, 0)
    first = start // BLOCK
    column = pl.Element(width)
    out = pl.BlockSpec((pl.Element(deep), column), lambda m, place, mask: (m * deep, start))
    return pl.pallas_call(
        functools.partial(weights_kernel, first=first, devices=devices),
        grid_spec=pltpu.PrefetchScalarGridSpec(
            num_scalar_prefetch=2,
            grid=(depth // deep,),
            in_specs=[
                pl.BlockSpec((deep, count), lambda m, place, mask: (m, 0)),
                pl.BlockSpec((pl.Element(back.shape[0]), column), lambda m, place, mask: (0, start)),
            ]
            + [pl.BlockSpec(x.shape, place_of) for x in coded]
            + [pl.BlockSpec(memory_space=pl.ANY)] * len(previous),
            out_specs=[pl.BlockSpec((pl.Element(owned), column), lambda m, place, mask: (0, start)), out, out],
            scratch_shapes=[
                pltpu.VMEM((count, 2 * width), jnp.bfloat16),
                pltpu.VMEM((count, width), jnp.bfloat16),
            ],
        ),
        out_shape=shapes,
        input_output_aliases={4 + len(coded) + i: i for i in range(len(previous))},
        compiler_params=params(),
        cost_estimate=cost(),
        name="weight_grads",
    )(place, mask, turned, back, *coded, *previous)


def tie(value, *others):
    return lax.optimization_barrier((value, *others))[0]


def pick(condition, a, b):
    return lax.select(jnp.broadcast_to(condition, a.shape), a, b)


def gather_tokens(tokens, devices, others):
    pieces = [tokens]
    for other in range(2, devices, 2):
        pieces.append(lax.ppermute(tokens, "col", [(i, i ^ other) for i in range(devices)]))
    mine = tie(jnp.concatenate(pieces, axis=0), *others)
    return mine, lax.ppermute(mine, "col", [(i, i ^ 1) for i in range(devices)])


def on_device(tokens, gate_weight, up_weight, block_mask, hidden_grad, *, ring, devices):
    me = lax.axis_index("row")
    depth, local = gate_weight.shape
    left, right = ring // 2 - 1, ring // 2
    reach = ring // 2 - 1
    short = reach == 1
    distance = jnp.where(me >= right, me - right, left - me)
    shapes = [
        jax.ShapeDtypeStruct(hidden_grad.shape, jnp.bfloat16),
        jax.ShapeDtypeStruct((depth, local), jnp.float32),
        jax.ShapeDtypeStruct((depth, local), jnp.float32),
    ]
    widths = chunk_widths(local)
    starts = [sum(widths[:c]) for c in range(len(widths))]
    chunks = len(widths)

    def outward(value, hop):
        return lax.ppermute(value, "row", [(left - hop, left - hop - 1), (right + hop, right + hop + 1)])

    def inward(value, hop):
        return lax.ppermute(value, "row", [(left - hop - 1, left - hop), (right + hop + 1, right + hop)])

    def swap(value):
        return lax.ppermute(value, "row", [(left, right), (right, left)])

    def exchange(value):
        return lax.ppermute(value, "row", [(i, i ^ 1) for i in range(ring)])

    pair = [exchange(hidden_grad)] if short else []
    gathered = gather_tokens(tokens, devices, pair)
    on_left = me < right
    if short:
        sources = [jnp.where(on_left, i != me, 3 - i) for i in range(2)]
        sources += [jnp.where(on_left, i, i != me) for i in range(2, 4)]
    else:
        sources = list(range(ring))
    inner = (distance == 0) if short else 1
    place = jnp.stack([lax.axis_index("col"), me, inner, *sources]).astype(jnp.int32)
    own, sums, across, arrived, terms = [], [], [], [], []
    outs = ()

    def ordered(kernel, *args):
        nonlocal place
        out = kernel(place, *args)
        place = tie(place, out[0] if isinstance(out, (list, tuple)) else out)
        return out

    def run_forward(c):
        own.append(ordered(forward, block_mask, gathered, gate_weight, up_weight, starts[c], widths[c]))

    def run_weights(c, coded, back):
        nonlocal outs
        outs = ordered(
            weight_grads, block_mask, turned, back, coded, outs, shapes, starts[c], widths[c], devices
        )

    if not short:
        back = lax.all_gather(hidden_grad, "row", axis=0, tiled=True)
        turned = ordered(turn, *gathered)
        for c in range(chunks):
            run_forward(c)
            total = own[c]
            for hop in reversed(range(reach)):
                new = ordered(add, own[c], inward(total, hop))
                total = pick(distance == hop, new, total)
            coming = swap(total)
            for hop in range(reach):
                came = outward(ordered(add, own[c], coming), hop)
                coming = pick(distance == hop + 1, came, coming)
            run_weights(c, (total, coming, coming), back)
        return tuple(outs)

    ahead = min(AHEAD, chunks)
    run_forward(0)
    arrived.append(inward(own[0], 0))
    half = jnp.concatenate([hidden_grad, *pair], axis=0)
    other_half = swap(half)
    for c in range(1, ahead):
        run_forward(c)
        if c == 1:
            arrived.append(inward(own[1], 0))
    turned = ordered(turn, *gathered)
    for s in range(chunks + LAG):
        if s < chunks:
            if s == 1:
                place = tie(place, other_half)
            if s == LAG:
                place = tie(place, moved)
            if s + 2 < min(chunks, LAG):
                arrived.append(inward(tie(own[s + 2], arrived[s]), 0))
            sums.append(ordered(add, own[s], arrived[s]))
            across.append(swap(sums[s]))
        if s == 0:
            moved = outward(tie(other_half, place), 0)
        if s == LAG:
            far_half = pick(distance == 0, *lax.optimization_barrier((other_half, moved, place))[:2])
            back = jnp.concatenate([half, far_half], axis=0)
        if s >= LAG:
            c = s - LAG
            run_weights(c, (sums[c], across[c], arrived[s]), back)
        c = s - 1
        if 0 <= c < chunks:
            both_ways = c + LAG < chunks
            message = ordered(reply, own[c], across[c], own[c + LAG] if both_ways else own[c])
            arrived.append(exchange(message) if both_ways else outward(message, 0))
        if s + ahead < chunks:
            run_forward(s + ahead)
    return tuple(outs)


def solution(mesh):
    placed = (P("col", "row"), P("row", "col"), P("row", "col"), P("row", "col"), P("row", "col"))
    return jax.shard_map(
        functools.partial(on_device, ring=mesh.shape["row"], devices=mesh.shape["col"]),
        mesh=mesh,
        in_specs=placed,
        out_specs=(P("row", "col"), P("row", "col"), P("row", "col")),
        check_vma=False,
    )
```

```python
import functools

import jax
import jax.numpy as jnp
from jax import lax
from jax.experimental import pallas as pl
from jax.experimental.pallas import tpu as pltpu
from jax.sharding import PartitionSpec as P

BLOCK = 128
GROUPS = 16
CHUNK = 2
AHEAD = 3
LAG = 3
EARLY, LATE, TURN = 8000, 1, 8000
ROWS = 512
VMEM_LIMIT = 48 * 1024 * 1024


def params():
    return pltpu.CompilerParams(vmem_limit_bytes=VMEM_LIMIT)


def cost(megaflops=1):
    return pl.CostEstimate(flops=megaflops * 10**6, bytes_accessed=megaflops * 2500, transcendentals=0)


def chunk_widths(local):
    units = local // BLOCK
    rest = [CHUNK] * ((units - 1) // CHUNK)
    return [BLOCK * u for u in [units - sum(rest), *rest]]


def put(ref, value):
    rows, cols = value.shape
    grouped = value.reshape(GROUPS, rows // GROUPS, cols)
    top = jnp.max(jnp.abs(grouped), axis=1)
    power = jnp.floor(jnp.log2(jnp.maximum(top, 1e-30))) + 1.0
    codes = jnp.round(grouped * jnp.exp2(15.0 - power)[:, None, :])
    codes = jnp.clip(codes, -32767.0, 32767.0).reshape(rows, cols)
    ref[0:rows, :] = codes.astype(jnp.int32).astype(jnp.int16)
    ref[rows : rows + GROUPS, :] = power.astype(jnp.int32).astype(jnp.int16)


def scales(ref):
    rows = ref.shape[0] - GROUPS
    return jnp.exp2(ref[rows : rows + GROUPS, :].astype(jnp.int32).astype(jnp.float32) - 15.0)


def get(ref):
    rows = ref.shape[0] - GROUPS
    cols = ref.shape[1]
    codes = ref[0:rows, :].astype(jnp.int32).astype(jnp.float32)
    grouped = codes.reshape(GROUPS, rows // GROUPS, cols) * scales(ref)[:, None, :]
    return grouped.reshape(rows, cols)


def forward_kernel(place_ref, mask_ref, low_ref, high_ref, gate_ref, up_ref, out_ref, joined, held, *, first):
    depth = gate_ref.shape[0]
    half = low_ref.shape[0]

    @pl.when(pl.program_id(0) == 0)
    def _():
        joined[0:half, :] = low_ref[...]
        joined[half : 2 * half, :] = high_ref[...]

    for r in range(depth // BLOCK):
        rows = slice(r * BLOCK, (r + 1) * BLOCK)
        keep = mask_ref[r, first + pl.program_id(0)].astype(jnp.float32)
        keep = jnp.full((BLOCK, BLOCK), keep).astype(jnp.bfloat16)
        held[rows, :BLOCK] = gate_ref[rows, :] * keep
        held[rows, BLOCK:] = up_ref[rows, :] * keep
    put(out_ref, jnp.dot(joined[...], held[...], preferred_element_type=jnp.float32))


def forward(place, mask, tokens, gate_weight, up_weight, start, width):
    half, depth = tokens[0].shape
    count = 2 * half
    weight = pl.BlockSpec((depth, BLOCK), lambda j, place, mask: (0, start // BLOCK + j))
    return pl.pallas_call(
        functools.partial(forward_kernel, first=start // BLOCK),
        grid_spec=pltpu.PrefetchScalarGridSpec(
            num_scalar_prefetch=2,
            grid=(width // BLOCK,),
            in_specs=[pl.BlockSpec((half, depth), lambda j, place, mask: (0, 0))] * 2 + [weight] * 2,
            out_specs=pl.BlockSpec((count + GROUPS, 2 * BLOCK), lambda j, place, mask: (0, j)),
            scratch_shapes=[
                pltpu.VMEM((count, depth), jnp.bfloat16),
                pltpu.VMEM((depth, 2 * BLOCK), jnp.bfloat16),
            ],
        ),
        out_shape=jax.ShapeDtypeStruct((count + GROUPS, 2 * width), jnp.int16),
        compiler_params=params(),
        cost_estimate=cost(EARLY if start < 2 * width else LATE),
        name="forward",
    )(place, mask, *tokens, gate_weight, up_weight)


def add_kernel(place_ref, a_ref, b_ref, out_ref):
    inner = place_ref[2] != 0

    @pl.when(inner)
    def _():
        put(out_ref, get(a_ref) + get(b_ref))

    @pl.when(jnp.logical_not(inner))
    def _():
        out_ref[...] = a_ref[...]


def add(place, a, b):
    return pl.pallas_call(
        add_kernel,
        grid_spec=pltpu.PrefetchScalarGridSpec(
            num_scalar_prefetch=1,
            grid=(1,),
            in_specs=[pl.BlockSpec(x.shape, lambda j, place: (0, 0)) for x in (a, b)],
            out_specs=pl.BlockSpec(a.shape, lambda j, place: (0, 0)),
        ),
        out_shape=jax.ShapeDtypeStruct(a.shape, a.dtype),
        compiler_params=params(),
        cost_estimate=cost(),
        name="add",
    )(place, a, b)


def reply_kernel(place_ref, a_ref, b_ref, next_ref, out_ref):
    inner = place_ref[2] != 0

    @pl.when(inner)
    def _():
        put(out_ref.at[:, 0 : a_ref.shape[1]], get(a_ref) + get(b_ref))

    @pl.when(jnp.logical_not(inner))
    def _():
        out_ref[...] = next_ref[...]


def reply(place, a, b, following):
    return pl.pallas_call(
        reply_kernel,
        grid_spec=pltpu.PrefetchScalarGridSpec(
            num_scalar_prefetch=1,
            grid=(1,),
            in_specs=[pl.BlockSpec(x.shape, lambda j, place: (0, 0)) for x in (a, b, following)],
            out_specs=pl.BlockSpec(following.shape, lambda j, place: (0, 0)),
        ),
        out_shape=jax.ShapeDtypeStruct(following.shape, a.dtype),
        compiler_params=params(),
        cost_estimate=cost(),
        name="reply",
    )(place, a, b, following)


def turn_kernel(place_ref, low_ref, high_ref, out_ref):
    half = low_ref.shape[0]
    out_ref[:, 0:half] = low_ref[...].T
    out_ref[:, half : 2 * half] = high_ref[...].T


def turn(place, low, high):
    half, cols = low.shape
    deep = min(512, cols)
    return pl.pallas_call(
        turn_kernel,
        grid_spec=pltpu.PrefetchScalarGridSpec(
            num_scalar_prefetch=1,
            grid=(cols // deep,),
            in_specs=[pl.BlockSpec((half, deep), lambda i, place: (0, i))] * 2,
            out_specs=pl.BlockSpec((deep, 2 * half), lambda i, place: (i, 0)),
        ),
        out_shape=jax.ShapeDtypeStruct((cols, 2 * half), low.dtype),
        compiler_params=params(),
        cost_estimate=cost(TURN),
        name="turn",
    )(place, low, high)


def weights_kernel(place_ref, mask_ref, turned_ref, back_ref, own_ref, across_ref, out_ref, *rest, first, devices):
    hidden_ref, gate_ref, up_ref, deltas, hidden = rest[-5:]
    step = pl.program_id(0)
    depth, width = gate_ref.shape
    count = deltas.shape[0]
    share = count // devices
    col, row, inner = place_ref[0], place_ref[1], place_ref[2] != 0
    owned = hidden_ref.shape[0]

    @pl.when(step == 0)
    def _():
        span = 2 * width
        power = jnp.where(inner, across_ref[count : count + GROUPS, :span], out_ref[count : count + GROUPS, :span])
        scale = jnp.exp2(power.astype(jnp.int32).astype(jnp.float32) - 15.0)
        own_scale = scales(own_ref)
        size = min(share, count // GROUPS)
        for at in range(0, count, size):
            rows = slice(at, at + size)
            group = at // (count // GROUPS)
            slot = at // share
            other = (slot % (devices // 2)) * 2 + slot // (devices // 2)
            token = jnp.bitwise_xor(col, other) * share + at % share
            source = place_ref[3 + token // owned]
            start = pl.multiple_of(source * owned + token % owned, size)
            codes = jnp.where(inner, across_ref[rows, :span], out_ref[rows, :span])
            both = (
                own_ref[rows, :].astype(jnp.int32).astype(jnp.float32) * own_scale[group : group + 1, :]
                + codes.astype(jnp.int32).astype(jnp.float32) * scale[group : group + 1, :]
            )
            for q in range(width // BLOCK):
                cols = slice(q * BLOCK, (q + 1) * BLOCK)
                gate = both[:, 2 * q * BLOCK : (2 * q + 1) * BLOCK]
                up = both[:, (2 * q + 1) * BLOCK : (2 * q + 2) * BLOCK]
                back = back_ref[pl.ds(start, size), cols].astype(jnp.float32)
                sig = jax.nn.sigmoid(gate)
                silu = gate * sig
                hidden[rows, cols] = (silu * up).astype(jnp.bfloat16)
                delta = back * up * sig * (1.0 + gate * (1.0 - sig))
                deltas[rows, 2 * q * BLOCK : (2 * q + 1) * BLOCK] = delta.astype(jnp.bfloat16)
                deltas[rows, (2 * q + 1) * BLOCK : (2 * q + 2) * BLOCK] = (back * silu).astype(jnp.bfloat16)
        for at in range(0, owned, share):
            other = jnp.bitwise_xor(col, row * (owned // share) + at // share)
            slot = (other % 2) * (devices // 2) + other // 2
            hidden_ref[at : at + share, :] = hidden[pl.ds(pl.multiple_of(slot * share, share), share), :]

    total = jnp.dot(turned_ref[...], deltas[...], preferred_element_type=jnp.float32)
    for r in range(depth // BLOCK):
        rows = slice(r * BLOCK, (r + 1) * BLOCK)
        for q in range(width // BLOCK):
            cols = slice(q * BLOCK, (q + 1) * BLOCK)
            keep = mask_ref[step * (depth // BLOCK) + r, first + q].astype(jnp.float32)
            gate_ref[rows, cols] = total[rows, 2 * q * BLOCK : (2 * q + 1) * BLOCK] * keep
            up_ref[rows, cols] = total[rows, (2 * q + 1) * BLOCK : (2 * q + 2) * BLOCK] * keep


def weight_grads(place, mask, turned, back, coded, previous, shapes, start, width, devices):
    depth, count = turned.shape
    owned = shapes[0].shape[0]
    deep = min(ROWS, depth)
    place_of = lambda m, place, mask: (0, 0)
    first = start // BLOCK
    column = pl.Element(width)
    out = pl.BlockSpec((pl.Element(deep), column), lambda m, place, mask: (m * deep, start))
    return pl.pallas_call(
        functools.partial(weights_kernel, first=first, devices=devices),
        grid_spec=pltpu.PrefetchScalarGridSpec(
            num_scalar_prefetch=2,
            grid=(depth // deep,),
            in_specs=[
                pl.BlockSpec((deep, count), lambda m, place, mask: (m, 0)),
                pl.BlockSpec((pl.Element(back.shape[0]), column), lambda m, place, mask: (0, start)),
            ]
            + [pl.BlockSpec(x.shape, place_of) for x in coded]
            + [pl.BlockSpec(memory_space=pl.ANY)] * len(previous),
            out_specs=[pl.BlockSpec((pl.Element(owned), column), lambda m, place, mask: (0, start)), out, out],
            scratch_shapes=[
                pltpu.VMEM((count, 2 * width), jnp.bfloat16),
                pltpu.VMEM((count, width), jnp.bfloat16),
            ],
        ),
        out_shape=shapes,
        input_output_aliases={4 + len(coded) + i: i for i in range(len(previous))},
        compiler_params=params(),
        cost_estimate=cost(),
        name="weight_grads",
    )(place, mask, turned, back, *coded, *previous)


def tie(value, *others):
    return lax.optimization_barrier((value, *others))[0]


def pick(condition, a, b):
    return lax.select(jnp.broadcast_to(condition, a.shape), a, b)


def gather_tokens(tokens, devices, others):
    pieces = [tokens]
    for other in range(2, devices, 2):
        pieces.append(lax.ppermute(tokens, "col", [(i, i ^ other) for i in range(devices)]))
    mine = tie(jnp.concatenate(pieces, axis=0), *others)
    return mine, lax.ppermute(mine, "col", [(i, i ^ 1) for i in range(devices)])


def on_device(tokens, gate_weight, up_weight, block_mask, hidden_grad, *, ring, devices):
    me = lax.axis_index("row")
    depth, local = gate_weight.shape
    left, right = ring // 2 - 1, ring // 2
    reach = ring // 2 - 1
    short = reach == 1
    distance = jnp.where(me >= right, me - right, left - me)
    shapes = [
        jax.ShapeDtypeStruct(hidden_grad.shape, jnp.bfloat16),
        jax.ShapeDtypeStruct((depth, local), jnp.float32),
        jax.ShapeDtypeStruct((depth, local), jnp.float32),
    ]
    widths = chunk_widths(local)
    starts = [sum(widths[:c]) for c in range(len(widths))]
    chunks = len(widths)

    def outward(value, hop):
        return lax.ppermute(value, "row", [(left - hop, left - hop - 1), (right + hop, right + hop + 1)])

    def inward(value, hop):
        return lax.ppermute(value, "row", [(left - hop - 1, left - hop), (right + hop + 1, right + hop)])

    def swap(value):
        return lax.ppermute(value, "row", [(left, right), (right, left)])

    def exchange(value):
        return lax.ppermute(value, "row", [(i, i ^ 1) for i in range(ring)])

    pair = [exchange(hidden_grad)] if short else []
    gathered = gather_tokens(tokens, devices, pair)
    on_left = me < right
    if short:
        sources = [jnp.where(on_left, i != me, 3 - i) for i in range(2)]
        sources += [jnp.where(on_left, i, i != me) for i in range(2, 4)]
    else:
        sources = list(range(ring))
    inner = (distance == 0) if short else 1
    place = jnp.stack([lax.axis_index("col"), me, inner, *sources]).astype(jnp.int32)
    own, sums, across, arrived, terms = [], [], [], [], []
    outs = ()

    def ordered(kernel, *args):
        nonlocal place
        out = kernel(place, *args)
        place = tie(place, out[0] if isinstance(out, (list, tuple)) else out)
        return out

    def run_forward(c):
        own.append(ordered(forward, block_mask, gathered, gate_weight, up_weight, starts[c], widths[c]))

    def run_weights(c, coded, back):
        nonlocal outs
        outs = ordered(
            weight_grads, block_mask, turned, back, coded, outs, shapes, starts[c], widths[c], devices
        )

    if not short:
        back = lax.all_gather(hidden_grad, "row", axis=0, tiled=True)
        turned = ordered(turn, *gathered)
        for c in range(chunks):
            run_forward(c)
            total = own[c]
            for hop in reversed(range(reach)):
                new = ordered(add, own[c], inward(total, hop))
                total = pick(distance == hop, new, total)
            coming = swap(total)
            for hop in range(reach):
                came = outward(ordered(add, own[c], coming), hop)
                coming = pick(distance == hop + 1, came, coming)
            run_weights(c, (total, coming, coming), back)
        return tuple(outs)

    ahead = min(AHEAD, chunks)
    run_forward(0)
    arrived.append(inward(own[0], 0))
    half = jnp.concatenate([tie(hidden_grad, place), *pair], axis=0)
    other_half = swap(half)
    for c in range(1, ahead):
        run_forward(c)
        if c == 1:
            arrived.append(inward(own[1], 0))
    turned = ordered(turn, *gathered)
    for s in range(chunks + LAG):
        if s < chunks:
            if s == 1:
                place = tie(place, other_half)
            if s == LAG:
                place = tie(place, moved)
            if s + 2 < min(chunks, LAG):
                arrived.append(inward(tie(own[s + 2], arrived[s]), 0))
            sums.append(ordered(add, own[s], arrived[s]))
            across.append(swap(sums[s]))
        if s == 0:
            moved = outward(tie(other_half, place), 0)
        def weights_of(s):
            c = s - LAG
            run_weights(c, (sums[c], across[c], arrived[s]), back)

        if s == LAG:
            far_half = pick(distance == 0, *lax.optimization_barrier((other_half, moved, place))[:2])
            back = jnp.concatenate([half, far_half], axis=0)
        if LAG <= s < chunks - 1:
            weights_of(s)
        c = s - 1
        if 0 <= c < chunks:
            both_ways = c + LAG < chunks
            message = ordered(reply, own[c], across[c], own[c + LAG] if both_ways else own[c])
            arrived.append(exchange(message) if both_ways else outward(message, 0))
        if s >= max(LAG, chunks - 1):
            weights_of(s)
        if s + ahead < chunks:
            run_forward(s + ahead)
    return tuple(outs)


def solution(mesh):
    placed = (P("col", "row"), P("row", "col"), P("row", "col"), P("row", "col"), P("row", "col"))
    return jax.shard_map(
        functools.partial(on_device, ring=mesh.shape["row"], devices=mesh.shape["col"]),
        mesh=mesh,
        in_specs=placed,
        out_specs=(P("row", "col"), P("row", "col"), P("row", "col")),
        check_vma=False,
    )
```

```python
import functools

import jax
import jax.numpy as jnp
from jax import lax
from jax.experimental import pallas as pl
from jax.experimental.pallas import tpu as pltpu
from jax.sharding import PartitionSpec as P

BLOCK = 128
GROUPS = 16
CHUNK = 2
AHEAD = 5
LAG = 3
EARLY, LATE, TURN = 8000, 1, 1
ROWS = 512
VMEM_LIMIT = 48 * 1024 * 1024


def params():
    return pltpu.CompilerParams(vmem_limit_bytes=VMEM_LIMIT)


def cost(megaflops=1):
    return pl.CostEstimate(flops=megaflops * 10**6, bytes_accessed=megaflops * 2500, transcendentals=0)


def chunk_widths(local):
    units = local // BLOCK
    rest = [CHUNK] * ((units - 1) // CHUNK)
    return [BLOCK * u for u in [units - sum(rest), *rest]]


def put(ref, value):
    rows, cols = value.shape
    grouped = value.reshape(GROUPS, rows // GROUPS, cols)
    top = jnp.max(jnp.abs(grouped), axis=1)
    power = jnp.floor(jnp.log2(jnp.maximum(top, 1e-30))) + 1.0
    codes = jnp.round(grouped * jnp.exp2(15.0 - power)[:, None, :])
    codes = jnp.clip(codes, -32767.0, 32767.0).reshape(rows, cols)
    ref[0:rows, :] = codes.astype(jnp.int32).astype(jnp.int16)
    ref[rows : rows + GROUPS, :] = power.astype(jnp.int32).astype(jnp.int16)


def scales(ref):
    rows = ref.shape[0] - GROUPS
    return jnp.exp2(ref[rows : rows + GROUPS, :].astype(jnp.int32).astype(jnp.float32) - 15.0)


def get(ref):
    rows = ref.shape[0] - GROUPS
    cols = ref.shape[1]
    codes = ref[0:rows, :].astype(jnp.int32).astype(jnp.float32)
    grouped = codes.reshape(GROUPS, rows // GROUPS, cols) * scales(ref)[:, None, :]
    return grouped.reshape(rows, cols)


def forward_kernel(place_ref, mask_ref, low_ref, high_ref, gate_ref, up_ref, *rest, first, spans):
    *outs, joined, held, coded = rest
    step = pl.program_id(0)
    depth = gate_ref.shape[0]
    half = low_ref.shape[0]

    @pl.when(step == 0)
    def _():
        joined[0:half, :] = low_ref[...]
        joined[half : 2 * half, :] = high_ref[...]

    for r in range(depth // BLOCK):
        rows = slice(r * BLOCK, (r + 1) * BLOCK)
        keep = mask_ref[r, first + step].astype(jnp.float32)
        keep = jnp.full((BLOCK, BLOCK), keep).astype(jnp.bfloat16)
        held[rows, :BLOCK] = gate_ref[rows, :] * keep
        held[rows, BLOCK:] = up_ref[rows, :] * keep
    total = jnp.dot(joined[...], held[...], preferred_element_type=jnp.float32)
    if len(outs) == 1:
        put(outs[0], total)
        return
    put(coded, total)
    for out_ref, (begin, end) in zip(outs, spans):

        @pl.when(jnp.logical_and(step >= begin, step < end))
        def _(out_ref=out_ref):
            out_ref[...] = coded[...]


def forward(place, mask, tokens, gate_weight, up_weight, start, widths):
    half, depth = tokens[0].shape
    count = 2 * half
    ends = [sum(widths[: c + 1]) // BLOCK for c in range(len(widths))]
    spans = list(zip([0, *ends], ends))
    weight = pl.BlockSpec((depth, BLOCK), lambda j, place, mask: (0, start // BLOCK + j))

    def out(begin, end):
        block = (count + GROUPS, 2 * BLOCK)
        return pl.BlockSpec(block, lambda j, place, mask: (0, jnp.clip(j, begin, end - 1) - begin))

    return pl.pallas_call(
        functools.partial(forward_kernel, first=start // BLOCK, spans=spans),
        grid_spec=pltpu.PrefetchScalarGridSpec(
            num_scalar_prefetch=2,
            grid=(ends[-1],),
            in_specs=[pl.BlockSpec((half, depth), lambda j, place, mask: (0, 0))] * 2 + [weight] * 2,
            out_specs=[out(*span) for span in spans],
            scratch_shapes=[
                pltpu.VMEM((count, depth), jnp.bfloat16),
                pltpu.VMEM((depth, 2 * BLOCK), jnp.bfloat16),
                pltpu.VMEM((count + GROUPS, 2 * BLOCK), jnp.int16),
            ],
        ),
        out_shape=[jax.ShapeDtypeStruct((count + GROUPS, 2 * w), jnp.int16) for w in widths],
        compiler_params=params(),
        cost_estimate=cost(EARLY if start < 2 * widths[0] else LATE),
        name="forward",
    )(place, mask, *tokens, gate_weight, up_weight)


def add_kernel(place_ref, a_ref, b_ref, out_ref):
    inner = place_ref[2] != 0

    @pl.when(inner)
    def _():
        put(out_ref, get(a_ref) + get(b_ref))

    @pl.when(jnp.logical_not(inner))
    def _():
        out_ref[...] = a_ref[...]


def add(place, a, b):
    return pl.pallas_call(
        add_kernel,
        grid_spec=pltpu.PrefetchScalarGridSpec(
            num_scalar_prefetch=1,
            grid=(1,),
            in_specs=[pl.BlockSpec(x.shape, lambda j, place: (0, 0)) for x in (a, b)],
            out_specs=pl.BlockSpec(a.shape, lambda j, place: (0, 0)),
        ),
        out_shape=jax.ShapeDtypeStruct(a.shape, a.dtype),
        compiler_params=params(),
        cost_estimate=cost(),
        name="add",
    )(place, a, b)


def reply_kernel(place_ref, a_ref, b_ref, next_ref, out_ref):
    inner = place_ref[2] != 0

    @pl.when(inner)
    def _():
        put(out_ref.at[:, 0 : a_ref.shape[1]], get(a_ref) + get(b_ref))

    @pl.when(jnp.logical_not(inner))
    def _():
        out_ref[...] = next_ref[...]


def reply(place, a, b, following):
    return pl.pallas_call(
        reply_kernel,
        grid_spec=pltpu.PrefetchScalarGridSpec(
            num_scalar_prefetch=1,
            grid=(1,),
            in_specs=[pl.BlockSpec(x.shape, lambda j, place: (0, 0)) for x in (a, b, following)],
            out_specs=pl.BlockSpec(following.shape, lambda j, place: (0, 0)),
        ),
        out_shape=jax.ShapeDtypeStruct(following.shape, a.dtype),
        compiler_params=params(),
        cost_estimate=cost(),
        name="reply",
    )(place, a, b, following)


def turn_kernel(place_ref, low_ref, high_ref, out_ref):
    half = low_ref.shape[0]
    out_ref[:, 0:half] = low_ref[...].T
    out_ref[:, half : 2 * half] = high_ref[...].T


def turn(place, low, high):
    half, cols = low.shape
    deep = min(512, cols)
    return pl.pallas_call(
        turn_kernel,
        grid_spec=pltpu.PrefetchScalarGridSpec(
            num_scalar_prefetch=1,
            grid=(cols // deep,),
            in_specs=[pl.BlockSpec((half, deep), lambda i, place: (0, i))] * 2,
            out_specs=pl.BlockSpec((deep, 2 * half), lambda i, place: (i, 0)),
        ),
        out_shape=jax.ShapeDtypeStruct((cols, 2 * half), low.dtype),
        compiler_params=params(),
        cost_estimate=cost(TURN),
        name="turn",
    )(place, low, high)


def weights_kernel(place_ref, mask_ref, turned_ref, back_ref, own_ref, across_ref, out_ref, *rest, first, devices):
    hidden_ref, gate_ref, up_ref, deltas, hidden = rest[-5:]
    step = pl.program_id(0)
    depth, width = gate_ref.shape
    count = deltas.shape[0]
    share = count // devices
    col, row, inner = place_ref[0], place_ref[1], place_ref[2] != 0
    owned = hidden_ref.shape[0]

    @pl.when(step == 0)
    def _():
        span = 2 * width
        power = jnp.where(inner, across_ref[count : count + GROUPS, :span], out_ref[count : count + GROUPS, :span])
        scale = jnp.exp2(power.astype(jnp.int32).astype(jnp.float32) - 15.0)
        own_scale = scales(own_ref)
        size = min(share, count // GROUPS)
        for at in range(0, count, size):
            rows = slice(at, at + size)
            group = at // (count // GROUPS)
            slot = at // share
            other = (slot % (devices // 2)) * 2 + slot // (devices // 2)
            token = jnp.bitwise_xor(col, other) * share + at % share
            source = place_ref[3 + token // owned]
            start = pl.multiple_of(source * owned + token % owned, size)
            codes = jnp.where(inner, across_ref[rows, :span], out_ref[rows, :span])
            both = (
                own_ref[rows, :].astype(jnp.int32).astype(jnp.float32) * own_scale[group : group + 1, :]
                + codes.astype(jnp.int32).astype(jnp.float32) * scale[group : group + 1, :]
            )
            for q in range(width // BLOCK):
                cols = slice(q * BLOCK, (q + 1) * BLOCK)
                gate = both[:, 2 * q * BLOCK : (2 * q + 1) * BLOCK]
                up = both[:, (2 * q + 1) * BLOCK : (2 * q + 2) * BLOCK]
                back = back_ref[pl.ds(start, size), cols].astype(jnp.float32)
                sig = jax.nn.sigmoid(gate)
                silu = gate * sig
                hidden[rows, cols] = (silu * up).astype(jnp.bfloat16)
                delta = back * up * sig * (1.0 + gate * (1.0 - sig))
                deltas[rows, 2 * q * BLOCK : (2 * q + 1) * BLOCK] = delta.astype(jnp.bfloat16)
                deltas[rows, (2 * q + 1) * BLOCK : (2 * q + 2) * BLOCK] = (back * silu).astype(jnp.bfloat16)
        for at in range(0, owned, share):
            other = jnp.bitwise_xor(col, row * (owned // share) + at // share)
            slot = (other % 2) * (devices // 2) + other // 2
            hidden_ref[at : at + share, :] = hidden[pl.ds(pl.multiple_of(slot * share, share), share), :]

    total = jnp.dot(turned_ref[...], deltas[...], preferred_element_type=jnp.float32)
    for r in range(depth // BLOCK):
        rows = slice(r * BLOCK, (r + 1) * BLOCK)
        for q in range(width // BLOCK):
            cols = slice(q * BLOCK, (q + 1) * BLOCK)
            keep = mask_ref[step * (depth // BLOCK) + r, first + q].astype(jnp.float32)
            gate_ref[rows, cols] = total[rows, 2 * q * BLOCK : (2 * q + 1) * BLOCK] * keep
            up_ref[rows, cols] = total[rows, (2 * q + 1) * BLOCK : (2 * q + 2) * BLOCK] * keep


def weight_grads(place, mask, turned, back, coded, previous, shapes, start, width, devices):
    depth, count = turned.shape
    owned = shapes[0].shape[0]
    deep = min(ROWS, depth)
    place_of = lambda m, place, mask: (0, 0)
    first = start // BLOCK
    column = pl.Element(width)
    out = pl.BlockSpec((pl.Element(deep), column), lambda m, place, mask: (m * deep, start))
    return pl.pallas_call(
        functools.partial(weights_kernel, first=first, devices=devices),
        grid_spec=pltpu.PrefetchScalarGridSpec(
            num_scalar_prefetch=2,
            grid=(depth // deep,),
            in_specs=[
                pl.BlockSpec((deep, count), lambda m, place, mask: (m, 0)),
                pl.BlockSpec((pl.Element(back.shape[0]), column), lambda m, place, mask: (0, start)),
            ]
            + [pl.BlockSpec(x.shape, place_of) for x in coded]
            + [pl.BlockSpec(memory_space=pl.ANY)] * len(previous),
            out_specs=[pl.BlockSpec((pl.Element(owned), column), lambda m, place, mask: (0, start)), out, out],
            scratch_shapes=[
                pltpu.VMEM((count, 2 * width), jnp.bfloat16),
                pltpu.VMEM((count, width), jnp.bfloat16),
            ],
        ),
        out_shape=shapes,
        input_output_aliases={4 + len(coded) + i: i for i in range(len(previous))},
        compiler_params=params(),
        cost_estimate=cost(),
        name="weight_grads",
    )(place, mask, turned, back, *coded, *previous)


def tie(value, *others):
    return lax.optimization_barrier((value, *others))[0]


def pick(condition, a, b):
    return lax.select(jnp.broadcast_to(condition, a.shape), a, b)


def gather_tokens(tokens, devices, others):
    pieces = [tokens]
    for other in range(2, devices, 2):
        pieces.append(lax.ppermute(tokens, "col", [(i, i ^ other) for i in range(devices)]))
    mine = tie(jnp.concatenate(pieces, axis=0), *others)
    return mine, lax.ppermute(mine, "col", [(i, i ^ 1) for i in range(devices)])


def on_device(tokens, gate_weight, up_weight, block_mask, hidden_grad, *, ring, devices):
    me = lax.axis_index("row")
    depth, local = gate_weight.shape
    left, right = ring // 2 - 1, ring // 2
    reach = ring // 2 - 1
    short = reach == 1
    distance = jnp.where(me >= right, me - right, left - me)
    shapes = [
        jax.ShapeDtypeStruct(hidden_grad.shape, jnp.bfloat16),
        jax.ShapeDtypeStruct((depth, local), jnp.float32),
        jax.ShapeDtypeStruct((depth, local), jnp.float32),
    ]
    widths = chunk_widths(local)
    starts = [sum(widths[:c]) for c in range(len(widths))]
    chunks = len(widths)

    def outward(value, hop):
        return lax.ppermute(value, "row", [(left - hop, left - hop - 1), (right + hop, right + hop + 1)])

    def inward(value, hop):
        return lax.ppermute(value, "row", [(left - hop - 1, left - hop), (right + hop + 1, right + hop)])

    def swap(value):
        return lax.ppermute(value, "row", [(left, right), (right, left)])

    def exchange(value):
        return lax.ppermute(value, "row", [(i, i ^ 1) for i in range(ring)])

    near = [exchange(hidden_grad), swap(hidden_grad)] if short else []
    gathered = gather_tokens(tokens, devices, near)
    on_left = me < right
    if short:
        sources = [jnp.where(on_left, i != me, 3 - i) for i in range(2)]
        sources += [jnp.where(on_left, i, i != me) for i in range(2, 4)]
    else:
        sources = list(range(ring))
    inner = (distance == 0) if short else 1
    place = jnp.stack([lax.axis_index("col"), me, inner, *sources]).astype(jnp.int32)
    own, sums, across, arrived, terms = [], [], [], [], []
    outs = ()

    def ordered(kernel, *args):
        nonlocal place
        out = kernel(place, *args)
        place = tie(place, out[0] if isinstance(out, (list, tuple)) else out)
        return out

    def run_forward(c, end):
        own.extend(ordered(forward, block_mask, gathered, gate_weight, up_weight, starts[c], widths[c:end]))

    def run_weights(c, coded, back):
        nonlocal outs
        outs = ordered(
            weight_grads, block_mask, turned, back, coded, outs, shapes, starts[c], widths[c], devices
        )

    if not short:
        back = lax.all_gather(hidden_grad, "row", axis=0, tiled=True)
        turned = ordered(turn, *gathered)
        for c in range(chunks):
            run_forward(c, c + 1)
            total = own[c]
            for hop in reversed(range(reach)):
                new = ordered(add, own[c], inward(total, hop))
                total = pick(distance == hop, new, total)
            coming = swap(total)
            for hop in range(reach):
                came = outward(ordered(add, own[c], coming), hop)
                coming = pick(distance == hop + 1, came, coming)
            run_weights(c, (total, coming, coming), back)
        return tuple(outs)

    ahead = min(AHEAD, chunks)
    far = [near[1], swap(near[0])]
    moved = [outward(near[1], 0)]
    run_forward(0, 1)
    arrived.append(inward(own[0], 0))
    place = tie(place, far[1], moved[0])
    run_forward(1, 2)
    arrived.append(inward(own[1], 0))
    moved.append(outward(tie(far[1], place), 0))
    run_forward(2, ahead)
    turned = ordered(turn, *gathered)
    for s in range(chunks + LAG):
        if s < chunks:
            if s == 0:
                place = tie(place, moved[1])
            if s + 2 < min(chunks, LAG):
                arrived.append(inward(tie(own[s + 2], arrived[s]), 0))
            sums.append(ordered(add, own[s], arrived[s]))
            across.append(swap(sums[s]))
        def weights_of(s):
            c = s - LAG
            run_weights(c, (sums[c], across[c], arrived[s]), back)

        if s == LAG:
            *late, _ = lax.optimization_barrier((*far, *moved, place))
            others = [pick(distance == 0, a, b) for a, b in zip(late[:2], late[2:])]
            back = jnp.concatenate([hidden_grad, near[0], *others], axis=0)
        if LAG <= s < chunks - 1:
            weights_of(s)
        c = s - 1
        if 0 <= c < chunks:
            both_ways = c + LAG < chunks
            message = ordered(reply, own[c], across[c], own[c + LAG] if both_ways else own[c])
            arrived.append(exchange(message) if both_ways else outward(message, 0))
        if s >= max(LAG, chunks - 1):
            weights_of(s)
        if s + ahead < chunks:
            run_forward(s + ahead, s + ahead + 1)
    return tuple(outs)


def solution(mesh):
    placed = (P("col", "row"), P("row", "col"), P("row", "col"), P("row", "col"), P("row", "col"))
    return jax.shard_map(
        functools.partial(on_device, ring=mesh.shape["row"], devices=mesh.shape["col"]),
        mesh=mesh,
        in_specs=placed,
        out_specs=(P("row", "col"), P("row", "col"), P("row", "col")),
        check_vma=False,
    )
```

```python
import functools

import jax
import jax.numpy as jnp
from jax import lax
from jax.experimental import pallas as pl
from jax.experimental.pallas import tpu as pltpu
from jax.sharding import PartitionSpec as P

BLOCK = 128
GROUPS = 16
CHUNK = 2
AHEAD = 5
LAG = 3
EARLY, LATE, TURN = 8000, 1, 8000
ROWS = 512
VMEM_LIMIT = 48 * 1024 * 1024


def params():
    return pltpu.CompilerParams(vmem_limit_bytes=VMEM_LIMIT)


def cost(megaflops=1):
    return pl.CostEstimate(flops=megaflops * 10**6, bytes_accessed=megaflops * 2500, transcendentals=0)


def chunk_widths(local):
    units = local // BLOCK
    rest = [CHUNK] * ((units - 1) // CHUNK)
    return [BLOCK * u for u in [units - sum(rest), *rest]]


def put(ref, value):
    rows, cols = value.shape
    grouped = value.reshape(GROUPS, rows // GROUPS, cols)
    top = jnp.max(jnp.abs(grouped), axis=1)
    power = jnp.floor(jnp.log2(jnp.maximum(top, 1e-30))) + 1.0
    codes = jnp.round(grouped * jnp.exp2(15.0 - power)[:, None, :])
    codes = jnp.clip(codes, -32767.0, 32767.0).reshape(rows, cols)
    ref[0:rows, :] = codes.astype(jnp.int32).astype(jnp.int16)
    ref[rows : rows + GROUPS, :] = power.astype(jnp.int32).astype(jnp.int16)


def scales(ref):
    rows = ref.shape[0] - GROUPS
    return jnp.exp2(ref[rows : rows + GROUPS, :].astype(jnp.int32).astype(jnp.float32) - 15.0)


def get(ref):
    rows = ref.shape[0] - GROUPS
    cols = ref.shape[1]
    codes = ref[0:rows, :].astype(jnp.int32).astype(jnp.float32)
    grouped = codes.reshape(GROUPS, rows // GROUPS, cols) * scales(ref)[:, None, :]
    return grouped.reshape(rows, cols)


def forward_kernel(place_ref, mask_ref, low_ref, high_ref, gate_ref, up_ref, *rest, first, spans):
    *outs, joined, held, coded = rest
    step = pl.program_id(0)
    depth = gate_ref.shape[0]
    half = low_ref.shape[0]

    @pl.when(step == 0)
    def _():
        joined[0:half, :] = low_ref[...]
        joined[half : 2 * half, :] = high_ref[...]

    for r in range(depth // BLOCK):
        rows = slice(r * BLOCK, (r + 1) * BLOCK)
        keep = mask_ref[r, first + step].astype(jnp.float32)
        keep = jnp.full((BLOCK, BLOCK), keep).astype(jnp.bfloat16)
        held[rows, :BLOCK] = gate_ref[rows, :] * keep
        held[rows, BLOCK:] = up_ref[rows, :] * keep
    total = jnp.dot(joined[...], held[...], preferred_element_type=jnp.float32)
    if len(outs) == 1:
        put(outs[0], total)
        return
    put(coded, total)
    for out_ref, (begin, end) in zip(outs, spans):

        @pl.when(jnp.logical_and(step >= begin, step < end))
        def _(out_ref=out_ref):
            out_ref[...] = coded[...]


def forward(place, mask, tokens, gate_weight, up_weight, start, widths):
    half, depth = tokens[0].shape
    count = 2 * half
    ends = [sum(widths[: c + 1]) // BLOCK for c in range(len(widths))]
    spans = list(zip([0, *ends], ends))
    weight = pl.BlockSpec((depth, BLOCK), lambda j, place, mask: (0, start // BLOCK + j))

    def out(begin, end):
        block = (count + GROUPS, 2 * BLOCK)
        return pl.BlockSpec(block, lambda j, place, mask: (0, jnp.clip(j, begin, end - 1) - begin))

    return pl.pallas_call(
        functools.partial(forward_kernel, first=start // BLOCK, spans=spans),
        grid_spec=pltpu.PrefetchScalarGridSpec(
            num_scalar_prefetch=2,
            grid=(ends[-1],),
            in_specs=[pl.BlockSpec((half, depth), lambda j, place, mask: (0, 0))] * 2 + [weight] * 2,
            out_specs=[out(*span) for span in spans],
            scratch_shapes=[
                pltpu.VMEM((count, depth), jnp.bfloat16),
                pltpu.VMEM((depth, 2 * BLOCK), jnp.bfloat16),
                pltpu.VMEM((count + GROUPS, 2 * BLOCK), jnp.int16),
            ],
        ),
        out_shape=[jax.ShapeDtypeStruct((count + GROUPS, 2 * w), jnp.int16) for w in widths],
        compiler_params=params(),
        cost_estimate=cost(EARLY if start < 2 * widths[0] else LATE),
        name="forward",
    )(place, mask, *tokens, gate_weight, up_weight)


def add_kernel(place_ref, a_ref, b_ref, out_ref):
    inner = place_ref[2] != 0

    @pl.when(inner)
    def _():
        put(out_ref, get(a_ref) + get(b_ref))

    @pl.when(jnp.logical_not(inner))
    def _():
        out_ref[...] = a_ref[...]


def add(place, a, b):
    return pl.pallas_call(
        add_kernel,
        grid_spec=pltpu.PrefetchScalarGridSpec(
            num_scalar_prefetch=1,
            grid=(1,),
            in_specs=[pl.BlockSpec(x.shape, lambda j, place: (0, 0)) for x in (a, b)],
            out_specs=pl.BlockSpec(a.shape, lambda j, place: (0, 0)),
        ),
        out_shape=jax.ShapeDtypeStruct(a.shape, a.dtype),
        compiler_params=params(),
        cost_estimate=cost(),
        name="add",
    )(place, a, b)


def reply_kernel(place_ref, a_ref, b_ref, next_ref, out_ref):
    inner = place_ref[2] != 0

    @pl.when(inner)
    def _():
        put(out_ref.at[:, 0 : a_ref.shape[1]], get(a_ref) + get(b_ref))

    @pl.when(jnp.logical_not(inner))
    def _():
        out_ref[...] = next_ref[...]


def reply(place, a, b, following):
    return pl.pallas_call(
        reply_kernel,
        grid_spec=pltpu.PrefetchScalarGridSpec(
            num_scalar_prefetch=1,
            grid=(1,),
            in_specs=[pl.BlockSpec(x.shape, lambda j, place: (0, 0)) for x in (a, b, following)],
            out_specs=pl.BlockSpec(following.shape, lambda j, place: (0, 0)),
        ),
        out_shape=jax.ShapeDtypeStruct(following.shape, a.dtype),
        compiler_params=params(),
        cost_estimate=cost(),
        name="reply",
    )(place, a, b, following)


def turn_kernel(place_ref, low_ref, high_ref, out_ref):
    half = low_ref.shape[0]
    out_ref[:, 0:half] = low_ref[...].T
    out_ref[:, half : 2 * half] = high_ref[...].T


def turn(place, low, high):
    half, cols = low.shape
    deep = min(512, cols)
    return pl.pallas_call(
        turn_kernel,
        grid_spec=pltpu.PrefetchScalarGridSpec(
            num_scalar_prefetch=1,
            grid=(cols // deep,),
            in_specs=[pl.BlockSpec((half, deep), lambda i, place: (0, i))] * 2,
            out_specs=pl.BlockSpec((deep, 2 * half), lambda i, place: (i, 0)),
        ),
        out_shape=jax.ShapeDtypeStruct((cols, 2 * half), low.dtype),
        compiler_params=params(),
        cost_estimate=cost(TURN),
        name="turn",
    )(place, low, high)


def weights_kernel(place_ref, mask_ref, turned_ref, back_ref, own_ref, across_ref, out_ref, *rest, first, devices):
    hidden_ref, gate_ref, up_ref, deltas, hidden = rest[-5:]
    step = pl.program_id(0)
    depth, width = gate_ref.shape
    count = deltas.shape[0]
    share = count // devices
    col, row, inner = place_ref[0], place_ref[1], place_ref[2] != 0
    owned = hidden_ref.shape[0]

    @pl.when(step == 0)
    def _():
        span = 2 * width
        power = jnp.where(inner, across_ref[count : count + GROUPS, :span], out_ref[count : count + GROUPS, :span])
        scale = jnp.exp2(power.astype(jnp.int32).astype(jnp.float32) - 15.0)
        own_scale = scales(own_ref)
        size = min(share, count // GROUPS)
        for at in range(0, count, size):
            rows = slice(at, at + size)
            group = at // (count // GROUPS)
            slot = at // share
            other = (slot % (devices // 2)) * 2 + slot // (devices // 2)
            token = jnp.bitwise_xor(col, other) * share + at % share
            source = place_ref[3 + token // owned]
            start = pl.multiple_of(source * owned + token % owned, size)
            codes = jnp.where(inner, across_ref[rows, :span], out_ref[rows, :span])
            both = (
                own_ref[rows, :].astype(jnp.int32).astype(jnp.float32) * own_scale[group : group + 1, :]
                + codes.astype(jnp.int32).astype(jnp.float32) * scale[group : group + 1, :]
            )
            for q in range(width // BLOCK):
                cols = slice(q * BLOCK, (q + 1) * BLOCK)
                gate = both[:, 2 * q * BLOCK : (2 * q + 1) * BLOCK]
                up = both[:, (2 * q + 1) * BLOCK : (2 * q + 2) * BLOCK]
                back = back_ref[pl.ds(start, size), cols].astype(jnp.float32)
                sig = jax.nn.sigmoid(gate)
                silu = gate * sig
                hidden[rows, cols] = (silu * up).astype(jnp.bfloat16)
                delta = back * up * sig * (1.0 + gate * (1.0 - sig))
                deltas[rows, 2 * q * BLOCK : (2 * q + 1) * BLOCK] = delta.astype(jnp.bfloat16)
                deltas[rows, (2 * q + 1) * BLOCK : (2 * q + 2) * BLOCK] = (back * silu).astype(jnp.bfloat16)
        for at in range(0, owned, share):
            other = jnp.bitwise_xor(col, row * (owned // share) + at // share)
            slot = (other % 2) * (devices // 2) + other // 2
            hidden_ref[at : at + share, :] = hidden[pl.ds(pl.multiple_of(slot * share, share), share), :]

    total = jnp.dot(turned_ref[...], deltas[...], preferred_element_type=jnp.float32)
    for r in range(depth // BLOCK):
        rows = slice(r * BLOCK, (r + 1) * BLOCK)
        for q in range(width // BLOCK):
            cols = slice(q * BLOCK, (q + 1) * BLOCK)
            keep = mask_ref[step * (depth // BLOCK) + r, first + q].astype(jnp.float32)
            gate_ref[rows, cols] = total[rows, 2 * q * BLOCK : (2 * q + 1) * BLOCK] * keep
            up_ref[rows, cols] = total[rows, (2 * q + 1) * BLOCK : (2 * q + 2) * BLOCK] * keep


def weight_grads(place, mask, turned, back, coded, previous, shapes, start, width, devices):
    depth, count = turned.shape
    owned = shapes[0].shape[0]
    deep = min(ROWS, depth)
    place_of = lambda m, place, mask: (0, 0)
    first = start // BLOCK
    column = pl.Element(width)
    out = pl.BlockSpec((pl.Element(deep), column), lambda m, place, mask: (m * deep, start))
    return pl.pallas_call(
        functools.partial(weights_kernel, first=first, devices=devices),
        grid_spec=pltpu.PrefetchScalarGridSpec(
            num_scalar_prefetch=2,
            grid=(depth // deep,),
            in_specs=[
                pl.BlockSpec((deep, count), lambda m, place, mask: (m, 0)),
                pl.BlockSpec((pl.Element(back.shape[0]), column), lambda m, place, mask: (0, start)),
            ]
            + [pl.BlockSpec(x.shape, place_of) for x in coded]
            + [pl.BlockSpec(memory_space=pl.ANY)] * len(previous),
            out_specs=[pl.BlockSpec((pl.Element(owned), column), lambda m, place, mask: (0, start)), out, out],
            scratch_shapes=[
                pltpu.VMEM((count, 2 * width), jnp.bfloat16),
                pltpu.VMEM((count, width), jnp.bfloat16),
            ],
        ),
        out_shape=shapes,
        input_output_aliases={4 + len(coded) + i: i for i in range(len(previous))},
        compiler_params=params(),
        cost_estimate=cost(),
        name="weight_grads",
    )(place, mask, turned, back, *coded, *previous)


def tie(value, *others):
    return lax.optimization_barrier((value, *others))[0]


def pick(condition, a, b):
    return lax.select(jnp.broadcast_to(condition, a.shape), a, b)


def gather_tokens(tokens, devices, others):
    pieces = [tokens]
    for other in range(2, devices, 2):
        pieces.append(lax.ppermute(tokens, "col", [(i, i ^ other) for i in range(devices)]))
    mine = tie(jnp.concatenate(pieces, axis=0), *others)
    return mine, lax.ppermute(mine, "col", [(i, i ^ 1) for i in range(devices)])


def on_device(tokens, gate_weight, up_weight, block_mask, hidden_grad, *, ring, devices):
    me = lax.axis_index("row")
    depth, local = gate_weight.shape
    left, right = ring // 2 - 1, ring // 2
    reach = ring // 2 - 1
    short = reach == 1
    distance = jnp.where(me >= right, me - right, left - me)
    shapes = [
        jax.ShapeDtypeStruct(hidden_grad.shape, jnp.bfloat16),
        jax.ShapeDtypeStruct((depth, local), jnp.float32),
        jax.ShapeDtypeStruct((depth, local), jnp.float32),
    ]
    widths = chunk_widths(local)
    starts = [sum(widths[:c]) for c in range(len(widths))]
    chunks = len(widths)

    def outward(value, hop):
        return lax.ppermute(value, "row", [(left - hop, left - hop - 1), (right + hop, right + hop + 1)])

    def inward(value, hop):
        return lax.ppermute(value, "row", [(left - hop - 1, left - hop), (right + hop + 1, right + hop)])

    def swap(value):
        return lax.ppermute(value, "row", [(left, right), (right, left)])

    def exchange(value):
        return lax.ppermute(value, "row", [(i, i ^ 1) for i in range(ring)])

    near = [exchange(hidden_grad)] if short else []
    gathered = gather_tokens(tokens, devices, near)
    on_left = me < right
    if short:
        sources = [jnp.where(on_left, i != me, 3 - i) for i in range(2)]
        sources += [jnp.where(on_left, i, i != me) for i in range(2, 4)]
    else:
        sources = list(range(ring))
    inner = (distance == 0) if short else 1
    place = jnp.stack([lax.axis_index("col"), me, inner, *sources]).astype(jnp.int32)
    own, sums, across, arrived, terms = [], [], [], [], []
    outs = ()

    def ordered(kernel, *args):
        nonlocal place
        out = kernel(place, *args)
        place = tie(place, out[0] if isinstance(out, (list, tuple)) else out)
        return out

    def run_forward(c, end):
        own.extend(ordered(forward, block_mask, gathered, gate_weight, up_weight, starts[c], widths[c:end]))

    def run_weights(c, coded, back):
        nonlocal outs
        outs = ordered(
            weight_grads, block_mask, turned, back, coded, outs, shapes, starts[c], widths[c], devices
        )

    if not short:
        back = lax.all_gather(hidden_grad, "row", axis=0, tiled=True)
        turned = ordered(turn, *gathered)
        for c in range(chunks):
            run_forward(c, c + 1)
            total = own[c]
            for hop in reversed(range(reach)):
                new = ordered(add, own[c], inward(total, hop))
                total = pick(distance == hop, new, total)
            coming = swap(total)
            for hop in range(reach):
                came = outward(ordered(add, own[c], coming), hop)
                coming = pick(distance == hop + 1, came, coming)
            run_weights(c, (total, coming, coming), back)
        return tuple(outs)

    ahead = min(AHEAD, chunks)
    run_forward(0, 1)
    arrived.append(inward(own[0], 0))
    half = jnp.concatenate([tie(hidden_grad, place), *near], axis=0)
    far_half = swap(half)
    run_forward(1, 2)
    arrived.append(inward(own[1], 0))
    run_forward(2, ahead)
    turned = ordered(turn, *gathered)
    for s in range(chunks + LAG):
        if s < chunks:
            if s == LAG:
                place = tie(place, moved)
            if s + 2 < min(chunks, LAG):
                arrived.append(inward(tie(own[s + 2], arrived[s]), 0))
            sums.append(ordered(add, own[s], arrived[s]))
            across.append(swap(sums[s]))
        def weights_of(s):
            c = s - LAG
            run_weights(c, (sums[c], across[c], arrived[s]), back)

        if s == LAG:
            far_half = pick(distance == 0, *lax.optimization_barrier((far_half, moved, place))[:2])
            back = jnp.concatenate([half, far_half], axis=0)
        if LAG <= s < chunks - 1:
            weights_of(s)
        c = s - 1
        if 0 <= c < chunks:
            both_ways = c + LAG < chunks
            message = ordered(reply, own[c], across[c], own[c + LAG] if both_ways else own[c])
            arrived.append(exchange(message) if both_ways else outward(message, 0))
        if s >= max(LAG, chunks - 1):
            weights_of(s)
        if len(own) < chunks:
            run_forward(len(own), len(own) + 1)
        if s == 0:
            moved = outward(tie(far_half, place), 0)
    return tuple(outs)


def solution(mesh):
    placed = (P("col", "row"), P("row", "col"), P("row", "col"), P("row", "col"), P("row", "col"))
    return jax.shard_map(
        functools.partial(on_device, ring=mesh.shape["row"], devices=mesh.shape["col"]),
        mesh=mesh,
        in_specs=placed,
        out_specs=(P("row", "col"), P("row", "col"), P("row", "col")),
        check_vma=False,
    )
```

```python
import functools

import jax
import jax.numpy as jnp
from jax import lax
from jax.experimental import pallas as pl
from jax.experimental.pallas import tpu as pltpu
from jax.sharding import PartitionSpec as P

BLOCK = 128
GROUPS = 16
CHUNK = 2
AHEAD = 4
LAG = 3
EARLY, LATE, TURN = 8000, 1, 1
ROWS = 512
VMEM_LIMIT = 48 * 1024 * 1024


def params():
    return pltpu.CompilerParams(vmem_limit_bytes=VMEM_LIMIT)


def cost(megaflops=1):
    return pl.CostEstimate(flops=megaflops * 10**6, bytes_accessed=megaflops * 2500, transcendentals=0)


def chunk_widths(local):
    units = local // BLOCK
    rest = [CHUNK] * ((units - 1) // CHUNK)
    return [BLOCK * u for u in [units - sum(rest), *rest]]


def put(ref, value):
    rows, cols = value.shape
    grouped = value.reshape(GROUPS, rows // GROUPS, cols)
    top = jnp.max(jnp.abs(grouped), axis=1)
    power = jnp.floor(jnp.log2(jnp.maximum(top, 1e-30))) + 1.0
    codes = jnp.round(grouped * jnp.exp2(15.0 - power)[:, None, :])
    codes = jnp.clip(codes, -32767.0, 32767.0).reshape(rows, cols)
    ref[0:rows, :] = codes.astype(jnp.int32).astype(jnp.int16)
    ref[rows : rows + GROUPS, :] = power.astype(jnp.int32).astype(jnp.int16)


def scales(ref):
    rows = ref.shape[0] - GROUPS
    return jnp.exp2(ref[rows : rows + GROUPS, :].astype(jnp.int32).astype(jnp.float32) - 15.0)


def get(ref):
    rows = ref.shape[0] - GROUPS
    cols = ref.shape[1]
    codes = ref[0:rows, :].astype(jnp.int32).astype(jnp.float32)
    grouped = codes.reshape(GROUPS, rows // GROUPS, cols) * scales(ref)[:, None, :]
    return grouped.reshape(rows, cols)


def forward_kernel(place_ref, mask_ref, low_ref, high_ref, gate_ref, up_ref, *rest, first, spans):
    *outs, joined, held, coded = rest
    step = pl.program_id(0)
    depth = gate_ref.shape[0]
    half = low_ref.shape[0]

    @pl.when(step == 0)
    def _():
        joined[0:half, :] = low_ref[...]
        joined[half : 2 * half, :] = high_ref[...]

    for r in range(depth // BLOCK):
        rows = slice(r * BLOCK, (r + 1) * BLOCK)
        keep = mask_ref[r, first + step].astype(jnp.float32)
        keep = jnp.full((BLOCK, BLOCK), keep).astype(jnp.bfloat16)
        held[rows, :BLOCK] = gate_ref[rows, :] * keep
        held[rows, BLOCK:] = up_ref[rows, :] * keep
    total = jnp.dot(joined[...], held[...], preferred_element_type=jnp.float32)
    if len(outs) == 1:
        put(outs[0], total)
        return
    put(coded, total)
    for out_ref, (begin, end) in zip(outs, spans):

        @pl.when(jnp.logical_and(step >= begin, step < end))
        def _(out_ref=out_ref):
            out_ref[...] = coded[...]


def forward(place, mask, tokens, gate_weight, up_weight, start, widths):
    half, depth = tokens[0].shape
    count = 2 * half
    ends = [sum(widths[: c + 1]) // BLOCK for c in range(len(widths))]
    spans = list(zip([0, *ends], ends))
    weight = pl.BlockSpec((depth, BLOCK), lambda j, place, mask: (0, start // BLOCK + j))

    def out(begin, end):
        block = (count + GROUPS, 2 * BLOCK)
        return pl.BlockSpec(block, lambda j, place, mask: (0, jnp.clip(j, begin, end - 1) - begin))

    return pl.pallas_call(
        functools.partial(forward_kernel, first=start // BLOCK, spans=spans),
        grid_spec=pltpu.PrefetchScalarGridSpec(
            num_scalar_prefetch=2,
            grid=(ends[-1],),
            in_specs=[pl.BlockSpec((half, depth), lambda j, place, mask: (0, 0))] * 2 + [weight] * 2,
            out_specs=[out(*span) for span in spans],
            scratch_shapes=[
                pltpu.VMEM((count, depth), jnp.bfloat16),
                pltpu.VMEM((depth, 2 * BLOCK), jnp.bfloat16),
                pltpu.VMEM((count + GROUPS, 2 * BLOCK), jnp.int16),
            ],
        ),
        out_shape=[jax.ShapeDtypeStruct((count + GROUPS, 2 * w), jnp.int16) for w in widths],
        compiler_params=params(),
        cost_estimate=cost(EARLY if start < 2 * widths[0] else LATE),
        name="forward",
    )(place, mask, *tokens, gate_weight, up_weight)


def add_kernel(place_ref, a_ref, b_ref, out_ref):
    inner = place_ref[2] != 0

    @pl.when(inner)
    def _():
        put(out_ref, get(a_ref) + get(b_ref))

    @pl.when(jnp.logical_not(inner))
    def _():
        out_ref[...] = a_ref[...]


def add(place, a, b):
    return pl.pallas_call(
        add_kernel,
        grid_spec=pltpu.PrefetchScalarGridSpec(
            num_scalar_prefetch=1,
            grid=(1,),
            in_specs=[pl.BlockSpec(x.shape, lambda j, place: (0, 0)) for x in (a, b)],
            out_specs=pl.BlockSpec(a.shape, lambda j, place: (0, 0)),
        ),
        out_shape=jax.ShapeDtypeStruct(a.shape, a.dtype),
        compiler_params=params(),
        cost_estimate=cost(),
        name="add",
    )(place, a, b)


def reply_kernel(place_ref, a_ref, b_ref, next_ref, out_ref):
    inner = place_ref[2] != 0

    @pl.when(inner)
    def _():
        put(out_ref.at[:, 0 : a_ref.shape[1]], get(a_ref) + get(b_ref))

    @pl.when(jnp.logical_not(inner))
    def _():
        out_ref[...] = next_ref[...]


def reply(place, a, b, following):
    return pl.pallas_call(
        reply_kernel,
        grid_spec=pltpu.PrefetchScalarGridSpec(
            num_scalar_prefetch=1,
            grid=(1,),
            in_specs=[pl.BlockSpec(x.shape, lambda j, place: (0, 0)) for x in (a, b, following)],
            out_specs=pl.BlockSpec(following.shape, lambda j, place: (0, 0)),
        ),
        out_shape=jax.ShapeDtypeStruct(following.shape, a.dtype),
        compiler_params=params(),
        cost_estimate=cost(),
        name="reply",
    )(place, a, b, following)


def turn_kernel(place_ref, low_ref, high_ref, out_ref):
    half = low_ref.shape[0]
    out_ref[:, 0:half] = low_ref[...].T
    out_ref[:, half : 2 * half] = high_ref[...].T


def turn(place, low, high):
    half, cols = low.shape
    deep = min(512, cols)
    return pl.pallas_call(
        turn_kernel,
        grid_spec=pltpu.PrefetchScalarGridSpec(
            num_scalar_prefetch=1,
            grid=(cols // deep,),
            in_specs=[pl.BlockSpec((half, deep), lambda i, place: (0, i))] * 2,
            out_specs=pl.BlockSpec((deep, 2 * half), lambda i, place: (i, 0)),
        ),
        out_shape=jax.ShapeDtypeStruct((cols, 2 * half), low.dtype),
        compiler_params=params(),
        cost_estimate=cost(TURN),
        name="turn",
    )(place, low, high)


def weights_kernel(place_ref, mask_ref, turned_ref, back_ref, own_ref, across_ref, out_ref, *rest, first, devices):
    hidden_ref, gate_ref, up_ref, deltas, hidden = rest[-5:]
    step = pl.program_id(0)
    depth, width = gate_ref.shape
    count = deltas.shape[0]
    share = count // devices
    col, row, inner = place_ref[0], place_ref[1], place_ref[2] != 0
    owned = hidden_ref.shape[0]

    @pl.when(step == 0)
    def _():
        span = 2 * width
        power = jnp.where(inner, across_ref[count : count + GROUPS, :span], out_ref[count : count + GROUPS, :span])
        scale = jnp.exp2(power.astype(jnp.int32).astype(jnp.float32) - 15.0)
        own_scale = scales(own_ref)
        size = min(share, count // GROUPS)
        for at in range(0, count, size):
            rows = slice(at, at + size)
            group = at // (count // GROUPS)
            slot = at // share
            other = (slot % (devices // 2)) * 2 + slot // (devices // 2)
            token = jnp.bitwise_xor(col, other) * share + at % share
            source = place_ref[3 + token // owned]
            start = pl.multiple_of(source * owned + token % owned, size)
            codes = jnp.where(inner, across_ref[rows, :span], out_ref[rows, :span])
            both = (
                own_ref[rows, :].astype(jnp.int32).astype(jnp.float32) * own_scale[group : group + 1, :]
                + codes.astype(jnp.int32).astype(jnp.float32) * scale[group : group + 1, :]
            )
            for q in range(width // BLOCK):
                cols = slice(q * BLOCK, (q + 1) * BLOCK)
                gate = both[:, 2 * q * BLOCK : (2 * q + 1) * BLOCK]
                up = both[:, (2 * q + 1) * BLOCK : (2 * q + 2) * BLOCK]
                back = back_ref[pl.ds(start, size), cols].astype(jnp.float32)
                sig = jax.nn.sigmoid(gate)
                silu = gate * sig
                hidden[rows, cols] = (silu * up).astype(jnp.bfloat16)
                delta = back * up * sig * (1.0 + gate * (1.0 - sig))
                deltas[rows, 2 * q * BLOCK : (2 * q + 1) * BLOCK] = delta.astype(jnp.bfloat16)
                deltas[rows, (2 * q + 1) * BLOCK : (2 * q + 2) * BLOCK] = (back * silu).astype(jnp.bfloat16)
        for at in range(0, owned, share):
            other = jnp.bitwise_xor(col, row * (owned // share) + at // share)
            slot = (other % 2) * (devices // 2) + other // 2
            hidden_ref[at : at + share, :] = hidden[pl.ds(pl.multiple_of(slot * share, share), share), :]

    total = jnp.dot(turned_ref[...], deltas[...], preferred_element_type=jnp.float32)
    for r in range(depth // BLOCK):
        rows = slice(r * BLOCK, (r + 1) * BLOCK)
        for q in range(width // BLOCK):
            cols = slice(q * BLOCK, (q + 1) * BLOCK)
            keep = mask_ref[step * (depth // BLOCK) + r, first + q].astype(jnp.float32)
            gate_ref[rows, cols] = total[rows, 2 * q * BLOCK : (2 * q + 1) * BLOCK] * keep
            up_ref[rows, cols] = total[rows, (2 * q + 1) * BLOCK : (2 * q + 2) * BLOCK] * keep


def weight_grads(place, mask, turned, back, coded, previous, shapes, start, width, devices):
    depth, count = turned.shape
    owned = shapes[0].shape[0]
    deep = min(ROWS, depth)
    place_of = lambda m, place, mask: (0, 0)
    first = start // BLOCK
    column = pl.Element(width)
    out = pl.BlockSpec((pl.Element(deep), column), lambda m, place, mask: (m * deep, start))
    return pl.pallas_call(
        functools.partial(weights_kernel, first=first, devices=devices),
        grid_spec=pltpu.PrefetchScalarGridSpec(
            num_scalar_prefetch=2,
            grid=(depth // deep,),
            in_specs=[
                pl.BlockSpec((deep, count), lambda m, place, mask: (m, 0)),
                pl.BlockSpec((pl.Element(back.shape[0]), column), lambda m, place, mask: (0, start)),
            ]
            + [pl.BlockSpec(x.shape, place_of) for x in coded]
            + [pl.BlockSpec(memory_space=pl.ANY)] * len(previous),
            out_specs=[pl.BlockSpec((pl.Element(owned), column), lambda m, place, mask: (0, start)), out, out],
            scratch_shapes=[
                pltpu.VMEM((count, 2 * width), jnp.bfloat16),
                pltpu.VMEM((count, width), jnp.bfloat16),
            ],
        ),
        out_shape=shapes,
        input_output_aliases={4 + len(coded) + i: i for i in range(len(previous))},
        compiler_params=params(),
        cost_estimate=cost(),
        name="weight_grads",
    )(place, mask, turned, back, *coded, *previous)


def tie(value, *others):
    return lax.optimization_barrier((value, *others))[0]


def pick(condition, a, b):
    return lax.select(jnp.broadcast_to(condition, a.shape), a, b)


def gather_tokens(tokens, devices, others):
    pieces = [tokens]
    for other in range(2, devices, 2):
        pieces.append(lax.ppermute(tokens, "col", [(i, i ^ other) for i in range(devices)]))
    mine = tie(jnp.concatenate(pieces, axis=0), *others)
    return mine, lax.ppermute(mine, "col", [(i, i ^ 1) for i in range(devices)])


def on_device(tokens, gate_weight, up_weight, block_mask, hidden_grad, *, ring, devices):
    me = lax.axis_index("row")
    depth, local = gate_weight.shape
    left, right = ring // 2 - 1, ring // 2
    reach = ring // 2 - 1
    short = reach == 1
    distance = jnp.where(me >= right, me - right, left - me)
    shapes = [
        jax.ShapeDtypeStruct(hidden_grad.shape, jnp.bfloat16),
        jax.ShapeDtypeStruct((depth, local), jnp.float32),
        jax.ShapeDtypeStruct((depth, local), jnp.float32),
    ]
    widths = chunk_widths(local)
    starts = [sum(widths[:c]) for c in range(len(widths))]
    chunks = len(widths)

    def outward(value, hop):
        return lax.ppermute(value, "row", [(left - hop, left - hop - 1), (right + hop, right + hop + 1)])

    def inward(value, hop):
        return lax.ppermute(value, "row", [(left - hop - 1, left - hop), (right + hop + 1, right + hop)])

    def swap(value):
        return lax.ppermute(value, "row", [(left, right), (right, left)])

    def exchange(value):
        return lax.ppermute(value, "row", [(i, i ^ 1) for i in range(ring)])

    near = [exchange(hidden_grad)] if short else []
    gathered = gather_tokens(tokens, devices, near)
    on_left = me < right
    if short:
        sources = [jnp.where(on_left, i != me, 3 - i) for i in range(2)]
        sources += [jnp.where(on_left, i, i != me) for i in range(2, 4)]
    else:
        sources = list(range(ring))
    inner = (distance == 0) if short else 1
    place = jnp.stack([lax.axis_index("col"), me, inner, *sources]).astype(jnp.int32)
    own, sums, across, arrived, terms = [], [], [], [], []
    outs = ()

    def ordered(kernel, *args):
        nonlocal place
        out = kernel(place, *args)
        place = tie(place, out[0] if isinstance(out, (list, tuple)) else out)
        return out

    def run_forward(c, end):
        own.extend(ordered(forward, block_mask, gathered, gate_weight, up_weight, starts[c], widths[c:end]))

    def run_weights(c, coded, back):
        nonlocal outs
        outs = ordered(
            weight_grads, block_mask, turned, back, coded, outs, shapes, starts[c], widths[c], devices
        )

    if not short:
        back = lax.all_gather(hidden_grad, "row", axis=0, tiled=True)
        turned = ordered(turn, *gathered)
        for c in range(chunks):
            run_forward(c, c + 1)
            total = own[c]
            for hop in reversed(range(reach)):
                new = ordered(add, own[c], inward(total, hop))
                total = pick(distance == hop, new, total)
            coming = swap(total)
            for hop in range(reach):
                came = outward(ordered(add, own[c], coming), hop)
                coming = pick(distance == hop + 1, came, coming)
            run_weights(c, (total, coming, coming), back)
        return tuple(outs)

    ahead = min(AHEAD, chunks)
    run_forward(0, 1)
    arrived.append(inward(own[0], 0))
    far = [swap(hidden_grad), swap(tie(near[0], place))]
    run_forward(1, 2)
    arrived.append(inward(own[1], 0))
    moved = [outward(tie(far[0], place), 0)]
    run_forward(2, ahead)
    turned = ordered(turn, *gathered)
    for s in range(chunks + LAG):
        if s < chunks:
            if s == 0:
                place = tie(place, far[1], moved[0])
            if s + 2 < min(chunks, LAG):
                arrived.append(inward(tie(own[s + 2], arrived[s]), 0))
            sums.append(ordered(add, own[s], arrived[s]))
            across.append(swap(sums[s]))
        if s == 0:
            moved.append(outward(tie(far[1], place), 0))
        def weights_of(s):
            c = s - LAG
            run_weights(c, (sums[c], across[c], arrived[s]), back)

        if s == LAG:
            *late, _ = lax.optimization_barrier((*far, *moved, place))
            others = [pick(distance == 0, a, b) for a, b in zip(late[:2], late[2:])]
            back = jnp.concatenate([hidden_grad, near[0], *others], axis=0)
        if LAG <= s < chunks - 1:
            weights_of(s)
        c = s - 1
        if 0 <= c < chunks:
            if c == 0:
                place = tie(place, moved[1])
            both_ways = c + LAG < chunks
            message = ordered(reply, own[c], across[c], own[c + LAG] if both_ways else own[c])
            arrived.append(exchange(message) if both_ways else outward(message, 0))
        if s >= max(LAG, chunks - 1):
            weights_of(s)
        if len(own) < chunks:
            run_forward(len(own), len(own) + 1)
    return tuple(outs)


def solution(mesh):
    placed = (P("col", "row"), P("row", "col"), P("row", "col"), P("row", "col"), P("row", "col"))
    return jax.shard_map(
        functools.partial(on_device, ring=mesh.shape["row"], devices=mesh.shape["col"]),
        mesh=mesh,
        in_specs=placed,
        out_specs=(P("row", "col"), P("row", "col"), P("row", "col")),
        check_vma=False,
    )
```

```python
import functools

import jax
import jax.numpy as jnp
from jax import lax
from jax.experimental import pallas as pl
from jax.experimental.pallas import tpu as pltpu
from jax.sharding import PartitionSpec as P

BLOCK = 128
GROUPS = 16
CHUNK = 2
AHEAD = 5
LAG = 3
EARLY, LATE, TURN = 8000, 1, 1
ROWS = 512
VMEM_LIMIT = 48 * 1024 * 1024


def params():
    return pltpu.CompilerParams(vmem_limit_bytes=VMEM_LIMIT)


def cost(megaflops=1):
    return pl.CostEstimate(flops=megaflops * 10**6, bytes_accessed=megaflops * 2500, transcendentals=0)


def chunk_widths(local):
    units = local // BLOCK
    rest = [CHUNK] * ((units - 1) // CHUNK)
    return [BLOCK * u for u in [units - sum(rest), *rest]]


def put(ref, value):
    rows, cols = value.shape
    grouped = value.reshape(GROUPS, rows // GROUPS, cols)
    top = jnp.max(jnp.abs(grouped), axis=1)
    power = jnp.floor(jnp.log2(jnp.maximum(top, 1e-30))) + 1.0
    codes = jnp.round(grouped * jnp.exp2(15.0 - power)[:, None, :])
    codes = jnp.clip(codes, -32767.0, 32767.0).reshape(rows, cols)
    ref[0:rows, :] = codes.astype(jnp.int32).astype(jnp.int16)
    ref[rows : rows + GROUPS, :] = power.astype(jnp.int32).astype(jnp.int16)


def scales(ref):
    rows = ref.shape[0] - GROUPS
    return jnp.exp2(ref[rows : rows + GROUPS, :].astype(jnp.int32).astype(jnp.float32) - 15.0)


def get(ref):
    rows = ref.shape[0] - GROUPS
    cols = ref.shape[1]
    codes = ref[0:rows, :].astype(jnp.int32).astype(jnp.float32)
    grouped = codes.reshape(GROUPS, rows // GROUPS, cols) * scales(ref)[:, None, :]
    return grouped.reshape(rows, cols)


def forward_kernel(place_ref, mask_ref, low_ref, high_ref, gate_ref, up_ref, *rest, first, spans):
    *outs, joined, held, coded = rest
    step = pl.program_id(0)
    depth = gate_ref.shape[0]
    half = low_ref.shape[0]

    @pl.when(step == 0)
    def _():
        joined[0:half, :] = low_ref[...]
        joined[half : 2 * half, :] = high_ref[...]

    for r in range(depth // BLOCK):
        rows = slice(r * BLOCK, (r + 1) * BLOCK)
        keep = mask_ref[r, first + step].astype(jnp.float32)
        keep = jnp.full((BLOCK, BLOCK), keep).astype(jnp.bfloat16)
        held[rows, :BLOCK] = gate_ref[rows, :] * keep
        held[rows, BLOCK:] = up_ref[rows, :] * keep
    total = jnp.dot(joined[...], held[...], preferred_element_type=jnp.float32)
    if len(outs) == 1:
        put(outs[0], total)
        return
    put(coded, total)
    for out_ref, (begin, end) in zip(outs, spans):

        @pl.when(jnp.logical_and(step >= begin, step < end))
        def _(out_ref=out_ref):
            out_ref[...] = coded[...]


def forward(place, mask, tokens, gate_weight, up_weight, start, widths):
    half, depth = tokens[0].shape
    count = 2 * half
    ends = [sum(widths[: c + 1]) // BLOCK for c in range(len(widths))]
    spans = list(zip([0, *ends], ends))
    weight = pl.BlockSpec((depth, BLOCK), lambda j, place, mask: (0, start // BLOCK + j))

    def out(begin, end):
        block = (count + GROUPS, 2 * BLOCK)
        return pl.BlockSpec(block, lambda j, place, mask: (0, jnp.clip(j, begin, end - 1) - begin))

    return pl.pallas_call(
        functools.partial(forward_kernel, first=start // BLOCK, spans=spans),
        grid_spec=pltpu.PrefetchScalarGridSpec(
            num_scalar_prefetch=2,
            grid=(ends[-1],),
            in_specs=[pl.BlockSpec((half, depth), lambda j, place, mask: (0, 0))] * 2 + [weight] * 2,
            out_specs=[out(*span) for span in spans],
            scratch_shapes=[
                pltpu.VMEM((count, depth), jnp.bfloat16),
                pltpu.VMEM((depth, 2 * BLOCK), jnp.bfloat16),
                pltpu.VMEM((count + GROUPS, 2 * BLOCK), jnp.int16),
            ],
        ),
        out_shape=[jax.ShapeDtypeStruct((count + GROUPS, 2 * w), jnp.int16) for w in widths],
        compiler_params=params(),
        cost_estimate=cost(EARLY if start < 2 * widths[0] else LATE),
        name="forward",
    )(place, mask, *tokens, gate_weight, up_weight)


def add_kernel(place_ref, a_ref, b_ref, out_ref):
    inner = place_ref[2] != 0

    @pl.when(inner)
    def _():
        put(out_ref, get(a_ref) + get(b_ref))

    @pl.when(jnp.logical_not(inner))
    def _():
        out_ref[...] = a_ref[...]


def add(place, a, b):
    return pl.pallas_call(
        add_kernel,
        grid_spec=pltpu.PrefetchScalarGridSpec(
            num_scalar_prefetch=1,
            grid=(1,),
            in_specs=[pl.BlockSpec(x.shape, lambda j, place: (0, 0)) for x in (a, b)],
            out_specs=pl.BlockSpec(a.shape, lambda j, place: (0, 0)),
        ),
        out_shape=jax.ShapeDtypeStruct(a.shape, a.dtype),
        compiler_params=params(),
        cost_estimate=cost(),
        name="add",
    )(place, a, b)


def reply_kernel(place_ref, a_ref, b_ref, next_ref, out_ref):
    inner = place_ref[2] != 0

    @pl.when(inner)
    def _():
        put(out_ref.at[:, 0 : a_ref.shape[1]], get(a_ref) + get(b_ref))

    @pl.when(jnp.logical_not(inner))
    def _():
        out_ref[...] = next_ref[...]


def reply(place, a, b, following):
    return pl.pallas_call(
        reply_kernel,
        grid_spec=pltpu.PrefetchScalarGridSpec(
            num_scalar_prefetch=1,
            grid=(1,),
            in_specs=[pl.BlockSpec(x.shape, lambda j, place: (0, 0)) for x in (a, b, following)],
            out_specs=pl.BlockSpec(following.shape, lambda j, place: (0, 0)),
        ),
        out_shape=jax.ShapeDtypeStruct(following.shape, a.dtype),
        compiler_params=params(),
        cost_estimate=cost(),
        name="reply",
    )(place, a, b, following)


def turn_kernel(place_ref, low_ref, high_ref, out_ref):
    half = low_ref.shape[0]
    out_ref[:, 0:half] = low_ref[...].T
    out_ref[:, half : 2 * half] = high_ref[...].T


def turn(place, low, high):
    half, cols = low.shape
    deep = min(512, cols)
    return pl.pallas_call(
        turn_kernel,
        grid_spec=pltpu.PrefetchScalarGridSpec(
            num_scalar_prefetch=1,
            grid=(cols // deep,),
            in_specs=[pl.BlockSpec((half, deep), lambda i, place: (0, i))] * 2,
            out_specs=pl.BlockSpec((deep, 2 * half), lambda i, place: (i, 0)),
        ),
        out_shape=jax.ShapeDtypeStruct((cols, 2 * half), low.dtype),
        compiler_params=params(),
        cost_estimate=cost(TURN),
        name="turn",
    )(place, low, high)


def weights_kernel(place_ref, mask_ref, turned_ref, back_ref, own_ref, across_ref, out_ref, *rest, first, devices):
    hidden_ref, gate_ref, up_ref, deltas, hidden = rest[-5:]
    step = pl.program_id(0)
    depth, width = gate_ref.shape
    count = deltas.shape[0]
    share = count // devices
    col, row, inner = place_ref[0], place_ref[1], place_ref[2] != 0
    owned = hidden_ref.shape[0]

    @pl.when(step == 0)
    def _():
        span = 2 * width
        power = jnp.where(inner, across_ref[count : count + GROUPS, :span], out_ref[count : count + GROUPS, :span])
        scale = jnp.exp2(power.astype(jnp.int32).astype(jnp.float32) - 15.0)
        own_scale = scales(own_ref)
        size = min(share, count // GROUPS)
        for at in range(0, count, size):
            rows = slice(at, at + size)
            group = at // (count // GROUPS)
            slot = at // share
            other = (slot % (devices // 2)) * 2 + slot // (devices // 2)
            token = jnp.bitwise_xor(col, other) * share + at % share
            source = place_ref[3 + token // owned]
            start = pl.multiple_of(source * owned + token % owned, size)
            codes = jnp.where(inner, across_ref[rows, :span], out_ref[rows, :span])
            both = (
                own_ref[rows, :].astype(jnp.int32).astype(jnp.float32) * own_scale[group : group + 1, :]
                + codes.astype(jnp.int32).astype(jnp.float32) * scale[group : group + 1, :]
            )
            for q in range(width // BLOCK):
                cols = slice(q * BLOCK, (q + 1) * BLOCK)
                gate = both[:, 2 * q * BLOCK : (2 * q + 1) * BLOCK]
                up = both[:, (2 * q + 1) * BLOCK : (2 * q + 2) * BLOCK]
                back = back_ref[pl.ds(start, size), cols].astype(jnp.float32)
                sig = jax.nn.sigmoid(gate)
                silu = gate * sig
                hidden[rows, cols] = (silu * up).astype(jnp.bfloat16)
                delta = back * up * sig * (1.0 + gate * (1.0 - sig))
                deltas[rows, 2 * q * BLOCK : (2 * q + 1) * BLOCK] = delta.astype(jnp.bfloat16)
                deltas[rows, (2 * q + 1) * BLOCK : (2 * q + 2) * BLOCK] = (back * silu).astype(jnp.bfloat16)
        for at in range(0, owned, share):
            other = jnp.bitwise_xor(col, row * (owned // share) + at // share)
            slot = (other % 2) * (devices // 2) + other // 2
            hidden_ref[at : at + share, :] = hidden[pl.ds(pl.multiple_of(slot * share, share), share), :]

    total = jnp.dot(turned_ref[...], deltas[...], preferred_element_type=jnp.float32)
    for r in range(depth // BLOCK):
        rows = slice(r * BLOCK, (r + 1) * BLOCK)
        for q in range(width // BLOCK):
            cols = slice(q * BLOCK, (q + 1) * BLOCK)
            keep = mask_ref[step * (depth // BLOCK) + r, first + q].astype(jnp.float32)
            gate_ref[rows, cols] = total[rows, 2 * q * BLOCK : (2 * q + 1) * BLOCK] * keep
            up_ref[rows, cols] = total[rows, (2 * q + 1) * BLOCK : (2 * q + 2) * BLOCK] * keep


def weight_grads(place, mask, turned, back, coded, previous, shapes, start, width, devices):
    depth, count = turned.shape
    owned = shapes[0].shape[0]
    deep = min(ROWS, depth)
    place_of = lambda m, place, mask: (0, 0)
    first = start // BLOCK
    column = pl.Element(width)
    out = pl.BlockSpec((pl.Element(deep), column), lambda m, place, mask: (m * deep, start))
    return pl.pallas_call(
        functools.partial(weights_kernel, first=first, devices=devices),
        grid_spec=pltpu.PrefetchScalarGridSpec(
            num_scalar_prefetch=2,
            grid=(depth // deep,),
            in_specs=[
                pl.BlockSpec((deep, count), lambda m, place, mask: (m, 0)),
                pl.BlockSpec((pl.Element(back.shape[0]), column), lambda m, place, mask: (0, start)),
            ]
            + [pl.BlockSpec(x.shape, place_of) for x in coded]
            + [pl.BlockSpec(memory_space=pl.ANY)] * len(previous),
            out_specs=[pl.BlockSpec((pl.Element(owned), column), lambda m, place, mask: (0, start)), out, out],
            scratch_shapes=[
                pltpu.VMEM((count, 2 * width), jnp.bfloat16),
                pltpu.VMEM((count, width), jnp.bfloat16),
            ],
        ),
        out_shape=shapes,
        input_output_aliases={4 + len(coded) + i: i for i in range(len(previous))},
        compiler_params=params(),
        cost_estimate=cost(),
        name="weight_grads",
    )(place, mask, turned, back, *coded, *previous)


def tie(value, *others):
    return lax.optimization_barrier((value, *others))[0]


def pick(condition, a, b):
    return lax.select(jnp.broadcast_to(condition, a.shape), a, b)


def gather_tokens(tokens, devices, others):
    pieces = [tokens]
    for other in range(2, devices, 2):
        pieces.append(lax.ppermute(tokens, "col", [(i, i ^ other) for i in range(devices)]))
    mine = tie(jnp.concatenate(pieces, axis=0), *others)
    return mine, lax.ppermute(mine, "col", [(i, i ^ 1) for i in range(devices)])


def on_device(tokens, gate_weight, up_weight, block_mask, hidden_grad, *, ring, devices):
    me = lax.axis_index("row")
    depth, local = gate_weight.shape
    left, right = ring // 2 - 1, ring // 2
    reach = ring // 2 - 1
    short = reach == 1
    distance = jnp.where(me >= right, me - right, left - me)
    shapes = [
        jax.ShapeDtypeStruct(hidden_grad.shape, jnp.bfloat16),
        jax.ShapeDtypeStruct((depth, local), jnp.float32),
        jax.ShapeDtypeStruct((depth, local), jnp.float32),
    ]
    widths = chunk_widths(local)
    starts = [sum(widths[:c]) for c in range(len(widths))]
    chunks = len(widths)

    def outward(value, hop):
        return lax.ppermute(value, "row", [(left - hop, left - hop - 1), (right + hop, right + hop + 1)])

    def inward(value, hop):
        return lax.ppermute(value, "row", [(left - hop - 1, left - hop), (right + hop + 1, right + hop)])

    def swap(value):
        return lax.ppermute(value, "row", [(left, right), (right, left)])

    def exchange(value):
        return lax.ppermute(value, "row", [(i, i ^ 1) for i in range(ring)])

    near = [exchange(hidden_grad)] if short else []
    gathered = gather_tokens(tokens, devices, near)
    on_left = me < right
    if short:
        sources = [jnp.where(on_left, i != me, 3 - i) for i in range(2)]
        sources += [jnp.where(on_left, i, i != me) for i in range(2, 4)]
    else:
        sources = list(range(ring))
    inner = (distance == 0) if short else 1
    place = jnp.stack([lax.axis_index("col"), me, inner, *sources]).astype(jnp.int32)
    own, sums, across, arrived, terms = [], [], [], [], []
    outs = ()

    def ordered(kernel, *args):
        nonlocal place
        out = kernel(place, *args)
        place = tie(place, out[0] if isinstance(out, (list, tuple)) else out)
        return out

    def run_forward(c, end):
        own.extend(ordered(forward, block_mask, gathered, gate_weight, up_weight, starts[c], widths[c:end]))

    def run_weights(c, coded, back):
        nonlocal outs
        outs = ordered(
            weight_grads, block_mask, turned, back, coded, outs, shapes, starts[c], widths[c], devices
        )

    if not short:
        back = lax.all_gather(hidden_grad, "row", axis=0, tiled=True)
        turned = ordered(turn, *gathered)
        for c in range(chunks):
            run_forward(c, c + 1)
            total = own[c]
            for hop in reversed(range(reach)):
                new = ordered(add, own[c], inward(total, hop))
                total = pick(distance == hop, new, total)
            coming = swap(total)
            for hop in range(reach):
                came = outward(ordered(add, own[c], coming), hop)
                coming = pick(distance == hop + 1, came, coming)
            run_weights(c, (total, coming, coming), back)
        return tuple(outs)

    ahead = min(AHEAD, chunks)
    run_forward(0, 1)
    arrived.append(inward(own[0], 0))
    far = [swap(hidden_grad), swap(tie(near[0], place))]
    run_forward(1, 2)
    arrived.append(inward(own[1], 0))
    moved = [outward(tie(far[0], place), 0)]
    run_forward(2, ahead)
    turned = ordered(turn, *gathered)
    for s in range(chunks + LAG):
        if s < chunks:
            if s == 0:
                place = tie(place, far[1], moved[0])
            if s + 2 < min(chunks, LAG):
                arrived.append(inward(tie(own[s + 2], arrived[s]), 0))
            sums.append(ordered(add, own[s], arrived[s]))
            across.append(swap(sums[s]))
        if s == 0:
            moved.append(outward(tie(far[1], place), 0))
        def weights_of(s):
            c = s - LAG
            run_weights(c, (sums[c], across[c], arrived[s]), back)

        if s == LAG:
            *late, _ = lax.optimization_barrier((*far, *moved, place))
            others = [pick(distance == 0, a, b) for a, b in zip(late[:2], late[2:])]
            back = jnp.concatenate([hidden_grad, near[0], *others], axis=0)
        if LAG <= s < chunks - 1:
            weights_of(s)
        c = s - 1
        if 0 <= c < chunks:
            if c == 0:
                place = tie(place, moved[1])
            both_ways = c + LAG < chunks
            message = ordered(reply, own[c], across[c], own[c + LAG] if both_ways else own[c])
            arrived.append(exchange(message) if both_ways else outward(message, 0))
        if s >= max(LAG, chunks - 1):
            weights_of(s)
        if len(own) < chunks:
            run_forward(len(own), len(own) + 1)
    return tuple(outs)


def solution(mesh):
    placed = (P("col", "row"), P("row", "col"), P("row", "col"), P("row", "col"), P("row", "col"))
    return jax.shard_map(
        functools.partial(on_device, ring=mesh.shape["row"], devices=mesh.shape["col"]),
        mesh=mesh,
        in_specs=placed,
        out_specs=(P("row", "col"), P("row", "col"), P("row", "col")),
        check_vma=False,
    )
```

```python
import functools

import jax
import jax.numpy as jnp
from jax import lax
from jax.experimental import pallas as pl
from jax.experimental.pallas import tpu as pltpu
from jax.sharding import PartitionSpec as P

BLOCK = 128
GROUPS = 16
CHUNK = 2
AHEAD = 4
LAG = 3
EARLY, LATE, TURN = 8000, 1, 1
ROWS = 512
VMEM_LIMIT = 48 * 1024 * 1024


def params():
    return pltpu.CompilerParams(vmem_limit_bytes=VMEM_LIMIT)


def cost(megaflops=1):
    return pl.CostEstimate(flops=megaflops * 10**6, bytes_accessed=megaflops * 2500, transcendentals=0)


def chunk_widths(local):
    units = local // BLOCK
    rest = [CHUNK] * ((units - 1) // CHUNK)
    return [BLOCK * u for u in [units - sum(rest), *rest]]


def put(ref, value):
    rows, cols = value.shape
    grouped = value.reshape(GROUPS, rows // GROUPS, cols)
    top = jnp.max(jnp.abs(grouped), axis=1)
    power = jnp.floor(jnp.log2(jnp.maximum(top, 1e-30))) + 1.0
    codes = jnp.round(grouped * jnp.exp2(15.0 - power)[:, None, :])
    codes = jnp.clip(codes, -32767.0, 32767.0).reshape(rows, cols)
    ref[0:rows, :] = codes.astype(jnp.int32).astype(jnp.int16)
    ref[rows : rows + GROUPS, :] = power.astype(jnp.int32).astype(jnp.int16)


def scales(ref):
    rows = ref.shape[0] - GROUPS
    return jnp.exp2(ref[rows : rows + GROUPS, :].astype(jnp.int32).astype(jnp.float32) - 15.0)


def get(ref):
    rows = ref.shape[0] - GROUPS
    cols = ref.shape[1]
    codes = ref[0:rows, :].astype(jnp.int32).astype(jnp.float32)
    grouped = codes.reshape(GROUPS, rows // GROUPS, cols) * scales(ref)[:, None, :]
    return grouped.reshape(rows, cols)


def forward_kernel(place_ref, mask_ref, low_ref, high_ref, gate_ref, up_ref, *rest, first, spans):
    *outs, joined, held, coded = rest
    step = pl.program_id(0)
    depth = gate_ref.shape[0]
    half = low_ref.shape[0]

    @pl.when(step == 0)
    def _():
        joined[0:half, :] = low_ref[...]
        joined[half : 2 * half, :] = high_ref[...]

    for r in range(depth // BLOCK):
        rows = slice(r * BLOCK, (r + 1) * BLOCK)
        keep = mask_ref[r, first + step].astype(jnp.float32)
        keep = jnp.full((BLOCK, BLOCK), keep).astype(jnp.bfloat16)
        held[rows, :BLOCK] = gate_ref[rows, :] * keep
        held[rows, BLOCK:] = up_ref[rows, :] * keep
    total = jnp.dot(joined[...], held[...], preferred_element_type=jnp.float32)
    if len(outs) == 1:
        put(outs[0], total)
        return
    put(coded, total)
    for out_ref, (begin, end) in zip(outs, spans):

        @pl.when(jnp.logical_and(step >= begin, step < end))
        def _(out_ref=out_ref):
            out_ref[...] = coded[...]


def forward(place, mask, tokens, gate_weight, up_weight, start, widths):
    half, depth = tokens[0].shape
    count = 2 * half
    ends = [sum(widths[: c + 1]) // BLOCK for c in range(len(widths))]
    spans = list(zip([0, *ends], ends))
    weight = pl.BlockSpec((depth, BLOCK), lambda j, place, mask: (0, start // BLOCK + j))

    def out(begin, end):
        block = (count + GROUPS, 2 * BLOCK)
        return pl.BlockSpec(block, lambda j, place, mask: (0, jnp.clip(j, begin, end - 1) - begin))

    return pl.pallas_call(
        functools.partial(forward_kernel, first=start // BLOCK, spans=spans),
        grid_spec=pltpu.PrefetchScalarGridSpec(
            num_scalar_prefetch=2,
            grid=(ends[-1],),
            in_specs=[pl.BlockSpec((half, depth), lambda j, place, mask: (0, 0))] * 2 + [weight] * 2,
            out_specs=[out(*span) for span in spans],
            scratch_shapes=[
                pltpu.VMEM((count, depth), jnp.bfloat16),
                pltpu.VMEM((depth, 2 * BLOCK), jnp.bfloat16),
                pltpu.VMEM((count + GROUPS, 2 * BLOCK), jnp.int16),
            ],
        ),
        out_shape=[jax.ShapeDtypeStruct((count + GROUPS, 2 * w), jnp.int16) for w in widths],
        compiler_params=params(),
        cost_estimate=cost(EARLY if start < 2 * widths[0] else LATE),
        name="forward",
    )(place, mask, *tokens, gate_weight, up_weight)


def add_kernel(place_ref, a_ref, b_ref, out_ref):
    inner = place_ref[2] != 0

    @pl.when(inner)
    def _():
        put(out_ref, get(a_ref) + get(b_ref))

    @pl.when(jnp.logical_not(inner))
    def _():
        out_ref[...] = a_ref[...]


def add(place, a, b):
    return pl.pallas_call(
        add_kernel,
        grid_spec=pltpu.PrefetchScalarGridSpec(
            num_scalar_prefetch=1,
            grid=(1,),
            in_specs=[pl.BlockSpec(x.shape, lambda j, place: (0, 0)) for x in (a, b)],
            out_specs=pl.BlockSpec(a.shape, lambda j, place: (0, 0)),
        ),
        out_shape=jax.ShapeDtypeStruct(a.shape, a.dtype),
        compiler_params=params(),
        cost_estimate=cost(),
        name="add",
    )(place, a, b)


def reply_kernel(place_ref, a_ref, b_ref, next_ref, out_ref):
    inner = place_ref[2] != 0

    @pl.when(inner)
    def _():
        put(out_ref.at[:, 0 : a_ref.shape[1]], get(a_ref) + get(b_ref))

    @pl.when(jnp.logical_not(inner))
    def _():
        out_ref[...] = next_ref[...]


def reply(place, a, b, following):
    return pl.pallas_call(
        reply_kernel,
        grid_spec=pltpu.PrefetchScalarGridSpec(
            num_scalar_prefetch=1,
            grid=(1,),
            in_specs=[pl.BlockSpec(x.shape, lambda j, place: (0, 0)) for x in (a, b, following)],
            out_specs=pl.BlockSpec(following.shape, lambda j, place: (0, 0)),
        ),
        out_shape=jax.ShapeDtypeStruct(following.shape, a.dtype),
        compiler_params=params(),
        cost_estimate=cost(),
        name="reply",
    )(place, a, b, following)


def turn_kernel(place_ref, low_ref, high_ref, out_ref):
    half = low_ref.shape[0]
    out_ref[:, 0:half] = low_ref[...].T
    out_ref[:, half : 2 * half] = high_ref[...].T


def turn(place, low, high):
    half, cols = low.shape
    deep = min(512, cols)
    return pl.pallas_call(
        turn_kernel,
        grid_spec=pltpu.PrefetchScalarGridSpec(
            num_scalar_prefetch=1,
            grid=(cols // deep,),
            in_specs=[pl.BlockSpec((half, deep), lambda i, place: (0, i))] * 2,
            out_specs=pl.BlockSpec((deep, 2 * half), lambda i, place: (i, 0)),
        ),
        out_shape=jax.ShapeDtypeStruct((cols, 2 * half), low.dtype),
        compiler_params=params(),
        cost_estimate=cost(TURN),
        name="turn",
    )(place, low, high)


def weights_kernel(place_ref, mask_ref, turned_ref, back_ref, own_ref, across_ref, out_ref, *rest, first, devices):
    hidden_ref, gate_ref, up_ref, deltas, hidden = rest[-5:]
    step = pl.program_id(0)
    depth, width = gate_ref.shape
    count = deltas.shape[0]
    share = count // devices
    col, row, inner = place_ref[0], place_ref[1], place_ref[2] != 0
    owned = hidden_ref.shape[0]

    @pl.when(step == 0)
    def _():
        span = 2 * width
        power = jnp.where(inner, across_ref[count : count + GROUPS, :span], out_ref[count : count + GROUPS, :span])
        scale = jnp.exp2(power.astype(jnp.int32).astype(jnp.float32) - 15.0)
        own_scale = scales(own_ref)
        size = min(share, count // GROUPS)
        for at in range(0, count, size):
            rows = slice(at, at + size)
            group = at // (count // GROUPS)
            slot = at // share
            other = (slot % (devices // 2)) * 2 + slot // (devices // 2)
            token = jnp.bitwise_xor(col, other) * share + at % share
            source = place_ref[3 + token // owned]
            start = pl.multiple_of(source * owned + token % owned, size)
            codes = jnp.where(inner, across_ref[rows, :span], out_ref[rows, :span])
            both = (
                own_ref[rows, :].astype(jnp.int32).astype(jnp.float32) * own_scale[group : group + 1, :]
                + codes.astype(jnp.int32).astype(jnp.float32) * scale[group : group + 1, :]
            )
            for q in range(width // BLOCK):
                cols = slice(q * BLOCK, (q + 1) * BLOCK)
                gate = both[:, 2 * q * BLOCK : (2 * q + 1) * BLOCK]
                up = both[:, (2 * q + 1) * BLOCK : (2 * q + 2) * BLOCK]
                back = back_ref[pl.ds(start, size), cols].astype(jnp.float32)
                sig = jax.nn.sigmoid(gate)
                silu = gate * sig
                hidden[rows, cols] = (silu * up).astype(jnp.bfloat16)
                delta = back * up * sig * (1.0 + gate * (1.0 - sig))
                deltas[rows, 2 * q * BLOCK : (2 * q + 1) * BLOCK] = delta.astype(jnp.bfloat16)
                deltas[rows, (2 * q + 1) * BLOCK : (2 * q + 2) * BLOCK] = (back * silu).astype(jnp.bfloat16)
        for at in range(0, owned, share):
            other = jnp.bitwise_xor(col, row * (owned // share) + at // share)
            slot = (other % 2) * (devices // 2) + other // 2
            hidden_ref[at : at + share, :] = hidden[pl.ds(pl.multiple_of(slot * share, share), share), :]

    total = jnp.dot(turned_ref[...], deltas[...], preferred_element_type=jnp.float32)
    for r in range(depth // BLOCK):
        rows = slice(r * BLOCK, (r + 1) * BLOCK)
        for q in range(width // BLOCK):
            cols = slice(q * BLOCK, (q + 1) * BLOCK)
            keep = mask_ref[step * (depth // BLOCK) + r, first + q].astype(jnp.float32)
            gate_ref[rows, cols] = total[rows, 2 * q * BLOCK : (2 * q + 1) * BLOCK] * keep
            up_ref[rows, cols] = total[rows, (2 * q + 1) * BLOCK : (2 * q + 2) * BLOCK] * keep


def weight_grads(place, mask, turned, back, coded, previous, shapes, start, width, devices):
    depth, count = turned.shape
    owned = shapes[0].shape[0]
    deep = min(ROWS, depth)
    place_of = lambda m, place, mask: (0, 0)
    first = start // BLOCK
    column = pl.Element(width)
    out = pl.BlockSpec((pl.Element(deep), column), lambda m, place, mask: (m * deep, start))
    return pl.pallas_call(
        functools.partial(weights_kernel, first=first, devices=devices),
        grid_spec=pltpu.PrefetchScalarGridSpec(
            num_scalar_prefetch=2,
            grid=(depth // deep,),
            in_specs=[
                pl.BlockSpec((deep, count), lambda m, place, mask: (m, 0)),
                pl.BlockSpec((pl.Element(back.shape[0]), column), lambda m, place, mask: (0, start)),
            ]
            + [pl.BlockSpec(x.shape, place_of) for x in coded]
            + [pl.BlockSpec(memory_space=pl.ANY)] * len(previous),
            out_specs=[pl.BlockSpec((pl.Element(owned), column), lambda m, place, mask: (0, start)), out, out],
            scratch_shapes=[
                pltpu.VMEM((count, 2 * width), jnp.bfloat16),
                pltpu.VMEM((count, width), jnp.bfloat16),
            ],
        ),
        out_shape=shapes,
        input_output_aliases={4 + len(coded) + i: i for i in range(len(previous))},
        compiler_params=params(),
        cost_estimate=cost(),
        name="weight_grads",
    )(place, mask, turned, back, *coded, *previous)


def tie(value, *others):
    return lax.optimization_barrier((value, *others))[0]


def pick(condition, a, b):
    return lax.select(jnp.broadcast_to(condition, a.shape), a, b)


def gather_tokens(tokens, devices, others):
    pieces = [tokens]
    for other in range(2, devices, 2):
        pieces.append(lax.ppermute(tokens, "col", [(i, i ^ other) for i in range(devices)]))
    mine = tie(jnp.concatenate(pieces, axis=0), *others)
    return mine, lax.ppermute(mine, "col", [(i, i ^ 1) for i in range(devices)])


def on_device(tokens, gate_weight, up_weight, block_mask, hidden_grad, *, ring, devices):
    me = lax.axis_index("row")
    depth, local = gate_weight.shape
    left, right = ring // 2 - 1, ring // 2
    reach = ring // 2 - 1
    short = reach == 1
    distance = jnp.where(me >= right, me - right, left - me)
    shapes = [
        jax.ShapeDtypeStruct(hidden_grad.shape, jnp.bfloat16),
        jax.ShapeDtypeStruct((depth, local), jnp.float32),
        jax.ShapeDtypeStruct((depth, local), jnp.float32),
    ]
    widths = chunk_widths(local)
    starts = [sum(widths[:c]) for c in range(len(widths))]
    chunks = len(widths)

    def outward(value, hop):
        return lax.ppermute(value, "row", [(left - hop, left - hop - 1), (right + hop, right + hop + 1)])

    def inward(value, hop):
        return lax.ppermute(value, "row", [(left - hop - 1, left - hop), (right + hop + 1, right + hop)])

    def swap(value):
        return lax.ppermute(value, "row", [(left, right), (right, left)])

    def exchange(value):
        return lax.ppermute(value, "row", [(i, i ^ 1) for i in range(ring)])

    near = [exchange(hidden_grad)] if short else []
    gathered = gather_tokens(tokens, devices, near)
    on_left = me < right
    if short:
        sources = [jnp.where(on_left, i != me, 3 - i) for i in range(2)]
        sources += [jnp.where(on_left, i, i != me) for i in range(2, 4)]
    else:
        sources = list(range(ring))
    inner = (distance == 0) if short else 1
    place = jnp.stack([lax.axis_index("col"), me, inner, *sources]).astype(jnp.int32)
    own, sums, across, arrived, terms = [], [], [], [], []
    outs = ()

    def ordered(kernel, *args):
        nonlocal place
        out = kernel(place, *args)
        place = tie(place, out[0] if isinstance(out, (list, tuple)) else out)
        return out

    def run_forward(c, end):
        own.extend(ordered(forward, block_mask, gathered, gate_weight, up_weight, starts[c], widths[c:end]))

    def run_weights(c, coded, back):
        nonlocal outs
        outs = ordered(
            weight_grads, block_mask, turned, back, coded, outs, shapes, starts[c], widths[c], devices
        )

    if not short:
        back = lax.all_gather(hidden_grad, "row", axis=0, tiled=True)
        turned = ordered(turn, *gathered)
        for c in range(chunks):
            run_forward(c, c + 1)
            total = own[c]
            for hop in reversed(range(reach)):
                new = ordered(add, own[c], inward(total, hop))
                total = pick(distance == hop, new, total)
            coming = swap(total)
            for hop in range(reach):
                came = outward(ordered(add, own[c], coming), hop)
                coming = pick(distance == hop + 1, came, coming)
            run_weights(c, (total, coming, coming), back)
        return tuple(outs)

    ahead = min(AHEAD, chunks)
    run_forward(0, 1)
    arrived.append(inward(own[0], 0))
    far = [swap(hidden_grad), swap(tie(near[0], place))]
    run_forward(1, 2)
    arrived.append(inward(own[1], 0))
    moved = [outward(tie(far[0], place), 0)]
    run_forward(2, ahead)
    for s in range(chunks + LAG):
        if s < chunks:
            if s + 2 < min(chunks, LAG):
                arrived.append(inward(tie(own[s + 2], arrived[s]), 0))
            sums.append(ordered(add, own[s], arrived[s]))
            across.append(swap(sums[s]))
        if s == 0:
            place = tie(place, far[1], moved[0])
            moved.append(outward(tie(far[1], place), 0))
        def weights_of(s):
            c = s - LAG
            run_weights(c, (sums[c], across[c], arrived[s]), back)

        if s == LAG:
            *late, _ = lax.optimization_barrier((*far, *moved, place))
            others = [pick(distance == 0, a, b) for a, b in zip(late[:2], late[2:])]
            back = jnp.concatenate([hidden_grad, near[0], *others], axis=0)
        if LAG <= s < chunks - 1:
            weights_of(s)
        c = s - 1
        if 0 <= c < chunks:
            if c == 0:
                place = tie(place, moved[1])
            both_ways = c + LAG < chunks
            message = ordered(reply, own[c], across[c], own[c + LAG] if both_ways else own[c])
            arrived.append(exchange(message) if both_ways else outward(message, 0))
        if s >= max(LAG, chunks - 1):
            weights_of(s)
        if len(own) < chunks:
            run_forward(len(own), min(len(own) + (2 if s == 0 else 1), chunks))
        if s == 2:
            turned = ordered(turn, *gathered)
    return tuple(outs)


def solution(mesh):
    placed = (P("col", "row"), P("row", "col"), P("row", "col"), P("row", "col"), P("row", "col"))
    return jax.shard_map(
        functools.partial(on_device, ring=mesh.shape["row"], devices=mesh.shape["col"]),
        mesh=mesh,
        in_specs=placed,
        out_specs=(P("row", "col"), P("row", "col"), P("row", "col")),
        check_vma=False,
    )
```

```python
import functools

import jax
import jax.numpy as jnp
from jax import lax
from jax.experimental import pallas as pl
from jax.experimental.pallas import tpu as pltpu
from jax.sharding import PartitionSpec as P

BLOCK = 128
GROUPS = 16
CHUNK = 2
AHEAD = 4
LAG = 3
EARLY, LATE, TURN = 8000, 1, 1
ROWS = 512
VMEM_LIMIT = 48 * 1024 * 1024


def params():
    return pltpu.CompilerParams(vmem_limit_bytes=VMEM_LIMIT)


def cost(megaflops=1):
    return pl.CostEstimate(flops=megaflops * 10**6, bytes_accessed=megaflops * 2500, transcendentals=0)


def chunk_widths(local):
    units = local // BLOCK
    rest = [CHUNK] * ((units - 1) // CHUNK)
    return [BLOCK * u for u in [units - sum(rest), *rest]]


def put(ref, value):
    rows, cols = value.shape
    grouped = value.reshape(GROUPS, rows // GROUPS, cols)
    top = jnp.max(jnp.abs(grouped), axis=1)
    power = jnp.floor(jnp.log2(jnp.maximum(top, 1e-30))) + 1.0
    codes = jnp.round(grouped * jnp.exp2(15.0 - power)[:, None, :])
    codes = jnp.clip(codes, -32767.0, 32767.0).reshape(rows, cols)
    ref[0:rows, :] = codes.astype(jnp.int32).astype(jnp.int16)
    ref[rows : rows + GROUPS, :] = power.astype(jnp.int32).astype(jnp.int16)


def scales(ref):
    rows = ref.shape[0] - GROUPS
    return jnp.exp2(ref[rows : rows + GROUPS, :].astype(jnp.int32).astype(jnp.float32) - 15.0)


def get(ref):
    rows = ref.shape[0] - GROUPS
    cols = ref.shape[1]
    codes = ref[0:rows, :].astype(jnp.int32).astype(jnp.float32)
    grouped = codes.reshape(GROUPS, rows // GROUPS, cols) * scales(ref)[:, None, :]
    return grouped.reshape(rows, cols)


def forward_kernel(place_ref, mask_ref, low_ref, high_ref, gate_ref, up_ref, *rest, first, spans):
    *outs, joined, held, coded = rest
    step = pl.program_id(0)
    depth = gate_ref.shape[0]
    half = low_ref.shape[0]

    @pl.when(step == 0)
    def _():
        joined[0:half, :] = low_ref[...]
        joined[half : 2 * half, :] = high_ref[...]

    for r in range(depth // BLOCK):
        rows = slice(r * BLOCK, (r + 1) * BLOCK)
        keep = mask_ref[r, first + step].astype(jnp.float32)
        keep = jnp.full((BLOCK, BLOCK), keep).astype(jnp.bfloat16)
        held[rows, :BLOCK] = gate_ref[rows, :] * keep
        held[rows, BLOCK:] = up_ref[rows, :] * keep
    total = jnp.dot(joined[...], held[...], preferred_element_type=jnp.float32)
    if len(outs) == 1:
        put(outs[0], total)
        return
    put(coded, total)
    for out_ref, (begin, end) in zip(outs, spans):

        @pl.when(jnp.logical_and(step >= begin, step < end))
        def _(out_ref=out_ref):
            out_ref[...] = coded[...]


def forward(place, mask, tokens, gate_weight, up_weight, start, widths):
    half, depth = tokens[0].shape
    count = 2 * half
    ends = [sum(widths[: c + 1]) // BLOCK for c in range(len(widths))]
    spans = list(zip([0, *ends], ends))
    weight = pl.BlockSpec((depth, BLOCK), lambda j, place, mask: (0, start // BLOCK + j))

    def out(begin, end):
        block = (count + GROUPS, 2 * BLOCK)
        return pl.BlockSpec(block, lambda j, place, mask: (0, jnp.clip(j, begin, end - 1) - begin))

    return pl.pallas_call(
        functools.partial(forward_kernel, first=start // BLOCK, spans=spans),
        grid_spec=pltpu.PrefetchScalarGridSpec(
            num_scalar_prefetch=2,
            grid=(ends[-1],),
            in_specs=[pl.BlockSpec((half, depth), lambda j, place, mask: (0, 0))] * 2 + [weight] * 2,
            out_specs=[out(*span) for span in spans],
            scratch_shapes=[
                pltpu.VMEM((count, depth), jnp.bfloat16),
                pltpu.VMEM((depth, 2 * BLOCK), jnp.bfloat16),
                pltpu.VMEM((count + GROUPS, 2 * BLOCK), jnp.int16),
            ],
        ),
        out_shape=[jax.ShapeDtypeStruct((count + GROUPS, 2 * w), jnp.int16) for w in widths],
        compiler_params=params(),
        cost_estimate=cost(EARLY if start < 2 * widths[0] else LATE),
        name="forward",
    )(place, mask, *tokens, gate_weight, up_weight)


def add_kernel(place_ref, a_ref, b_ref, out_ref):
    inner = place_ref[2] != 0

    @pl.when(inner)
    def _():
        put(out_ref, get(a_ref) + get(b_ref))

    @pl.when(jnp.logical_not(inner))
    def _():
        out_ref[...] = a_ref[...]


def add(place, a, b):
    return pl.pallas_call(
        add_kernel,
        grid_spec=pltpu.PrefetchScalarGridSpec(
            num_scalar_prefetch=1,
            grid=(1,),
            in_specs=[pl.BlockSpec(x.shape, lambda j, place: (0, 0)) for x in (a, b)],
            out_specs=pl.BlockSpec(a.shape, lambda j, place: (0, 0)),
        ),
        out_shape=jax.ShapeDtypeStruct(a.shape, a.dtype),
        compiler_params=params(),
        cost_estimate=cost(),
        name="add",
    )(place, a, b)


def reply_kernel(place_ref, a_ref, b_ref, next_ref, out_ref):
    inner = place_ref[2] != 0

    @pl.when(inner)
    def _():
        put(out_ref.at[:, 0 : a_ref.shape[1]], get(a_ref) + get(b_ref))

    @pl.when(jnp.logical_not(inner))
    def _():
        out_ref[...] = next_ref[...]


def reply(place, a, b, following):
    return pl.pallas_call(
        reply_kernel,
        grid_spec=pltpu.PrefetchScalarGridSpec(
            num_scalar_prefetch=1,
            grid=(1,),
            in_specs=[pl.BlockSpec(x.shape, lambda j, place: (0, 0)) for x in (a, b, following)],
            out_specs=pl.BlockSpec(following.shape, lambda j, place: (0, 0)),
        ),
        out_shape=jax.ShapeDtypeStruct(following.shape, a.dtype),
        compiler_params=params(),
        cost_estimate=cost(),
        name="reply",
    )(place, a, b, following)


def turn_kernel(place_ref, low_ref, high_ref, out_ref):
    half = low_ref.shape[0]
    out_ref[:, 0:half] = low_ref[...].T
    out_ref[:, half : 2 * half] = high_ref[...].T


def turn(place, low, high):
    half, cols = low.shape
    deep = min(512, cols)
    return pl.pallas_call(
        turn_kernel,
        grid_spec=pltpu.PrefetchScalarGridSpec(
            num_scalar_prefetch=1,
            grid=(cols // deep,),
            in_specs=[pl.BlockSpec((half, deep), lambda i, place: (0, i))] * 2,
            out_specs=pl.BlockSpec((deep, 2 * half), lambda i, place: (i, 0)),
        ),
        out_shape=jax.ShapeDtypeStruct((cols, 2 * half), low.dtype),
        compiler_params=params(),
        cost_estimate=cost(TURN),
        name="turn",
    )(place, low, high)


def weights_kernel(place_ref, mask_ref, turned_ref, back_ref, own_ref, across_ref, out_ref, *rest, first, devices):
    hidden_ref, gate_ref, up_ref, deltas, hidden = rest[-5:]
    step = pl.program_id(0)
    depth, width = gate_ref.shape
    count = deltas.shape[0]
    share = count // devices
    col, row, inner = place_ref[0], place_ref[1], place_ref[2] != 0
    owned = hidden_ref.shape[0]

    @pl.when(step == 0)
    def _():
        span = 2 * width
        power = jnp.where(inner, across_ref[count : count + GROUPS, :span], out_ref[count : count + GROUPS, :span])
        scale = jnp.exp2(power.astype(jnp.int32).astype(jnp.float32) - 15.0)
        own_scale = scales(own_ref)
        size = min(share, count // GROUPS)
        for at in range(0, count, size):
            rows = slice(at, at + size)
            group = at // (count // GROUPS)
            slot = at // share
            other = (slot % (devices // 2)) * 2 + slot // (devices // 2)
            token = jnp.bitwise_xor(col, other) * share + at % share
            source = place_ref[3 + token // owned]
            start = pl.multiple_of(source * owned + token % owned, size)
            codes = jnp.where(inner, across_ref[rows, :span], out_ref[rows, :span])
            both = (
                own_ref[rows, :].astype(jnp.int32).astype(jnp.float32) * own_scale[group : group + 1, :]
                + codes.astype(jnp.int32).astype(jnp.float32) * scale[group : group + 1, :]
            )
            for q in range(width // BLOCK):
                cols = slice(q * BLOCK, (q + 1) * BLOCK)
                gate = both[:, 2 * q * BLOCK : (2 * q + 1) * BLOCK]
                up = both[:, (2 * q + 1) * BLOCK : (2 * q + 2) * BLOCK]
                back = back_ref[pl.ds(start, size), cols].astype(jnp.float32)
                sig = jax.nn.sigmoid(gate)
                silu = gate * sig
                hidden[rows, cols] = (silu * up).astype(jnp.bfloat16)
                delta = back * up * sig * (1.0 + gate * (1.0 - sig))
                deltas[rows, 2 * q * BLOCK : (2 * q + 1) * BLOCK] = delta.astype(jnp.bfloat16)
                deltas[rows, (2 * q + 1) * BLOCK : (2 * q + 2) * BLOCK] = (back * silu).astype(jnp.bfloat16)
        for at in range(0, owned, share):
            other = jnp.bitwise_xor(col, row * (owned // share) + at // share)
            slot = (other % 2) * (devices // 2) + other // 2
            hidden_ref[at : at + share, :] = hidden[pl.ds(pl.multiple_of(slot * share, share), share), :]

    total = jnp.dot(turned_ref[...], deltas[...], preferred_element_type=jnp.float32)
    for r in range(depth // BLOCK):
        rows = slice(r * BLOCK, (r + 1) * BLOCK)
        for q in range(width // BLOCK):
            cols = slice(q * BLOCK, (q + 1) * BLOCK)
            keep = mask_ref[step * (depth // BLOCK) + r, first + q].astype(jnp.float32)
            gate_ref[rows, cols] = total[rows, 2 * q * BLOCK : (2 * q + 1) * BLOCK] * keep
            up_ref[rows, cols] = total[rows, (2 * q + 1) * BLOCK : (2 * q + 2) * BLOCK] * keep


def weight_grads(place, mask, turned, back, coded, previous, shapes, start, width, devices):
    depth, count = turned.shape
    owned = shapes[0].shape[0]
    deep = min(ROWS, depth)
    place_of = lambda m, place, mask: (0, 0)
    first = start // BLOCK
    column = pl.Element(width)
    out = pl.BlockSpec((pl.Element(deep), column), lambda m, place, mask: (m * deep, start))
    return pl.pallas_call(
        functools.partial(weights_kernel, first=first, devices=devices),
        grid_spec=pltpu.PrefetchScalarGridSpec(
            num_scalar_prefetch=2,
            grid=(depth // deep,),
            in_specs=[
                pl.BlockSpec((deep, count), lambda m, place, mask: (m, 0)),
                pl.BlockSpec((pl.Element(back.shape[0]), column), lambda m, place, mask: (0, start)),
            ]
            + [pl.BlockSpec(x.shape, place_of) for x in coded]
            + [pl.BlockSpec(memory_space=pl.ANY)] * len(previous),
            out_specs=[pl.BlockSpec((pl.Element(owned), column), lambda m, place, mask: (0, start)), out, out],
            scratch_shapes=[
                pltpu.VMEM((count, 2 * width), jnp.bfloat16),
                pltpu.VMEM((count, width), jnp.bfloat16),
            ],
        ),
        out_shape=shapes,
        input_output_aliases={4 + len(coded) + i: i for i in range(len(previous))},
        compiler_params=params(),
        cost_estimate=cost(),
        name="weight_grads",
    )(place, mask, turned, back, *coded, *previous)


def tie(value, *others):
    return lax.optimization_barrier((value, *others))[0]


def pick(condition, a, b):
    return lax.select(jnp.broadcast_to(condition, a.shape), a, b)


def gather_tokens(tokens, devices, others):
    pieces = [tokens]
    for other in range(2, devices, 2):
        pieces.append(lax.ppermute(tokens, "col", [(i, i ^ other) for i in range(devices)]))
    mine = tie(jnp.concatenate(pieces, axis=0), *others)
    return mine, lax.ppermute(mine, "col", [(i, i ^ 1) for i in range(devices)])


def on_device(tokens, gate_weight, up_weight, block_mask, hidden_grad, *, ring, devices):
    me = lax.axis_index("row")
    depth, local = gate_weight.shape
    left, right = ring // 2 - 1, ring // 2
    reach = ring // 2 - 1
    short = reach == 1
    distance = jnp.where(me >= right, me - right, left - me)
    shapes = [
        jax.ShapeDtypeStruct(hidden_grad.shape, jnp.bfloat16),
        jax.ShapeDtypeStruct((depth, local), jnp.float32),
        jax.ShapeDtypeStruct((depth, local), jnp.float32),
    ]
    widths = chunk_widths(local)
    starts = [sum(widths[:c]) for c in range(len(widths))]
    chunks = len(widths)

    def outward(value, hop):
        return lax.ppermute(value, "row", [(left - hop, left - hop - 1), (right + hop, right + hop + 1)])

    def inward(value, hop):
        return lax.ppermute(value, "row", [(left - hop - 1, left - hop), (right + hop + 1, right + hop)])

    def swap(value):
        return lax.ppermute(value, "row", [(left, right), (right, left)])

    def exchange(value):
        return lax.ppermute(value, "row", [(i, i ^ 1) for i in range(ring)])

    near = [exchange(hidden_grad)] if short else []
    gathered = gather_tokens(tokens, devices, near)
    on_left = me < right
    if short:
        sources = [jnp.where(on_left, i != me, 3 - i) for i in range(2)]
        sources += [jnp.where(on_left, i, i != me) for i in range(2, 4)]
    else:
        sources = list(range(ring))
    inner = (distance == 0) if short else 1
    place = jnp.stack([lax.axis_index("col"), me, inner, *sources]).astype(jnp.int32)
    own, sums, across, arrived, terms = [], [], [], [], []
    outs = ()

    def ordered(kernel, *args):
        nonlocal place
        out = kernel(place, *args)
        place = tie(place, out[0] if isinstance(out, (list, tuple)) else out)
        return out

    def run_forward(c, end):
        own.extend(ordered(forward, block_mask, gathered, gate_weight, up_weight, starts[c], widths[c:end]))

    def run_weights(c, coded, back):
        nonlocal outs
        outs = ordered(
            weight_grads, block_mask, turned, back, coded, outs, shapes, starts[c], widths[c], devices
        )

    if not short:
        back = lax.all_gather(hidden_grad, "row", axis=0, tiled=True)
        turned = ordered(turn, *gathered)
        for c in range(chunks):
            run_forward(c, c + 1)
            total = own[c]
            for hop in reversed(range(reach)):
                new = ordered(add, own[c], inward(total, hop))
                total = pick(distance == hop, new, total)
            coming = swap(total)
            for hop in range(reach):
                came = outward(ordered(add, own[c], coming), hop)
                coming = pick(distance == hop + 1, came, coming)
            run_weights(c, (total, coming, coming), back)
        return tuple(outs)

    ahead = min(AHEAD, chunks)
    run_forward(0, 1)
    arrived.append(inward(own[0], 0))
    far = [swap(hidden_grad), swap(tie(near[0], place))]
    run_forward(1, 2)
    arrived.append(inward(own[1], 0))
    moved = [outward(tie(far[0], place), 0)]
    run_forward(2, ahead)
    for s in range(chunks + LAG):
        if s < chunks:
            if s + 2 < min(chunks, LAG):
                arrived.append(inward(tie(own[s + 2], arrived[s]), 0))
            sums.append(ordered(add, own[s], arrived[s]))
            across.append(swap(sums[s]))
        if s == 0:
            place = tie(place, far[1], moved[0])
            moved.append(outward(tie(far[1], place), 0))
        def weights_of(s):
            c = s - LAG
            run_weights(c, (sums[c], across[c], arrived[s]), back)

        if s == LAG:
            *late, _ = lax.optimization_barrier((*far, *moved, place))
            others = [pick(distance == 0, a, b) for a, b in zip(late[:2], late[2:])]
            back = jnp.concatenate([hidden_grad, near[0], *others], axis=0)
        if LAG <= s < chunks - 2:
            weights_of(s)
        c = s - 1
        if 0 <= c < chunks:
            if c == 0:
                place = tie(place, moved[1])
            both_ways = c + LAG < chunks
            message = ordered(reply, own[c], across[c], own[c + LAG] if both_ways else own[c])
            arrived.append(exchange(message) if both_ways else outward(message, 0))
        if s >= max(LAG, chunks - 2):
            weights_of(s)
        if len(own) < chunks:
            run_forward(len(own), min(len(own) + (2 if s == 0 else 1), chunks))
        if s == 2:
            turned = ordered(turn, *gathered)
    return tuple(outs)


def solution(mesh):
    placed = (P("col", "row"), P("row", "col"), P("row", "col"), P("row", "col"), P("row", "col"))
    return jax.shard_map(
        functools.partial(on_device, ring=mesh.shape["row"], devices=mesh.shape["col"]),
        mesh=mesh,
        in_specs=placed,
        out_specs=(P("row", "col"), P("row", "col"), P("row", "col")),
        check_vma=False,
    )
```
